32 devices in a mesh: dp: 8 (over y, x, core), tower: 4 (over z).
Axes of the slice: x: 2, y: 2, z: 4, core: 2. Of those that a mesh axis runs over, the one named last changes fastest.
Arguments:
- features: bfloat16 [8, 32, 64, 256], P('dp', 'tower'), may hold values from -18 to 18
- crop_ids: int32 [8, 32], P('dp'), may hold values from 0 to 3, never falling along the last dimension, each value on 1 to 16 neighbouring positions
- labels: int32 [8, 32, 64, 9], P('dp', 'tower'), may hold values from -1 to 79
- positive: int32 [8, 32, 64, 9], P('dp', 'tower'), may hold values from 0 to 1
- box_targets: float32 [8, 32, 64, 36], P('dp', 'tower'), may hold values from -4 to 4
- tower_weights: float32 [4, 2, 2304, 256], P(None, None, ('dp', 'tower')), may hold values from -0.1875 to 0.1875
- head_weights: float32 [2304, 756], P(('dp', 'tower')), may hold values from -0.1875 to 0.1875
- biases: float32 [2804], replicated, may hold values from -0.3 to 0.3
- tower_m: float32 [4, 2, 2304, 256], P(None, None, ('dp', 'tower')), may hold values from -0.34785053 to 0.34785053
- tower_v: float32 [4, 2, 2304, 256], P(None, None, ('dp', 'tower')), may hold values from 0.000625 to 0.0025
- head_m: float32 [2304, 756], P(('dp', 'tower')), may hold values from -0.2 to 0.2
- head_v: float32 [2304, 756], P(('dp', 'tower')), may hold values from 0.00019753087 to 0.0007901235
- bias_m: float32 [2804], replicated, may hold values from -0.3888889 to 0.3888889
- bias_v: float32 [2804], replicated, may hold values from 0.0007901235 to 0.003160494
- step_count: int32 [1], replicated, may hold values from 2 to 20
Outputs:
- logits: bfloat16 [8, 32, 64, 720], P('dp', 'tower')
- deltas: bfloat16 [8, 32, 64, 36], P('dp', 'tower')
- loss: float32 [], replicated
- feature_grad: float32 [8, 32, 64, 256], P('dp', 'tower')
- tower_grad: float32 [4, 2304, 256], P(None, ('dp', 'tower'))
- box_tower_grad: float32 [4, 2304, 256], P(None, ('dp', 'tower'))
- head_grad: float32 [2304, 756], P(('dp', 'tower'))
- bias_grad: float32 [2768], replicated
- box_bias_grad: float32 [36], replicated
- tower_new: float32 [4, 2, 2304, 256], P(None, None, ('dp', 'tower'))
- head_new: float32 [2304, 756], P(('dp', 'tower'))
- bias_new: float32 [2804], replicated
- tower_m_new: float32 [4, 2, 2304, 256], P(None, None, ('dp', 'tower'))
- tower_v_new: float32 [4, 2, 2304, 256], P(None, None, ('dp', 'tower'))
- head_m_new: float32 [2304, 756], P(('dp', 'tower'))
- head_v_new: float32 [2304, 756], P(('dp', 'tower'))
- bias_m_new: float32 [2804], replicated
- bias_v_new: float32 [2804], replicated
- tower_copy: bfloat16 [4, 2, 2304, 256], P(None, None, ('dp', 'tower'))
- head_copy: bfloat16 [2304, 756], P(('dp', 'tower'))
The draws below stay inside these ranges and needn't reach their ends.
Inputs may be any that keep to these rules, and one draw needn't show every extreme that they name: `crop_ids`: crop numbers never fall along a canvas's rows, each crop spans 1 to 16 rows, one spans exactly 16.
All inputs are finite; a program needn't handle non-finite values.
Results may differ from the reference program's by a relative error of at most 0.012.
Values may be sent and summed in bfloat16 or wider, within the bound.
A program may use at most 192 MiB of HBM per device.

```python
import math
import jax
import jax.numpy as jnp
import numpy as np
from jax import lax

C = 256
ANCHORS = 9
CLASSES = 80
LAYERS = 4
WIDE = 64
CROPS = 4
H = 32
CANVASES = 8
KIN = 2304
CLS_OUT = 720
HEAD_OUT = 756
BIASES = 2804
CROP_MOST = 16


def draw_features(key, part):
    canvas_index = jnp.arange(CANVASES, dtype=jnp.float32)
    rise = canvas_index / float(max(CANVASES - 1, 1))
    scales = 0.6 * jnp.power(5.0, rise)
    base = jnp.clip(jax.random.normal(key, (CANVASES, H, WIDE, C), jnp.float32), -6.0, 6.0)
    return (base * scales[:, None, None, None]).astype(jnp.bfloat16)


def draw_positive(key, part):
    canvas_index = jnp.arange(CANVASES, dtype=jnp.int32)
    thresholds = 20 + 40 * canvas_index // max(CANVASES - 1, 1)
    raw_draw = jax.random.randint(key, (CANVASES, H, WIDE, ANCHORS), 0, 1000, dtype=jnp.int32)
    return (raw_draw < thresholds[:, None, None, None]).astype(jnp.int32)


def with_ends(array, key, low, high):
    dims = array.shape
    index_at = [jax.random.randint(jax.random.fold_in(key, axis), (), 0, dims[axis]) for axis in range(len(dims))]
    array = array.at[tuple(index_at)].set(low)
    longest = dims.index(max(dims))
    index_at[longest] = (index_at[longest] + 1) % dims[longest]
    return array.at[tuple(index_at)].set(high)


def level_of(key, dims, pieces, smallest, top_value):
    gain = 1.0
    for position, blocks in pieces:
        heights = jax.random.uniform(jax.random.fold_in(jax.random.fold_in(key, 6), position), (blocks,), jnp.float32, smallest / len(pieces), top_value / len(pieces))
        gain = gain * jnp.repeat(jnp.exp(heights), dims[position] // blocks).reshape((-1,) + (1,) * (len(dims) - 1 - position))
    return gain


def split_up(number_of, total, reach, skew):
    weights = [(1 << 20) // math.isqrt(grade ** skew) + 1 for grade in range(2, number_of + 1)]
    rest, holding = total - reach - (number_of - 1), [1] * (number_of - 1)
    while rest > 0:
        candidates = [i for i in range(number_of - 1) if holding[i] < reach]
        mass, remaining = sum([weights[i] for i in candidates]), rest
        for i in candidates:
            more = min(reach - holding[i], max(1, remaining * weights[i] // mass), rest)
            holding[i] = holding[i] + more
            rest = rest - more
    return np.array([reach] + holding)


def ragged(own_key, amount, total, limit, lean):
    if amount == 2:
        one = jax.random.randint(own_key, (), max(1, total - limit), min(limit, total - 1) + 1)
        return jnp.stack([one, total - one])
    sizes = jnp.asarray(split_up(amount, total, limit, lean), jnp.int32)
    pairs = (amount - 1) // 2
    source_of, taker = sizes[1:1 + 2 * pairs:2], sizes[2:2 + 2 * pairs:2]
    room = jnp.minimum(source_of - 1, limit - taker)
    moved = jax.random.randint(jax.random.fold_in(own_key, 1), (pairs,), 0, 1 << 20) % (room + 1)
    sizes = sizes.at[1:1 + 2 * pairs:2].set(source_of - moved).at[2:2 + 2 * pairs:2].set(taker + moved)
    return sizes[jax.random.permutation(jax.random.fold_in(own_key, 2), amount)]


def scatter_about(stream_key, dims, scale, limit, cuts=(), held_as=jnp.bfloat16):
    result = jax.random.normal(stream_key, dims, jnp.float32) * scale
    if len(cuts) > 0:
        result = level_of(stream_key, dims, cuts, -0.22, 0.18) * result
    return jnp.clip(result, min=-limit, max=limit).astype(held_as)


def setup_inputs(seed: int = 0) -> dict:
    streams_of = jax.random.split(jax.random.key(seed), 16)
    features = draw_features(jax.random.fold_in(streams_of[15], 71), 0)
    crop_ids = jax.vmap(lambda own: jnp.searchsorted(jnp.cumsum(ragged(own, CROPS, H, CROP_MOST, 1)), jnp.arange(H), side="right"))(jax.random.split(streams_of[1], CANVASES)).reshape((CANVASES, H)).astype(jnp.int32)
    labels = with_ends(jax.random.randint(streams_of[2], (CANVASES, H, WIDE, ANCHORS), -1, CLASSES), jax.random.fold_in(streams_of[2], 1), -1, CLASSES - 1).astype(jnp.int32)
    positive = draw_positive(jax.random.fold_in(streams_of[15], 71), 0)
    box_targets = scatter_about(streams_of[4], (CANVASES, H, WIDE, 4 * ANCHORS), 0.5, 4.0, ((0, 8), (1, 4)), jnp.float32)
    tower_weights = scatter_about(streams_of[5], (LAYERS, 2, KIN, C), (KIN // 2) ** -0.5, 0.1875, ((2, 32),), jnp.float32)
    head_weights = scatter_about(streams_of[6], (KIN, HEAD_OUT), (KIN // 2) ** -0.5, 0.1875, ((0, 32),), jnp.float32)
    biases = scatter_about(streams_of[7], (BIASES,), 0.05, 0.3, (), jnp.float32)
    tower_m = scatter_about(streams_of[8], (LAYERS, 2, KIN, C), (0.33 / ANCHORS * (2 * CLS_OUT / C) ** 0.5), 0.34785053, ((2, 32),), jnp.float32)
    tower_v = jnp.clip(jnp.exp(math.log(0.0025) - 1.3862944 * jax.random.uniform(streams_of[9], (LAYERS, 2, KIN, C), jnp.float32) ** level_of(streams_of[9], (LAYERS, 2, KIN, C), ((2, 32),), -0.2, 0.2)), 0.000625, 0.0025)
    head_m = scatter_about(streams_of[10], (KIN, HEAD_OUT), (0.44 / ANCHORS), 0.2, ((0, 32),), jnp.float32)
    head_v = jnp.clip(jnp.exp(math.log(0.0007901235) - 1.3862944 * jax.random.uniform(streams_of[11], (KIN, HEAD_OUT), jnp.float32) ** level_of(streams_of[11], (KIN, HEAD_OUT), ((0, 32),), -0.2, 0.2)), 0.00019753087, 0.0007901235)
    bias_m = scatter_about(streams_of[12], (BIASES,), (0.88 / ANCHORS), 0.3888889, (), jnp.float32)
    bias_v = jnp.clip(jnp.exp(jax.random.uniform(streams_of[13], (BIASES,), jnp.float32, math.log(0.0007901235), math.log(0.003160494))), 0.0007901235, 0.003160494)
    step_count = jax.random.randint(streams_of[14], (1,), 2, 21).astype(jnp.int32)
    return {"features": features, "crop_ids": crop_ids, "labels": labels, "positive": positive, "box_targets": box_targets, "tower_weights": tower_weights, "head_weights": head_weights, "biases": biases, "tower_m": tower_m, "tower_v": tower_v, "head_m": head_m, "head_v": head_v, "bias_m": bias_m, "bias_v": bias_v, "step_count": step_count}


beta_one = 0.9
beta_two = 0.999
adam_eps = 1e-08
learn_rate = 0.03
decay_rate = 0.05
focal_alpha = 0.25
smooth_beta = 1.0 / 9.0

@jax.custom_vjp
def low(v):
    return lax.optimization_barrier(v.astype(jnp.bfloat16)).astype(jnp.float32)

@jax.custom_vjp
def low_back(v):
    return v

def low_keep(v):
    return (low(v), None)

def low_pass(kept, grad):
    return (grad,)

def back_keep(v):
    return (v, None)

def back_low(kept, grad):
    return (low(grad),)
low.defvjp(low_keep, low_pass)
low_back.defvjp(back_keep, back_low)

def conv_same(inputs, weight):
    channels_in = weight.shape[0] // 9
    kernel = weight.reshape(3, 3, channels_in, weight.shape[-1])
    return lax.conv_general_dilated(inputs, kernel, (1, 1), ((1, 1), (1, 1)), dimension_numbers=('NHWC', 'HWIO', 'NHWC'), precision=lax.Precision.HIGHEST)

def adam_update(weight, grad, first, second, step_float, decay):
    first_new = beta_one * first + (1.0 - beta_one) * grad
    second_new = beta_two * second + (1.0 - beta_two) * grad * grad
    first_hat = first_new / (1.0 - jnp.power(beta_one, step_float))
    second_hat = second_new / (1.0 - jnp.power(beta_two, step_float))
    weight_new = weight - learn_rate * (first_hat / (jnp.sqrt(second_hat) + adam_eps) + decay * weight)
    return (weight_new, first_new, second_new)

def reference(features, crop_ids, labels, positive, box_targets, tower_weights, head_weights, biases, tower_m, tower_v, head_m, head_v, bias_m, bias_v, step_count):
    same_rows = crop_ids[:, 1:] == crop_ids[:, :-1]
    edge_true = jnp.ones((crop_ids.shape[0], 1), dtype=jnp.bool_)
    row_ok = jnp.concatenate([edge_true, same_rows], 1) & jnp.concatenate([same_rows, edge_true], 1)
    valid = (labels >= 0) & row_ok[:, :, None, None]
    chosen = valid & (positive > 0)
    valid_f = valid.astype(jnp.float32)
    chosen_f = chosen.astype(jnp.float32)
    targets = ((labels[..., None] == jnp.arange(CLASSES, dtype=jnp.int32)) & chosen[..., None]).astype(jnp.float32)
    denom = jnp.maximum(jnp.sum(chosen_f), 1.0)

    def loss_terms(cls_vals, box_vals):
        logit_view = cls_vals.reshape(targets.shape)
        prob = jax.nn.sigmoid(logit_view)
        cross = jax.nn.softplus(logit_view) - targets * logit_view
        prob_true = prob * targets + (1.0 - prob) * (1.0 - targets)
        alpha_weight = focal_alpha * targets + (1.0 - focal_alpha) * (1.0 - targets)
        focal = jnp.sum(alpha_weight * (1.0 - prob_true) ** 2 * cross * valid_f[..., None])
        diff = box_vals.reshape(chosen.shape + (4,)) - box_targets.reshape(chosen.shape + (4,))
        abs_diff = jnp.abs(diff)
        smooth = jnp.where(abs_diff < smooth_beta, 0.5 * diff * diff / smooth_beta, abs_diff - 0.5 * smooth_beta)
        return focal + jnp.sum(smooth * chosen_f[..., None])

    def forward(feats, tower_w, head_w, bias_all):
        tower_b = bias_all[:2 * LAYERS * C].reshape(LAYERS, 2, C)
        head_b = bias_all[2 * LAYERS * C:]
        tops = []
        for side in range(2):
            hidden = feats
            for layer in range(LAYERS):
                inputs = hidden if layer == 0 else low(hidden)
                raw_out = low_back(conv_same(inputs, low(tower_w[layer, side])) + tower_b[layer, side])
                hidden = raw_out * jax.nn.sigmoid(raw_out)
            tops.append(low(hidden))
        cls_raw = low_back(conv_same(tops[0], low(head_w[:, :CLS_OUT])) + head_b[:CLS_OUT])
        box_raw = low_back(conv_same(tops[1], low(head_w[:, CLS_OUT:])) + head_b[CLS_OUT:])
        terms = loss_terms(cls_raw, box_raw)
        return (terms / denom, (cls_raw, box_raw, terms))
    feats = features.astype(jnp.float32)
    scaled, pullback, extras = jax.vjp(forward, feats, tower_weights, head_weights, biases, has_aux=True)
    feature_grad, tower_grad, head_grad, bias_grad = pullback(jnp.ones_like(scaled))
    cls_raw, box_raw, terms = extras
    loss = terms / denom
    step_float = step_count[0].astype(jnp.float32)
    tower_new, tower_m_new, tower_v_new = adam_update(tower_weights, tower_grad, tower_m, tower_v, step_float, decay_rate)
    head_new, head_m_new, head_v_new = adam_update(head_weights, head_grad, head_m, head_v, step_float, decay_rate)
    bias_new, bias_m_new, bias_v_new = adam_update(biases, bias_grad, bias_m, bias_v, step_float, 0.0)
    split_at = BIASES - 4 * ANCHORS
    return (cls_raw.astype(jnp.bfloat16), box_raw.astype(jnp.bfloat16), loss, feature_grad, tower_grad[:, 0], tower_grad[:, 1], head_grad, bias_grad[:split_at], bias_grad[split_at:], tower_new, head_new, bias_new, tower_m_new, tower_v_new, head_m_new, head_v_new, bias_m_new, bias_v_new, tower_new.astype(jnp.bfloat16), head_new.astype(jnp.bfloat16))
```

```python
from functools import partial

import jax
import jax.numpy as jnp
from jax import lax
from jax.experimental import pallas as pl
from jax.experimental.pallas import tpu as pltpu
from jax.sharding import PartitionSpec as P

beta_one = 0.9
beta_two = 0.999
adam_eps = 1e-08
learn_rate = 0.03
decay_rate = 0.05
focal_alpha = 0.25
smooth_beta = 1.0 / 9.0


def with_halo(shard, sides, width):
    for axis, dim in sides:
        size, length = (lax.axis_size(axis), shard.shape[dim])
        up = [(i, (i + 1) % size) for i in range(size - 1)]
        down = [(j, i) for i, j in up]
        last = lax.slice_in_dim(shard, length - width, length, axis=dim)
        initial = lax.slice_in_dim(shard, 0, width, axis=dim)
        before = lax.ppermute(last, axis, up)
        after = lax.ppermute(initial, axis, down)
        shard = jnp.concatenate([before, shard, after], axis=dim)
    return shard


def act_rim(values):
    return with_halo(values, (("tower", 2),), 1)


def grad_rim(values):
    return with_halo(values, (("tower", 2),), 1)


def pad_cols(values):
    return jnp.pad(values, ((0, 0), (0, 0), (0, 0), (1, 1), (0, 0)))


def silu_value(values):
    return values * jax.nn.sigmoid(values)


def silu_slope(values):
    sig = jax.nn.sigmoid(values)
    return sig * (1.0 + values * (1.0 - sig))


def conv_forward(padded, weight, out_rows, out_cols):
    stacks, canvases, channels = (padded.shape[0], padded.shape[1], padded.shape[-1])
    summed = None
    for row_off in range(3):
        for col_off in range(3):
            tap_index = row_off * 3 + col_off
            window = padded[
                :, :, row_off : row_off + out_rows, col_off : col_off + out_cols, :
            ].reshape(stacks, -1, channels)
            contrib = jnp.einsum(
                "snk,skm->snm",
                window,
                weight[:, tap_index * channels : (tap_index + 1) * channels, :],
                preferred_element_type=jnp.float32,
            )
            summed = contrib if summed is None else summed + contrib
    return summed.reshape(stacks, canvases, out_rows, out_cols, weight.shape[-1])


def conv_input_grad(grad_pad, weight, out_rows, out_cols):
    stacks, canvases, outputs = (grad_pad.shape[0], grad_pad.shape[1], grad_pad.shape[-1])
    channels = weight.shape[1] // 9
    summed = None
    for row_off in range(3):
        for col_off in range(3):
            tap_index = row_off * 3 + col_off
            window = grad_pad[
                :, :, 2 - row_off : 2 - row_off + out_rows, 2 - col_off : 2 - col_off + out_cols, :
            ].reshape(stacks, -1, outputs)
            contrib = jnp.einsum(
                "snm,skm->snk",
                window,
                weight[:, tap_index * channels : (tap_index + 1) * channels, :],
                preferred_element_type=jnp.float32,
            )
            summed = contrib if summed is None else summed + contrib
    return summed.reshape(stacks, canvases, out_rows, out_cols, channels)


def conv_weight_grad(padded, grads):
    stacks, channels = (padded.shape[0], padded.shape[-1])
    out_rows, out_cols = (grads.shape[2], grads.shape[3])
    flat_grads = grads.reshape(stacks, -1, grads.shape[-1])
    pieces = []
    for row_off in range(3):
        for col_off in range(3):
            window = padded[
                :, :, row_off : row_off + out_rows, col_off : col_off + out_cols, :
            ].reshape(stacks, -1, channels)
            pieces.append(
                jnp.einsum("snk,snm->skm", window, flat_grads, preferred_element_type=jnp.float32)
            )
    return jnp.concatenate(pieces, 1)


def adam_update(weight, grad, first, second, step_float, decay):
    first_new = beta_one * first + (1.0 - beta_one) * grad
    second_new = beta_two * second + (1.0 - beta_two) * grad * grad
    first_hat = first_new / (1.0 - jnp.power(beta_one, step_float))
    second_hat = second_new / (1.0 - jnp.power(beta_two, step_float))
    weight_new = weight - learn_rate * (
        first_hat / (jnp.sqrt(second_hat) + adam_eps) + decay * weight
    )
    return (weight_new, first_new, second_new)


def anchor_masks(label_rows, positive_rows, row_flags, classes):
    valid = (label_rows >= 0) & row_flags[:, :, None, None]
    chosen = valid & (positive_rows > 0)
    targets = (
        (label_rows[..., None] == jnp.arange(classes, dtype=jnp.int32)) & chosen[..., None]
    ).astype(jnp.float32)
    return (valid.astype(jnp.float32), chosen.astype(jnp.float32), targets)


def focal_terms(cls_vals, targets, valid_f):
    logit_view = cls_vals.reshape(targets.shape)
    prob = jax.nn.sigmoid(logit_view)
    cross = jax.nn.softplus(logit_view) - targets * logit_view
    prob_true = prob * targets + (1.0 - prob) * (1.0 - targets)
    alpha_weight = focal_alpha * targets + (1.0 - focal_alpha) * (1.0 - targets)
    return jnp.sum(alpha_weight * (1.0 - prob_true) ** 2 * cross * valid_f[..., None])


def smooth_terms(box_vals, goals, chosen_f):
    diff = box_vals.reshape(chosen_f.shape + (4,)) - goals.reshape(chosen_f.shape + (4,))
    abs_diff = jnp.abs(diff)
    smooth = jnp.where(
        abs_diff < smooth_beta, 0.5 * diff * diff / smooth_beta, abs_diff - 0.5 * smooth_beta
    )
    return jnp.sum(smooth * chosen_f[..., None])


def plain_shards(
    features,
    crop_ids,
    labels,
    positive,
    box_targets,
    tower_weights,
    head_weights,
    biases,
    tower_m,
    tower_v,
    head_m,
    head_v,
    bias_m,
    bias_v,
    step_count,
):
    canvases, row_count, col_count, channels = features.shape
    layers = tower_weights.shape[0]
    anchors = labels.shape[-1]
    head_out = head_weights.shape[1]
    box_out = 4 * anchors
    cls_out = head_out - box_out
    classes = cls_out // anchors
    shard = lax.axis_index("tower")
    tower_low, head_stack = (
        lax.all_gather(tower_weights.astype(jnp.bfloat16), ("dp", "tower"), axis=2, tiled=True),
        lax.all_gather(
            head_weights.astype(jnp.bfloat16)[None, None], ("dp", "tower"), axis=2, tiled=True
        ),
    )
    head_low = head_stack[0, 0]
    tower_bias = biases[: 2 * layers * channels].reshape(layers, 2, channels)
    head_bias = biases[2 * layers * channels :]
    cls_weight = head_low[:, :cls_out][None]
    box_weight = head_low[:, cls_out:][None]
    same_rows = crop_ids[:, 1:] == crop_ids[:, :-1]
    edge_true = jnp.ones((crop_ids.shape[0], 1), dtype=jnp.bool_)
    row_ok = jnp.concatenate([edge_true, same_rows], 1) & jnp.concatenate([same_rows, edge_true], 1)
    own_ok = lax.dynamic_slice_in_dim(row_ok, shard * row_count, row_count, 1)
    own_valid, own_chosen, own_targets = anchor_masks(labels, positive, own_ok, classes)
    count_all = lax.psum(jnp.sum(own_chosen), ("dp", "tower"))
    denom = jnp.maximum(count_all, 1.0)
    grad_scale = 1.0 / denom
    kept = []
    preact = []
    current = features[None]
    for layer in range(layers):
        padded = pad_cols(act_rim(current))
        if layer == 0:
            padded = jnp.broadcast_to(padded, (2,) + padded.shape[1:])
        kept.append(padded)
        summed = (
            conv_forward(padded, tower_low[layer], row_count, col_count)
            + tower_bias[layer][:, None, None, None, :]
        )
        preact.append(summed)
        current = silu_value(summed).astype(jnp.bfloat16)
    head_in = pad_cols(act_rim(current))
    kept.append(head_in)
    cls_raw = conv_forward(head_in[0:1], cls_weight, row_count, col_count)[0] + head_bias[:cls_out]
    box_raw = conv_forward(head_in[1:2], box_weight, row_count, col_count)[0] + head_bias[cls_out:]
    focal_value, focal_back = jax.vjp(
        partial(focal_terms, targets=own_targets, valid_f=own_valid), cls_raw
    )
    smooth_value, smooth_back = jax.vjp(
        partial(smooth_terms, goals=box_targets, chosen_f=own_chosen), box_raw
    )
    loss_local = focal_value + smooth_value
    cls_low = focal_back(grad_scale)[0].astype(jnp.bfloat16)
    box_low = smooth_back(grad_scale)[0].astype(jnp.bfloat16)
    head_wgrad = jnp.concatenate(
        [
            conv_weight_grad(head_in[0:1], cls_low[None])[0],
            conv_weight_grad(head_in[1:2], box_low[None])[0],
        ],
        1,
    )
    head_bgrad = jnp.concatenate(
        [
            jnp.sum(cls_low, axis=(0, 1, 2), dtype=jnp.float32),
            jnp.sum(box_low, axis=(0, 1, 2), dtype=jnp.float32),
        ]
    )
    joined = pad_cols(grad_rim(jnp.concatenate([cls_low, box_low], -1)[None]))
    upstream = jnp.concatenate(
        [
            conv_input_grad(joined[..., :cls_out], cls_weight, row_count, col_count),
            conv_input_grad(joined[..., cls_out:], box_weight, row_count, col_count),
        ],
        0,
    )
    tower_grads = [None] * layers
    bias_grads = [None] * layers
    for layer in reversed(range(layers)):
        grad_low = (upstream * silu_slope(preact[layer])).astype(jnp.bfloat16)
        bias_grads[layer] = jnp.sum(grad_low, axis=(1, 2, 3), dtype=jnp.float32)
        tower_grads[layer] = conv_weight_grad(kept[layer], grad_low)
        padded_grad = pad_cols(grad_rim(grad_low))
        upstream = conv_input_grad(padded_grad, tower_low[layer], row_count, col_count)
    feature_grad = upstream[0] + upstream[1]
    tower_shard, head_pair = (
        lax.psum_scatter(
            jnp.stack(tower_grads, 0), ("dp", "tower"), scatter_dimension=2, tiled=True
        ),
        lax.psum_scatter(head_wgrad[None, None], ("dp", "tower"), scatter_dimension=2, tiled=True),
    )
    head_shard = head_pair[0, 0]
    bias_local = jnp.concatenate([jnp.stack(bias_grads, 0).reshape(-1), head_bgrad])
    logits_out = cls_raw.astype(jnp.bfloat16)
    deltas_out = box_raw.astype(jnp.bfloat16)
    bias_grad, loss_total = lax.psum((bias_local, loss_local), ("dp", "tower"))
    loss = loss_total / denom
    step_float = step_count[0].astype(jnp.float32)
    tower_new, tower_m_new, tower_v_new = adam_update(
        tower_weights, tower_shard, tower_m, tower_v, step_float, decay_rate
    )
    head_new, head_m_new, head_v_new = adam_update(
        head_weights, head_shard, head_m, head_v, step_float, decay_rate
    )
    bias_new, bias_m_new, bias_v_new = adam_update(
        biases, bias_grad, bias_m, bias_v, step_float, 0.0
    )
    split_at = bias_grad.shape[0] - box_out
    return (
        logits_out,
        deltas_out,
        loss,
        feature_grad,
        tower_shard[:, 0],
        tower_shard[:, 1],
        head_shard,
        bias_grad[:split_at],
        bias_grad[split_at:],
        tower_new,
        head_new,
        bias_new,
        tower_m_new,
        tower_v_new,
        head_m_new,
        head_v_new,
        bias_m_new,
        bias_v_new,
        tower_new.astype(jnp.bfloat16),
        head_new.astype(jnp.bfloat16),
    )


MESH = pl.DeviceIdType.MESH
low = jnp.bfloat16
full = jnp.float32
LANES = 128
CUT = 256


def mega_kernel(
    feat, code, goals, tow, hed, bias,
    logits, deltas, fgrad, tgrad, hgrad, bsum, loss_out,
    W, D, RD, RY, RZ, RX, RP, A3, HA, G, Z, U, ACC, FP, CP, GP, LS, ES, FS, FR, CNT, BG, BR,
    ps, pr, zs, zr, ys, yr, ds, dr, xs, xr, fs, fr, hs, hr, gs, gr, ls, lr, es, er,
    rds, rdr, rys, ryr, rzs, rzr, rxs, rxr, rps, rpr, ns, nr, bs, br,
    *, rows, cols, layers, cls_out, box_out, anchors, piece,
):
    d = lax.axis_index("dp")
    z = lax.axis_index("tower")
    k = lax.rem(d, 2)
    x = lax.rem(d // 2, 2)
    y = d // 4
    sib = d + 1 - 2 * k
    par = d + 2 - 4 * x
    yn = d + 4 - 8 * y
    is_cls = x == 0
    is_box = x == 1
    block = 4 * piece
    px = rows * cols
    classes = cls_out // anchors

    def remote(src, dst, send, recv, dev):
        return pltpu.make_async_remote_copy(
            src_ref=src, dst_ref=dst, send_sem=send, recv_sem=recv, device_id=dev, device_id_type=MESH
        )

    def blk(yy, xx, kk):
        return pl.ds(((yy * 2 + xx) * 2 + kk) * block, block)

    def pcs(yy, xx, kk, zz):
        return pl.ds(((yy * 2 + xx) * 2 + kk) * block + zz * piece, piece)

    def zpeer(o):
        return lax.rem(z + o, 4)

    def zfrom(o):
        return lax.rem(z + 4 - o, 4)

    barrier = pltpu.get_barrier_semaphore()
    for dev in [(sib, z), (par, z), (yn, z)] + [(d, zpeer(o)) for o in (1, 2, 3)]:
        pl.semaphore_signal(barrier, inc=1, device_id=dev, device_id_type=MESH)
    pl.semaphore_wait(barrier, 6)

    def slot_of(step):
        return jnp.where(step == 4, 4 + 2 * x, step)

    def p_send(step):
        return remote(
            tow.at[step, 1 - x], W.at[step, pcs(y, x, k, z)], ps.at[step], pr.at[step], (par, z)
        )

    def p_head(cut, index):
        return remote(
            hed.at[cut], W.at[4 + cut, pcs(y, x, k, z)], ps.at[index], pr.at[index], (par, z)
        )

    def p_recv(step):
        slot = slot_of(step)
        there = W.at[slot, pcs(y, 1 - x, k, z)]
        return remote(there, there, ps.at[step], pr.at[step], (par, z))

    def z_send(step, xx, o):
        here = W.at[slot_of(step), pcs(y, xx, k, z)]
        return remote(here, here, zs.at[step, xx, o - 1], zr.at[step, xx, o - 1], (d, zpeer(o)))

    def z_recv(step, xx, o):
        here = W.at[slot_of(step), pcs(y, xx, k, zfrom(o))]
        return remote(here, here, zs.at[step, xx, o - 1], zr.at[step, xx, o - 1], (d, zpeer(o)))

    def y_copy(step, xx, yy):
        here = W.at[slot_of(step), blk(yy, xx, k)]
        return remote(here, here, ys.at[step, xx], yr.at[step, xx], (yn, z))

    def d_copy(slot, yy, xx, kk):
        here = W.at[slot, blk(yy, xx, kk)]
        return remote(here, here, ds.at[slot, yy * 2 + xx], dr.at[slot, yy * 2 + xx], (sib, z))

    def x_copy(yy, xx):
        here = W.at[6, blk(yy, xx, k)]
        return remote(here, here, xs.at[yy * 2 + xx], xr.at[yy * 2 + xx], (par, z))

    def has(step):
        return (step < 5) | is_cls

    def do_z(step):
        @pl.when(has(step))
        def _():
            p_recv(step).wait_recv()
            for o in (1, 3, 2):
                for xx in range(2):
                    z_send(step, xx, o).start()

    def spread(step, yy):
        slot = slot_of(step)
        for xx in range(2):
            d_copy(slot, yy, xx, k).start()

        @pl.when(is_box & (step == 4))
        def _():
            for xx in range(2):
                x_copy(yy, xx).start()

    def do_y(step):
        @pl.when(has(step))
        def _():
            for xx in range(2):
                for o in (1, 2, 3):
                    z_recv(step, xx, o).wait_recv()
            for xx in range(2):
                y_copy(step, xx, y).start()
            spread(step, y)

    def do_d(step):
        @pl.when(has(step))
        def _():
            for xx in range(2):
                y_copy(step, xx, 1 - y).wait_recv()
            spread(step, 1 - y)

    def gathered(slot):
        for b in range(4):
            d_copy(slot, b // 2, b % 2, 1 - k).wait_recv()

    for step in range(4):
        p_send(step).start()
        if step == 0:
            pltpu_feature = remote(feat, FP, fs.at[0], fr.at[0], (par, z))
        W[step, pcs(y, x, k, z)] = tow[step, x]
    pltpu_feature.start()

    @pl.when(is_cls)
    def _():
        p_head(2, 4).start()
        W[4, pcs(y, x, k, z)] = hed[0]
        W[5, pcs(y, x, k, z)] = hed[1]

    @pl.when(is_box)
    def _():
        p_head(0, 4).start()
        p_head(1, 5).start()
        W[6, pcs(y, x, k, z)] = hed[2]

    code_copy = remote(code, CP.at[x], fs.at[1], fr.at[1], (par, z))
    code_copy.start()
    goal_copy = remote(goals, GP.at[x], fs.at[2], fr.at[2], (par, z))
    CP[x] = code[...]
    GP[x] = goals[...]

    @pl.when(is_cls)
    def _():
        goal_copy.start()

    do_z(0)
    do_z(1)

    def n_copy(index, dst, dev):
        return remote(CNT.at[index], CNT.at[dst], ns.at[dst], nr.at[dst], dev)

    picked = (code[...].astype(full) < -110.0).astype(full)
    CNT[0] = jnp.broadcast_to(jnp.sum(picked.reshape(px // 8, 8, LANES), axis=0).sum(), (8, LANES))
    n_copy(0, 4, (sib, z)).start()

    col = lax.broadcasted_iota(jnp.int32, (cols, CUT), 0)
    first_col = col == 0
    last_col = col == cols - 1

    def move_right(v):
        return jnp.where(first_col, 0.0, pltpu.roll(v, 1, 0))

    def move_left(v):
        return jnp.where(last_col, 0.0, pltpu.roll(v, cols - 1, 0))

    def put_row(layer, cv, row, value):
        at = pl.ds(pl.multiple_of(row * cols, cols), cols)
        A3[layer, cv, at, 0:CUT] = move_right(value).astype(low)
        A3[layer, cv, at, CUT : 2 * CUT] = value.astype(low)
        A3[layer, cv, at, 2 * CUT : 3 * CUT] = move_left(value).astype(low)

    def up_ok():
        return z > 0

    def down_ok():
        return z < 3

    def a_edge(layer, side, cv):
        row = rows if side == 0 else 1
        src = A3.at[layer, cv, pl.ds(row * cols, cols), pl.ds(CUT, CUT)]
        dev = (d, lax.rem(z + 1, 4)) if side == 0 else (d, lax.rem(z + 3, 4))
        return remote(src, HA.at[layer, side, cv], hs.at[layer, side, cv], hr.at[layer, side, cv], dev)

    def send_edges(layer, cvs):
        @pl.when(down_ok())
        def _():
            for cv in cvs:
                a_edge(layer, 0, cv).start()

        @pl.when(up_ok())
        def _():
            for cv in cvs:
                a_edge(layer, 1, cv).start()

    def take_edges(layer):
        @pl.when(up_ok())
        def _():
            for cv in range(2):
                a_edge(layer, 0, cv).wait_recv()
                put_row(layer, cv, 0, HA[layer, 0, cv].astype(full))

        @pl.when(down_ok())
        def _():
            for cv in range(2):
                a_edge(layer, 1, cv).wait_recv()
                put_row(layer, cv, rows + 1, HA[layer, 1, cv].astype(full))

    def g_edge(slot, side, cv):
        src = G.at[slot, cv, pl.ds((rows if side == 0 else 1) * cols, cols)]
        dst = G.at[slot, cv, pl.ds(0 if side == 0 else (rows + 1) * cols, cols)]
        dev = (d, lax.rem(z + 1, 4)) if side == 0 else (d, lax.rem(z + 3, 4))
        return remote(src, dst, gs.at[slot, side, cv], gr.at[slot, side, cv], dev)

    def g_recv(slot, side, cv):
        dst = G.at[slot, cv, pl.ds(0 if side == 0 else (rows + 1) * cols, cols)]
        return remote(dst, dst, gs.at[slot, side, cv], gr.at[slot, side, cv], (d, lax.rem(z + 1, 4)))

    def send_g(slot):
        @pl.when(down_ok())
        def _():
            for cv in range(2):
                g_edge(slot, 0, cv).start()

        @pl.when(up_ok())
        def _():
            for cv in range(2):
                g_edge(slot, 1, cv).start()

    def take_g(slot):
        @pl.when(up_ok())
        def _():
            for cv in range(2):
                g_recv(slot, 0, cv).wait_recv()

        @pl.when(down_ok())
        def _():
            for cv in range(2):
                g_recv(slot, 1, cv).wait_recv()

    def fill(layer_src, cv):
        def body(r, carry):
            put_row(0, cv, r + 1, layer_src[pl.ds(pl.multiple_of(r * cols, cols), cols), :].astype(full))
            return carry

        lax.fori_loop(0, rows, body, 0)

    fill(feat, x)
    send_edges(0, [x])

    def clear(at, layer_count, slot_count):
        def a_body(layer, carry):
            for cv in range(2):
                A3[layer, cv, at, :] = jnp.zeros((cols, 3 * CUT), low)
            return carry

        def g_body(slot, carry):
            for cv in range(2):
                G[slot, cv, at, :] = jnp.zeros((cols, CUT), low)
            return carry

        lax.fori_loop(0, layer_count, a_body, 0)
        lax.fori_loop(0, slot_count, g_body, 0)

    @pl.when(z == 0)
    def _():
        clear(pl.ds(0, cols), layers + 1, layers + 3)

    @pl.when(z == 3)
    def _():
        clear(pl.ds((rows + 1) * cols, cols), layers + 1, layers + 3)

    BG[...] = jnp.zeros((8, CUT), full)

    n_copy(0, 4, (sib, z)).wait_recv()
    CNT[1] = CNT[0] + CNT[4]
    n_copy(1, 5, (yn, z)).start()
    do_y(0)
    do_z(2)
    n_copy(1, 5, (yn, z)).wait_recv()
    CNT[2] = CNT[1] + CNT[5]
    n_copy(2, 6, (par, z)).start()
    pltpu_feature.wait_recv()
    fill(FP, 1 - x)
    send_edges(0, [1 - x])
    n_copy(2, 6, (par, z)).wait_recv()
    CNT[3] = CNT[2] + CNT[6]
    for o in (1, 2, 3):
        n_copy(3, 6 + o, (d, zpeer(o))).start()
    do_y(1)
    do_d(0)
    do_z(3)

    def conv(layer, slot, cv):
        total = None
        for dy in range(3):
            term = jnp.dot(
                A3[layer, cv, pl.ds(dy * cols, px), :],
                W[slot, pl.ds(dy * 96, 96)].reshape(3 * CUT, CUT),
                preferred_element_type=full,
            )
            total = term if total is None else total + term
        return total

    def forward(layer, carry):
        gathered(layer)
        take_edges(layer)
        shift = bias[pl.ds(2 * layer + x, 1), :]

        def canvas(cv, carry):
            Z[layer, cv] = conv(layer, layer, cv)

            def row(r, carry):
                at = pl.ds(pl.multiple_of(r * cols, cols), cols)
                value = Z[layer, cv, at, :] + shift
                Z[layer, cv, at, :] = value
                put_row(layer + 1, cv, r + 1, silu_value(value))
                return carry

            lax.fori_loop(0, rows, row, 0)
            return carry

        lax.fori_loop(0, 2, canvas, 0)
        send_edges(layer + 1, range(2))
        do_y_when = layer + 2
        do_y(do_y_when)
        do_d(layer + 1)

        @pl.when(layer < 2)
        def _():
            do_z(layer + 4)

        return carry

    lax.fori_loop(0, layers, forward, 0)
    do_d(5)
    for o in (1, 2, 3):
        n_copy(3, 6 + o, (d, zpeer(o))).wait_recv()
    count = CNT[3] + CNT[7] + CNT[8] + CNT[9]
    grad_scale = (1.0 / jnp.maximum(count, 1.0))[0:1, 0:1]
    take_edges(layers)

    def rd_send(slot, b):
        src = D.at[slot, blk(b // 2, b % 2, 1 - k)]
        return remote(src, RD.at[slot, b], rds.at[slot, b], rdr.at[slot, b], (sib, z))

    def ry_send(slot, xx):
        src = D.at[slot, blk(1 - y, xx, k)]
        return remote(src, RY.at[slot, xx], rys.at[slot, xx], ryr.at[slot, xx], (yn, z))

    def rz_send(slot, xx, o):
        src = D.at[slot, pcs(y, xx, k, zpeer(o))]
        return remote(
            src, RZ.at[slot, xx, o - 1], rzs.at[slot, xx, o - 1], rzr.at[slot, xx, o - 1], (d, zpeer(o))
        )

    def rx_send(b):
        src = D.at[6, blk(b // 2, b % 2, k)]
        return remote(src, RX.at[b], rxs.at[b], rxr.at[b], (par, z))

    def add_into(slot, place, terms):
        units = block // 3

        def body(i, carry):
            here = pl.ds(place + i * units, units)
            there = pl.ds(i * units, units)
            total = D[slot, here].astype(full)
            for ref in terms:
                total = total + ref[there].astype(full)
            D[slot, here] = total.astype(low)
            return carry

        lax.fori_loop(0, 3, body, 0)

    def start_of(yy, xx, kk):
        return ((yy * 2 + xx) * 2 + kk) * block

    def do_rd(slot):
        for b in range(4):
            rd_send(slot, b).start()

    def do_ry(slot, relay=False):
        for xx in range(2):
            b = (1 - y) * 2 + xx
            rd_send(slot, b).wait_recv()
            terms = [RD.at[slot, b]]
            if relay:
                rx_send(b).wait_recv()
                terms.append(RX.at[b])
            add_into(slot, start_of(1 - y, xx, k), terms)
            ry_send(slot, xx).start()
        for xx in range(2):
            b = y * 2 + xx
            rd_send(slot, b).wait_recv()
            terms = [RD.at[slot, b]]
            if relay:
                rx_send(b).wait_recv()
                terms.append(RX.at[b])
            add_into(slot, start_of(y, xx, k), terms)

    def do_rx():
        for b in range(4):
            rd_send(6, b).wait_recv()
            add_into(6, start_of(b // 2, b % 2, k), [RD.at[6, b]])
            rx_send(b).start()

    def do_rz(slot):
        for xx in range(2):
            ry_send(slot, xx).wait_recv()
            add_into(slot, start_of(y, xx, k), [RY.at[slot, xx]])
            for o in (2, 1, 3):
                rz_send(slot, xx, o).start()

    def piece_sum(slot, xx):
        total = D[slot, pcs(y, xx, k, z)].astype(full)
        for o in (1, 2, 3):
            rz_send(slot, xx, o).wait_recv()
            total = total + RZ[slot, xx, o - 1].astype(full)
        return total

    def rp_send(slot, dst):
        return remote(RP.at[slot], dst, rps.at[slot], rpr.at[slot], (par, z))

    def do_rp(slot, dst_own, dst_other):
        RP[slot] = piece_sum(slot, 1 - x)
        rp_send(slot, dst_other).start()
        dst_own[...] = piece_sum(slot, x)

    def do_rp_layer(layer):
        do_rp(layer, tgrad.at[layer, x], tgrad.at[layer, x])

    def do_rp_head(slot):
        do_rp(slot, hgrad.at[slot - 4], hgrad.at[slot - 4])

    def weight_grad(layer, slot):
        for dy in range(3):
            total = None
            for cv in range(2):
                term = lax.dot_general(
                    A3[layer, cv, pl.ds(dy * cols, px), :],
                    G[slot, cv, pl.ds(cols, px), :],
                    (((0,), (0,)), ((), ())),
                    preferred_element_type=full,
                )
                total = term if total is None else total + term
            D[slot, pl.ds(dy * 96, 96)] = total.astype(low).reshape(96, 8, CUT)

    def input_grad(slot, add):
        def canvas(cv, carry):
            for dx in range(3):
                total = None
                for dy in range(3):
                    term = lax.dot_general(
                        G[slot, cv, pl.ds((2 - dy) * cols, px), :],
                        W[slot, pl.ds((3 * dy + dx) * 32, 32)].reshape(CUT, CUT),
                        (((1,), (1,)), ((), ())),
                        preferred_element_type=full,
                    )
                    total = term if total is None else total + term
                if add:
                    U[dx, cv] = U[dx, cv] + total
                else:
                    U[dx, cv] = total
            return carry

        lax.fori_loop(0, 2, canvas, 0)

    def upstream_row(cv, r):
        at = pl.ds(pl.multiple_of(r * cols, cols), cols)
        return U[1, cv, at, :] + move_left(U[0, cv, at, :]) + move_right(U[2, cv, at, :])

    def fold(value):
        return jnp.sum(value.reshape(cols // 8, 8, CUT), axis=0)

    lane = lax.broadcasted_iota(jnp.int32, (1, CUT), 1)
    lane_tab = lax.broadcasted_iota(jnp.int32, (LANES, CUT), 1)
    anchor_tab = lax.broadcasted_iota(jnp.int32, (LANES, CUT), 0)
    box_from = cls_out - 2 * CUT

    def cls_rows(cut, cv, shift):
        channel = lane_tab + cut * CUT
        spread_tab = (
            (channel >= anchor_tab * classes) & (channel < (anchor_tab + 1) * classes) & (channel < cls_out)
        ).astype(full).astype(low)
        here = lane + cut * CUT
        number = here
        for a in range(1, anchors):
            number = number - jnp.where(here >= a * classes, classes, 0)
        number = number.astype(full) - 200.0

        def row(r, carry):
            b_sum, l_sum = carry
            at = pl.ds(pl.multiple_of(r * cols, cols), cols)
            raw = ACC[at, :] + shift
            LS[cut, cv, at, :] = raw.astype(low)
            marks = jnp.dot(CP[cv, at, :], spread_tab, preferred_element_type=full)
            hit = marks == number
            seen = marks < -50.0
            s = jnp.where(hit, -raw, raw)
            e = jnp.exp(-jnp.abs(s))
            inv = 1.0 / (1.0 + e)
            other = e * inv
            q = jnp.where(s >= 0.0, inv, other)
            p = jnp.where(s >= 0.0, other, inv)
            soft = jnp.maximum(s, 0.0) + jnp.log1p(e)
            t = jnp.where(seen, jnp.where(hit, focal_alpha, 1.0 - focal_alpha), 0.0) * q * q
            slope = t * (2.0 * p * soft + q) * grad_scale
            g = jnp.where(hit, -slope, slope).astype(low)
            G[4 + cut, cv, pl.ds(pl.multiple_of((r + 1) * cols, cols), cols), :] = g
            return b_sum + fold(g.astype(full)), l_sum + fold(t * soft)

        return row

    def box_rows(cut, cv, shift):
        spot = lane_tab - box_from
        spread_tab = (
            (spot >= anchor_tab * 4) & (spot < (anchor_tab + 1) * 4) & (anchor_tab < anchors)
        ).astype(full).astype(low)

        def row(r, carry):
            b_sum, l_sum = carry
            at = pl.ds(pl.multiple_of(r * cols, cols), cols)
            raw = ACC[at, :] + shift
            ES[cv, at, :] = raw.astype(low)
            marks = jnp.dot(CP[cv, at, :], spread_tab, preferred_element_type=full)
            chosen = marks < -110.0
            want = GP[cv, at, :]
            want = jnp.concatenate([jnp.zeros((cols, LANES), full), want], axis=1)
            diff = raw - want
            size = jnp.abs(diff)
            value = jnp.where(
                size < smooth_beta, 0.5 * diff * diff / smooth_beta, size - 0.5 * smooth_beta
            )
            slope = jnp.where(
                size < smooth_beta, diff / smooth_beta, jnp.where(diff > 0.0, 1.0, -1.0)
            )
            g = jnp.where(chosen, slope * grad_scale, 0.0).astype(low)
            G[4 + cut, cv, pl.ds(pl.multiple_of((r + 1) * cols, cols), cols), :] = g
            return b_sum + fold(g.astype(full)), l_sum + fold(jnp.where(chosen, value, 0.0))

        return row

    nothing = jnp.zeros((8, CUT), full)

    def l_copy(cut):
        return remote(LS.at[cut, 1 - x], logits.at[cut], ls.at[cut], lr.at[cut], (par, z))

    def e_copy():
        return remote(ES.at[1 - x], deltas, es.at[0], er.at[0], (par, z))

    U[...] = jnp.zeros(U.shape, full)
    remote(code, CP.at[1 - x], fs.at[1], fr.at[1], (par, z)).wait_recv()

    @pl.when(is_box)
    def _():
        remote(goals, GP.at[1 - x], fs.at[2], fr.at[2], (par, z)).wait_recv()

    def head(cut, carry):
        slot = 4 + cut

        @pl.when(is_cls & (cut == 2))
        def _():
            for b in range(4):
                x_copy(b // 2, b % 2).wait_recv()
                d_copy(6, b // 2, b % 2, k).start()

        gathered(slot)
        shift = bias[pl.ds(2 * layers + cut, 1), :]

        def canvas(cv, carry):
            b_sum, l_sum = carry
            ACC[...] = conv(layers, slot, cv)
            return lax.cond(
                is_cls,
                lambda: lax.fori_loop(0, rows, cls_rows(cut, cv, shift), (b_sum, l_sum)),
                lambda: lax.fori_loop(0, rows, box_rows(cut, cv, shift), (b_sum, l_sum)),
            )

        b_sum, l_sum = lax.fori_loop(0, 2, canvas, (nothing, nothing))
        send_g(slot)

        @pl.when(is_cls)
        def _():
            l_copy(cut).start()

        @pl.when(is_box)
        def _():
            e_copy().start()

        BG[pl.ds(slot, 1), :] = jnp.sum(b_sum, axis=0, keepdims=True)
        BG[pl.ds(7, 1), :] = BG[pl.ds(7, 1), :] + jnp.sum(l_sum, axis=0, keepdims=True)
        weight_grad(layers, slot)
        do_rd(slot)

        @pl.when(is_cls & (cut == 1))
        def _():
            do_ry(4)

        @pl.when(is_cls & (cut == 2))
        def _():
            do_ry(5)
            do_rz(4)

        take_g(slot)
        input_grad(slot, True)
        return carry

    lax.fori_loop(2 * x, 3, head, 0)

    @pl.when(is_cls)
    def _():
        do_rx()
        for cut in range(3):
            logits[cut] = LS[cut, 0]

    @pl.when(is_box)
    def _():
        deltas[...] = ES[1]

    def b_copy(src, dst, dev):
        return remote(src, BR.at[dst], bs.at[dst], br.at[dst], dev)

    def backward(j, carry):
        layer = layers - 1 - j

        def canvas(cv, b_sum):
            def row(r, b_sum):
                at = pl.ds(pl.multiple_of(r * cols, cols), cols)
                g = (upstream_row(cv, r) * silu_slope(Z[layer, cv, at, :])).astype(low)
                G[layer, cv, pl.ds(pl.multiple_of((r + 1) * cols, cols), cols), :] = g
                return b_sum + fold(g.astype(full))

            return lax.fori_loop(0, rows, row, b_sum)

        b_sum = lax.fori_loop(0, 2, canvas, nothing)
        send_g(layer)
        BG[pl.ds(layer, 1), :] = jnp.sum(b_sum, axis=0, keepdims=True)
        weight_grad(layer, layer)
        do_rd(layer)

        @pl.when(j == 3)
        def _():
            b_copy(BG, 0, (sib, z)).start()

        @pl.when(j > 0)
        def _():
            do_ry(layer + 1)

        @pl.when(j > 1)
        def _():
            do_rz(layer + 2)

        @pl.when(j > 2)
        def _():
            do_rp_layer(3)

        @pl.when(is_cls & (j == 0))
        def _():
            do_rz(5)
            do_rp_head(4)

        @pl.when(is_cls & (j == 1))
        def _():
            do_rp_head(5)

        @pl.when(is_box & (j == 1))
        def _():
            do_ry(6, relay=True)

        @pl.when(is_box & (j == 2))
        def _():
            do_rz(6)

        @pl.when(is_box & (j == 3))
        def _():
            do_rp_head(6)

        take_g(layer)
        input_grad(layer, False)
        return carry

    lax.fori_loop(0, layers, backward, 0)

    def feature_rows(cv, dst):
        def row(r, carry):
            dst[pl.ds(pl.multiple_of(r * cols, cols), cols), :] = upstream_row(cv, r)
            return carry

        lax.fori_loop(0, rows, row, 0)

    f_copy = remote(FS, FR, fs.at[3], fr.at[3], (par, z))
    feature_rows(1 - x, FS)
    f_copy.start()
    do_ry(0)
    do_rz(1)
    do_rp_layer(2)
    b_copy(BG, 0, (sib, z)).wait_recv()
    BR[6] = BG[...] + BR[0]
    b_copy(BR.at[6], 1, (yn, z)).start()
    feature_rows(x, fgrad)
    b_copy(BR.at[6], 1, (yn, z)).wait_recv()
    total = BR[6] + BR[1]
    for zz in range(4):
        @pl.when(z == zz)
        def _():
            BR[7 + zz] = total
            for o in (1, 2, 3):
                remote(
                    BR.at[7 + zz], BR.at[7 + zz], bs.at[1 + o], br.at[1 + o], (d, zpeer(o))
                ).start()
    do_rz(0)
    do_rp_layer(1)
    for o in (1, 2, 3):
        for zz in range(4):
            @pl.when(zfrom(o) == zz)
            def _():
                remote(
                    BR.at[7 + zz], BR.at[7 + zz], bs.at[1 + o], br.at[1 + o], (d, zpeer(o))
                ).wait_recv()
    total = (BR[7] + BR[8]) + (BR[9] + BR[10])
    BR[5] = total
    last = remote(BR.at[5], bsum.at[x], bs.at[5], br.at[5], (par, z))
    last.start()
    bsum[x] = total
    f_copy.wait_recv()
    fgrad[...] = fgrad[...] + FR[...]
    do_rp_layer(0)
    remote(BR.at[5], bsum.at[1 - x], bs.at[5], br.at[5], (par, z)).wait_recv()
    loss = jnp.sum(bsum[0, 7:8, :] + bsum[1, 7:8, :], axis=1, keepdims=True)
    loss_out[...] = jnp.broadcast_to(loss, (8, LANES)) / jnp.maximum(count, 1.0)

    for layer in range(layers):
        rp_send(layer, tgrad.at[layer, 1 - x]).wait_recv()

    @pl.when(is_cls)
    def _():
        rp_send(6, hgrad.at[2]).wait_recv()
        e_copy().wait_recv()
        for b in range(4):
            rx_send(b).wait_send()
            d_copy(6, b // 2, b % 2, k).wait_send()
        for cut in range(3):
            l_copy(cut).wait_send()
        p_head(2, 4).wait_send()
        goal_copy.wait_send()

    @pl.when(is_box)
    def _():
        for cut in range(2):
            rp_send(4 + cut, hgrad.at[cut]).wait_recv()
        for cut in range(3):
            l_copy(cut).wait_recv()
        for b in range(4):
            x_copy(b // 2, b % 2).wait_send()
            d_copy(6, b // 2, b % 2, k).wait_send()
        e_copy().wait_send()
        p_head(0, 4).wait_send()
        p_head(1, 5).wait_send()

    def close_gather(step, carry):
        for xx in range(2):
            for o in (1, 2, 3):
                z_send(step, xx, o).wait_send()
            y_copy(step, xx, y).wait_send()
        return carry

    lax.fori_loop(0, 6 - x, close_gather, 0)

    def close_slot(slot, carry):
        @pl.when((slot < 4) | is_cls)
        def _():
            for b in range(4):
                d_copy(slot, b // 2, b % 2, k).wait_send()

        return carry

    lax.fori_loop(0, 6 - 2 * x, close_slot, 0)

    def close_layer(layer, carry):
        @pl.when(layer < layers)
        def _():
            p_send(jnp.minimum(layer, layers - 1)).wait_send()

        @pl.when(down_ok())
        def _():
            for cv in range(2):
                a_edge(layer, 0, cv).wait_send()

        @pl.when(up_ok())
        def _():
            for cv in range(2):
                a_edge(layer, 1, cv).wait_send()

        return carry

    lax.fori_loop(0, layers + 1, close_layer, 0)

    def close_grad(slot, carry):
        @pl.when(is_cls | (slot < 4) | (slot == 6))
        def _():
            for b in range(4):
                rd_send(slot, b).wait_send()

            @pl.when(down_ok())
            def _():
                for cv in range(2):
                    g_edge(slot, 0, cv).wait_send()

            @pl.when(up_ok())
            def _():
                for cv in range(2):
                    g_edge(slot, 1, cv).wait_send()

        @pl.when((slot < 4) | (is_cls & (slot < 6)) | (is_box & (slot == 6)))
        def _():
            for xx in range(2):
                ry_send(slot, xx).wait_send()
                for o in (1, 2, 3):
                    rz_send(slot, xx, o).wait_send()
            rp_send(slot, RP.at[slot]).wait_send()

        return carry

    lax.fori_loop(0, layers + 3, close_grad, 0)
    pltpu_feature.wait_send()
    code_copy.wait_send()
    f_copy.wait_send()
    n_copy(0, 4, (sib, z)).wait_send()
    n_copy(1, 5, (yn, z)).wait_send()
    n_copy(2, 6, (par, z)).wait_send()
    b_copy(BG, 0, (sib, z)).wait_send()
    b_copy(BR.at[6], 1, (yn, z)).wait_send()
    for o in (1, 2, 3):
        n_copy(3, 6 + o, (d, zpeer(o))).wait_send()
        remote(BR.at[7], BR.at[7], bs.at[1 + o], br.at[1 + o], (d, zpeer(o))).wait_send()
    last.wait_send()


def finish_kernel(
    scal, lg, dl, fg, tg, hg, tw, hw, tm, tv, hm, hv,
    o_lg, o_dl, o_fg, o_tg, o_bg, o_hg, o_tn, o_hn, o_tm, o_tv, o_hm, o_hv, o_tc, o_hc,
    *, layers, cls_out, box_out,
):
    tail = cls_out - 2 * CUT

    def adam(weight, grad, first, second):
        first_new = beta_one * first + (1.0 - beta_one) * grad
        second_new = beta_two * second + (1.0 - beta_two) * grad * grad
        first_hat = first_new / scal[0]
        second_hat = second_new / scal[1]
        weight_new = weight - learn_rate * (
            first_hat / (jnp.sqrt(second_hat) + adam_eps) + decay_rate * weight
        )
        return weight_new, first_new, second_new

    def layer_body(layer, carry):
        for t in range(2):
            grad = tg[layer, t]
            (o_tg if t == 0 else o_bg)[layer] = grad
            w_new, m_new, v_new = adam(tw[layer, t], grad, tm[layer, t], tv[layer, t])
            o_tn[layer, t] = w_new
            o_tm[layer, t] = m_new
            o_tv[layer, t] = v_new
            o_tc[layer, t] = w_new.astype(low)
        return carry

    lax.fori_loop(0, layers, layer_body, 0)
    for cut, width in ((0, CUT), (1, CUT), (2, tail + box_out)):
        at = slice(cut * CUT, cut * CUT + width)
        grad = hg[cut][:, :width]
        o_hg[:, at] = grad
        w_new, m_new, v_new = adam(hw[:, at], grad, hm[:, at], hv[:, at])
        o_hn[:, at] = w_new
        o_hm[:, at] = m_new
        o_hv[:, at] = v_new
        o_hc[:, at] = w_new.astype(low)
        if cut < 2:
            o_lg[:, at] = lg[cut]
        else:
            o_lg[:, cut * CUT : cls_out] = lg[cut][:, :tail]
    o_dl[...] = dl[:, tail : tail + box_out]
    o_fg[...] = fg[...]


def fused_shards(
    features,
    crop_ids,
    labels,
    positive,
    box_targets,
    tower_weights,
    head_weights,
    biases,
    tower_m,
    tower_v,
    head_m,
    head_v,
    bias_m,
    bias_v,
    step_count,
):
    canvases, rows, cols, channels = features.shape
    layers = tower_weights.shape[0]
    shard_rows = tower_weights.shape[2]
    anchors = labels.shape[-1]
    head_out = head_weights.shape[1]
    box_out = 4 * anchors
    cls_out = head_out - box_out
    px = rows * cols
    piece = shard_rows // 8
    box_from = cls_out - 2 * CUT - LANES
    shard = lax.axis_index("tower")
    same_rows = crop_ids[:, 1:] == crop_ids[:, :-1]
    edge_true = jnp.ones((crop_ids.shape[0], 1), dtype=jnp.bool_)
    row_ok = jnp.concatenate([edge_true, same_rows], 1) & jnp.concatenate([same_rows, edge_true], 1)
    own_ok = lax.dynamic_slice_in_dim(row_ok, shard * rows, rows, 1)
    valid = (labels >= 0) & own_ok[:, :, None, None]
    code = jnp.where(valid, jnp.where(positive > 0, labels - 200, -100), 0).astype(low)
    code = jnp.pad(code.reshape(px, anchors), ((0, 0), (0, LANES - anchors)))
    goals = jnp.pad(
        box_targets.reshape(px, box_out), ((0, 0), (box_from, LANES - box_from - box_out))
    )
    tow = tower_weights.astype(low).reshape(layers, 2, piece, 8, channels)
    hed = jnp.pad(head_weights.astype(low), ((0, 0), (0, 3 * CUT - head_out)))
    hed = hed.reshape(shard_rows, 3, CUT).transpose(1, 0, 2).reshape(3, piece, 8, CUT)
    bias = jnp.pad(biases, (0, (2 * layers + 8) * CUT - biases.shape[0])).reshape(-1, CUT)
    units = 32 * piece
    block = 4 * piece
    dma = pltpu.SemaphoreType.DMA
    vm = pl.BlockSpec(memory_space=pltpu.VMEM)
    shape = jax.ShapeDtypeStruct
    logits, deltas, fgrad, tgrad, hgrad, bsum, loss = pl.pallas_call(
        partial(
            mega_kernel,
            rows=rows, cols=cols, layers=layers, cls_out=cls_out, box_out=box_out, anchors=anchors, piece=piece,
        ),
        out_shape=(
            shape((3, px, CUT), low),
            shape((px, CUT), low),
            shape((px, CUT), full),
            shape((layers, 2, piece, 8, CUT), full),
            shape((3, piece, 8, CUT), full),
            shape((2, 8, CUT), full),
            shape((8, LANES), full),
        ),
        in_specs=[vm] * 6,
        out_specs=[vm] * 7,
        scratch_shapes=[
            pltpu.VMEM((7, units, 8, CUT), low),
            pltpu.VMEM((7, units, 8, CUT), low),
            pltpu.VMEM((7, 4, block, 8, CUT), low),
            pltpu.VMEM((7, 2, block, 8, CUT), low),
            pltpu.VMEM((7, 2, 3, piece, 8, CUT), low),
            pltpu.VMEM((4, block, 8, CUT), low),
            pltpu.VMEM((7, piece, 8, CUT), full),
            pltpu.VMEM((layers + 1, 2, px + 2 * cols, 3 * CUT), low),
            pltpu.VMEM((layers + 1, 2, 2, cols, CUT), low),
            pltpu.VMEM((7, 2, px + 2 * cols, CUT), low),
            pltpu.VMEM((layers, 2, px, CUT), full),
            pltpu.VMEM((3, 2, px, CUT), full),
            pltpu.VMEM((px, CUT), full),
            pltpu.VMEM((px, CUT), low),
            pltpu.VMEM((2, px, LANES), low),
            pltpu.VMEM((2, px, LANES), full),
            pltpu.VMEM((3, 2, px, CUT), low),
            pltpu.VMEM((2, px, CUT), low),
            pltpu.VMEM((px, CUT), full),
            pltpu.VMEM((px, CUT), full),
            pltpu.VMEM((10, 8, LANES), full),
            pltpu.VMEM((8, CUT), full),
            pltpu.VMEM((11, 8, CUT), full),
            dma((6,)), dma((6,)),
            dma((6, 2, 3)), dma((6, 2, 3)),
            dma((6, 2)), dma((6, 2)),
            dma((7, 4)), dma((7, 4)),
            dma((4,)), dma((4,)),
            dma((4,)), dma((4,)),
            dma((layers + 1, 2, 2)), dma((layers + 1, 2, 2)),
            dma((7, 2, 2)), dma((7, 2, 2)),
            dma((3,)), dma((3,)),
            dma((1,)), dma((1,)),
            dma((7, 4)), dma((7, 4)),
            dma((7, 2)), dma((7, 2)),
            dma((7, 2, 3)), dma((7, 2, 3)),
            dma((4,)), dma((4,)),
            dma((7,)), dma((7,)),
            dma((10,)), dma((10,)),
            dma((6,)), dma((6,)),
        ],
        compiler_params=pltpu.CompilerParams(
            vmem_limit_bytes=60 * 1024 * 1024, collective_id=0, has_side_effects=True
        ),
    )(features.reshape(px, channels), code, goals, tow, hed, bias)

    step_float = step_count[0].astype(full)
    scal = jnp.stack([1.0 - jnp.power(beta_one, step_float), 1.0 - jnp.power(beta_two, step_float)])
    tgrad = tgrad.reshape(layers, 2, shard_rows, channels)
    hgrad = hgrad.reshape(3, shard_rows, CUT)
    tower_shape = tower_weights.shape
    head_shape = head_weights.shape
    outs = pl.pallas_call(
        partial(finish_kernel, layers=layers, cls_out=cls_out, box_out=box_out),
        out_shape=(
            shape((px, cls_out), low),
            shape((px, box_out), low),
            shape((px, channels), full),
            shape((layers, shard_rows, channels), full),
            shape((layers, shard_rows, channels), full),
            shape(head_shape, full),
            shape(tower_shape, full),
            shape(head_shape, full),
            shape(tower_shape, full),
            shape(tower_shape, full),
            shape(head_shape, full),
            shape(head_shape, full),
            shape(tower_shape, low),
            shape(head_shape, low),
        ),
        in_specs=[pl.BlockSpec(memory_space=pltpu.SMEM)] + [vm] * 11,
        out_specs=[vm] * 14,
        compiler_params=pltpu.CompilerParams(vmem_limit_bytes=40 * 1024 * 1024),
    )(scal, logits, deltas, fgrad, tgrad, hgrad, tower_weights, head_weights, tower_m, tower_v, head_m, head_v)
    (
        o_lg, o_dl, o_fg, o_tg, o_bg, o_hg, o_tn, o_hn, o_tm, o_tv, o_hm, o_hv, o_tc, o_hc,
    ) = outs
    tail = cls_out - 2 * CUT
    bias_grad = jnp.concatenate(
        [
            jnp.stack([bsum[0, :layers], bsum[1, :layers]], 1).reshape(-1),
            bsum[0, 4:7].reshape(-1)[:cls_out],
            bsum[1, 6, tail : tail + box_out],
        ]
    )
    bias_new, bias_m_new, bias_v_new = adam_update(biases, bias_grad, bias_m, bias_v, step_float, 0.0)
    split_at = bias_grad.shape[0] - box_out
    field = (canvases, rows, cols, -1)
    return (
        o_lg.reshape(field),
        o_dl.reshape(field),
        loss[0, 0],
        o_fg.reshape(field),
        o_tg,
        o_bg,
        o_hg,
        bias_grad[:split_at],
        bias_grad[split_at:],
        o_tn,
        o_hn,
        bias_new,
        o_tm,
        o_tv,
        o_hm,
        o_hv,
        bias_m_new,
        bias_v_new,
        o_tc,
        o_hc,
    )


def solution(mesh):
    placed = (
        P("dp", "tower", None, None),
        P("dp", None),
        P("dp", "tower", None, None),
        P("dp", "tower", None, None),
        P("dp", "tower", None, None),
        P(None, None, ("dp", "tower"), None),
        P(("dp", "tower"), None),
        P(),
        P(None, None, ("dp", "tower"), None),
        P(None, None, ("dp", "tower"), None),
        P(("dp", "tower"), None),
        P(("dp", "tower"), None),
        P(),
        P(),
        P(),
    )
    fused = mesh.shape["dp"] == 8 and mesh.shape["tower"] == 4
    return jax.shard_map(
        fused_shards if fused else plain_shards,
        mesh=mesh,
        in_specs=placed,
        out_specs=(
            P("dp", "tower", None, None),
            P("dp", "tower", None, None),
            P(),
            P("dp", "tower", None, None),
            P(None, ("dp", "tower"), None),
            P(None, ("dp", "tower"), None),
            P(("dp", "tower"), None),
            P(),
            P(),
            P(None, None, ("dp", "tower"), None),
            P(("dp", "tower"), None),
            P(),
            P(None, None, ("dp", "tower"), None),
            P(None, None, ("dp", "tower"), None),
            P(("dp", "tower"), None),
            P(("dp", "tower"), None),
            P(),
            P(),
            P(None, None, ("dp", "tower"), None),
            P(("dp", "tower"), None),
        ),
        check_vma=False,
    )
```

```python
import math
from functools import partial

import jax
import jax.numpy as jnp
from jax import lax
from jax.experimental import pallas as pl
from jax.experimental.pallas import tpu as pltpu
from jax.sharding import PartitionSpec as P

beta_one = 0.9
beta_two = 0.999
adam_eps = 1e-08
learn_rate = 0.03
decay_rate = 0.05
focal_alpha = 0.25
smooth_beta = 1.0 / 9.0


def with_halo(shard, sides, width):
    for axis, dim in sides:
        size, length = (lax.axis_size(axis), shard.shape[dim])
        up = [(i, (i + 1) % size) for i in range(size - 1)]
        down = [(j, i) for i, j in up]
        last = lax.slice_in_dim(shard, length - width, length, axis=dim)
        initial = lax.slice_in_dim(shard, 0, width, axis=dim)
        before = lax.ppermute(last, axis, up)
        after = lax.ppermute(initial, axis, down)
        shard = jnp.concatenate([before, shard, after], axis=dim)
    return shard


def act_rim(values):
    return with_halo(values, (("tower", 2),), 1)


def grad_rim(values):
    return with_halo(values, (("tower", 2),), 1)


def pad_cols(values):
    return jnp.pad(values, ((0, 0), (0, 0), (0, 0), (1, 1), (0, 0)))


def silu_value(values):
    return values * jax.nn.sigmoid(values)


def silu_slope(values):
    sig = jax.nn.sigmoid(values)
    return sig * (1.0 + values * (1.0 - sig))


def conv_forward(padded, weight, out_rows, out_cols):
    stacks, canvases, channels = (padded.shape[0], padded.shape[1], padded.shape[-1])
    summed = None
    for row_off in range(3):
        for col_off in range(3):
            tap_index = row_off * 3 + col_off
            window = padded[
                :, :, row_off : row_off + out_rows, col_off : col_off + out_cols, :
            ].reshape(stacks, -1, channels)
            contrib = jnp.einsum(
                "snk,skm->snm",
                window,
                weight[:, tap_index * channels : (tap_index + 1) * channels, :],
                preferred_element_type=jnp.float32,
            )
            summed = contrib if summed is None else summed + contrib
    return summed.reshape(stacks, canvases, out_rows, out_cols, weight.shape[-1])


def conv_input_grad(grad_pad, weight, out_rows, out_cols):
    stacks, canvases, outputs = (grad_pad.shape[0], grad_pad.shape[1], grad_pad.shape[-1])
    channels = weight.shape[1] // 9
    summed = None
    for row_off in range(3):
        for col_off in range(3):
            tap_index = row_off * 3 + col_off
            window = grad_pad[
                :, :, 2 - row_off : 2 - row_off + out_rows, 2 - col_off : 2 - col_off + out_cols, :
            ].reshape(stacks, -1, outputs)
            contrib = jnp.einsum(
                "snm,skm->snk",
                window,
                weight[:, tap_index * channels : (tap_index + 1) * channels, :],
                preferred_element_type=jnp.float32,
            )
            summed = contrib if summed is None else summed + contrib
    return summed.reshape(stacks, canvases, out_rows, out_cols, channels)


def conv_weight_grad(padded, grads):
    stacks, channels = (padded.shape[0], padded.shape[-1])
    out_rows, out_cols = (grads.shape[2], grads.shape[3])
    flat_grads = grads.reshape(stacks, -1, grads.shape[-1])
    pieces = []
    for row_off in range(3):
        for col_off in range(3):
            window = padded[
                :, :, row_off : row_off + out_rows, col_off : col_off + out_cols, :
            ].reshape(stacks, -1, channels)
            pieces.append(
                jnp.einsum("snk,snm->skm", window, flat_grads, preferred_element_type=jnp.float32)
            )
    return jnp.concatenate(pieces, 1)


def adam_update(weight, grad, first, second, step_float, decay):
    first_new = beta_one * first + (1.0 - beta_one) * grad
    second_new = beta_two * second + (1.0 - beta_two) * grad * grad
    first_hat = first_new / (1.0 - jnp.power(beta_one, step_float))
    second_hat = second_new / (1.0 - jnp.power(beta_two, step_float))
    weight_new = weight - learn_rate * (
        first_hat / (jnp.sqrt(second_hat) + adam_eps) + decay * weight
    )
    return (weight_new, first_new, second_new)


def anchor_masks(label_rows, positive_rows, row_flags, classes):
    valid = (label_rows >= 0) & row_flags[:, :, None, None]
    chosen = valid & (positive_rows > 0)
    targets = (
        (label_rows[..., None] == jnp.arange(classes, dtype=jnp.int32)) & chosen[..., None]
    ).astype(jnp.float32)
    return (valid.astype(jnp.float32), chosen.astype(jnp.float32), targets)


def focal_terms(cls_vals, targets, valid_f):
    logit_view = cls_vals.reshape(targets.shape)
    prob = jax.nn.sigmoid(logit_view)
    cross = jax.nn.softplus(logit_view) - targets * logit_view
    prob_true = prob * targets + (1.0 - prob) * (1.0 - targets)
    alpha_weight = focal_alpha * targets + (1.0 - focal_alpha) * (1.0 - targets)
    return jnp.sum(alpha_weight * (1.0 - prob_true) ** 2 * cross * valid_f[..., None])


def smooth_terms(box_vals, goals, chosen_f):
    diff = box_vals.reshape(chosen_f.shape + (4,)) - goals.reshape(chosen_f.shape + (4,))
    abs_diff = jnp.abs(diff)
    smooth = jnp.where(
        abs_diff < smooth_beta, 0.5 * diff * diff / smooth_beta, abs_diff - 0.5 * smooth_beta
    )
    return jnp.sum(smooth * chosen_f[..., None])


def plain_shards(
    features,
    crop_ids,
    labels,
    positive,
    box_targets,
    tower_weights,
    head_weights,
    biases,
    tower_m,
    tower_v,
    head_m,
    head_v,
    bias_m,
    bias_v,
    step_count,
):
    canvases, row_count, col_count, channels = features.shape
    layers = tower_weights.shape[0]
    anchors = labels.shape[-1]
    head_out = head_weights.shape[1]
    box_out = 4 * anchors
    cls_out = head_out - box_out
    classes = cls_out // anchors
    shard = lax.axis_index("tower")
    tower_low, head_stack = (
        lax.all_gather(tower_weights.astype(jnp.bfloat16), ("dp", "tower"), axis=2, tiled=True),
        lax.all_gather(
            head_weights.astype(jnp.bfloat16)[None, None], ("dp", "tower"), axis=2, tiled=True
        ),
    )
    head_low = head_stack[0, 0]
    tower_bias = biases[: 2 * layers * channels].reshape(layers, 2, channels)
    head_bias = biases[2 * layers * channels :]
    cls_weight = head_low[:, :cls_out][None]
    box_weight = head_low[:, cls_out:][None]
    same_rows = crop_ids[:, 1:] == crop_ids[:, :-1]
    edge_true = jnp.ones((crop_ids.shape[0], 1), dtype=jnp.bool_)
    row_ok = jnp.concatenate([edge_true, same_rows], 1) & jnp.concatenate([same_rows, edge_true], 1)
    own_ok = lax.dynamic_slice_in_dim(row_ok, shard * row_count, row_count, 1)
    own_valid, own_chosen, own_targets = anchor_masks(labels, positive, own_ok, classes)
    count_all = lax.psum(jnp.sum(own_chosen), ("dp", "tower"))
    denom = jnp.maximum(count_all, 1.0)
    grad_scale = 1.0 / denom
    kept = []
    preact = []
    current = features[None]
    for layer in range(layers):
        padded = pad_cols(act_rim(current))
        if layer == 0:
            padded = jnp.broadcast_to(padded, (2,) + padded.shape[1:])
        kept.append(padded)
        summed = (
            conv_forward(padded, tower_low[layer], row_count, col_count)
            + tower_bias[layer][:, None, None, None, :]
        )
        preact.append(summed)
        current = silu_value(summed).astype(jnp.bfloat16)
    head_in = pad_cols(act_rim(current))
    kept.append(head_in)
    cls_raw = conv_forward(head_in[0:1], cls_weight, row_count, col_count)[0] + head_bias[:cls_out]
    box_raw = conv_forward(head_in[1:2], box_weight, row_count, col_count)[0] + head_bias[cls_out:]
    focal_value, focal_back = jax.vjp(
        partial(focal_terms, targets=own_targets, valid_f=own_valid), cls_raw
    )
    smooth_value, smooth_back = jax.vjp(
        partial(smooth_terms, goals=box_targets, chosen_f=own_chosen), box_raw
    )
    loss_local = focal_value + smooth_value
    cls_low = focal_back(grad_scale)[0].astype(jnp.bfloat16)
    box_low = smooth_back(grad_scale)[0].astype(jnp.bfloat16)
    head_wgrad = jnp.concatenate(
        [
            conv_weight_grad(head_in[0:1], cls_low[None])[0],
            conv_weight_grad(head_in[1:2], box_low[None])[0],
        ],
        1,
    )
    head_bgrad = jnp.concatenate(
        [
            jnp.sum(cls_low, axis=(0, 1, 2), dtype=jnp.float32),
            jnp.sum(box_low, axis=(0, 1, 2), dtype=jnp.float32),
        ]
    )
    joined = pad_cols(grad_rim(jnp.concatenate([cls_low, box_low], -1)[None]))
    upstream = jnp.concatenate(
        [
            conv_input_grad(joined[..., :cls_out], cls_weight, row_count, col_count),
            conv_input_grad(joined[..., cls_out:], box_weight, row_count, col_count),
        ],
        0,
    )
    tower_grads = [None] * layers
    bias_grads = [None] * layers
    for layer in reversed(range(layers)):
        grad_low = (upstream * silu_slope(preact[layer])).astype(jnp.bfloat16)
        bias_grads[layer] = jnp.sum(grad_low, axis=(1, 2, 3), dtype=jnp.float32)
        tower_grads[layer] = conv_weight_grad(kept[layer], grad_low)
        padded_grad = pad_cols(grad_rim(grad_low))
        upstream = conv_input_grad(padded_grad, tower_low[layer], row_count, col_count)
    feature_grad = upstream[0] + upstream[1]
    tower_shard, head_pair = (
        lax.psum_scatter(
            jnp.stack(tower_grads, 0), ("dp", "tower"), scatter_dimension=2, tiled=True
        ),
        lax.psum_scatter(head_wgrad[None, None], ("dp", "tower"), scatter_dimension=2, tiled=True),
    )
    head_shard = head_pair[0, 0]
    bias_local = jnp.concatenate([jnp.stack(bias_grads, 0).reshape(-1), head_bgrad])
    logits_out = cls_raw.astype(jnp.bfloat16)
    deltas_out = box_raw.astype(jnp.bfloat16)
    bias_grad, loss_total = lax.psum((bias_local, loss_local), ("dp", "tower"))
    loss = loss_total / denom
    step_float = step_count[0].astype(jnp.float32)
    tower_new, tower_m_new, tower_v_new = adam_update(
        tower_weights, tower_shard, tower_m, tower_v, step_float, decay_rate
    )
    head_new, head_m_new, head_v_new = adam_update(
        head_weights, head_shard, head_m, head_v, step_float, decay_rate
    )
    bias_new, bias_m_new, bias_v_new = adam_update(
        biases, bias_grad, bias_m, bias_v, step_float, 0.0
    )
    split_at = bias_grad.shape[0] - box_out
    return (
        logits_out,
        deltas_out,
        loss,
        feature_grad,
        tower_shard[:, 0],
        tower_shard[:, 1],
        head_shard,
        bias_grad[:split_at],
        bias_grad[split_at:],
        tower_new,
        head_new,
        bias_new,
        tower_m_new,
        tower_v_new,
        head_m_new,
        head_v_new,
        bias_m_new,
        bias_v_new,
        tower_new.astype(jnp.bfloat16),
        head_new.astype(jnp.bfloat16),
    )


MESH = pl.DeviceIdType.MESH
low = jnp.bfloat16
full = jnp.float32
LANES = 128
CUT = 256


def mega_kernel(
    feat, crops, marked, lit, goals, tow, hed, bias_all,
    logits, deltas, fgrad, tgrad, hgrad, bsum, loss_out,
    W, D, RD, RY, RZ, RX, RP, A3, HA, G, Z, U, ACC, FP, CP, GP, LS, ES, FS, FR, CNT, BG, BR, TB, HB, bias,
    ps, pr, zs, zr, ys, yr, ds, dr, xs, xr, fs, fr, hs, hr, gs, gr, ls, lr, es, er,
    rds, rdr, rys, ryr, rzs, rzr, rxs, rxr, rps, rpr, ns, nr, bs, br,
    *, rows, cols, layers, cls_out, box_out, anchors, piece,
):
    d = lax.axis_index("dp")
    z = lax.axis_index("tower")
    k = lax.rem(d, 2)
    x = lax.rem(d // 2, 2)
    y = d // 4
    sib = d + 1 - 2 * k
    par = d + 2 - 4 * x
    yn = d + 4 - 8 * y
    is_cls = x == 0
    is_box = x == 1
    block = 4 * piece
    px = rows * cols
    classes = cls_out // anchors

    def remote(src, dst, send, recv, dev):
        return pltpu.make_async_remote_copy(
            src_ref=src, dst_ref=dst, send_sem=send, recv_sem=recv, device_id=dev, device_id_type=MESH
        )

    def blk(yy, xx, kk):
        return pl.ds(((yy * 2 + xx) * 2 + kk) * block, block)

    def pcs(yy, xx, kk, zz):
        return pl.ds(((yy * 2 + xx) * 2 + kk) * block + zz * piece, piece)

    def zpeer(o):
        return lax.rem(z + o, 4)

    def zfrom(o):
        return lax.rem(z + 4 - o, 4)

    barrier = pltpu.get_barrier_semaphore()
    for dev in [(sib, z), (par, z), (yn, z)] + [(d, zpeer(o)) for o in (1, 2, 3)]:
        pl.semaphore_signal(barrier, inc=1, device_id=dev, device_id_type=MESH)
    pl.semaphore_wait(barrier, 6)

    def slot_of(step):
        return jnp.where(step == 4, 4 + 2 * x, step)

    def p_send(step):
        return remote(
            TB.at[step], W.at[step, pcs(y, x, k, z)], ps.at[step], pr.at[step], (par, z)
        )

    def p_head(cut, index):
        return remote(
            HB.at[cut], W.at[4 + cut, pcs(y, x, k, z)], ps.at[index], pr.at[index], (par, z)
        )

    def p_recv(step):
        slot = slot_of(step)
        there = W.at[slot, pcs(y, 1 - x, k, z)]
        return remote(there, there, ps.at[step], pr.at[step], (par, z))

    def z_send(step, xx, o):
        here = W.at[slot_of(step), pcs(y, xx, k, z)]
        return remote(here, here, zs.at[step, xx, o - 1], zr.at[step, xx, o - 1], (d, zpeer(o)))

    def z_recv(step, xx, o):
        here = W.at[slot_of(step), pcs(y, xx, k, zfrom(o))]
        return remote(here, here, zs.at[step, xx, o - 1], zr.at[step, xx, o - 1], (d, zpeer(o)))

    def y_copy(step, xx, yy):
        here = W.at[slot_of(step), blk(yy, xx, k)]
        return remote(here, here, ys.at[step, xx], yr.at[step, xx], (yn, z))

    def d_copy(slot, yy, xx, kk):
        here = W.at[slot, blk(yy, xx, kk)]
        return remote(here, here, ds.at[slot, yy * 2 + xx], dr.at[slot, yy * 2 + xx], (sib, z))

    def x_copy(yy, xx):
        here = W.at[6, blk(yy, xx, k)]
        return remote(here, here, xs.at[yy * 2 + xx], xr.at[yy * 2 + xx], (par, z))

    def has(step):
        return (step < 5) | is_cls

    def do_z(step):
        @pl.when(has(step))
        def _():
            p_recv(step).wait_recv()
            for xx in range(2):
                for o in (2, 1, 3):
                    z_send(step, xx, o).start()

    def spread(step, yy, xx):
        d_copy(slot_of(step), yy, xx, k).start()

        @pl.when(is_box & (step == 4))
        def _():
            x_copy(yy, xx).start()

    def do_y(step):
        @pl.when(has(step))
        def _():
            for xx in range(2):
                for o in (1, 2, 3):
                    z_recv(step, xx, o).wait_recv()
                y_copy(step, xx, y).start()
                spread(step, y, xx)

    def do_d(step):
        @pl.when(has(step))
        def _():
            for xx in range(2):
                y_copy(step, xx, 1 - y).wait_recv()
                spread(step, 1 - y, xx)

    def gathered(slot):
        for b in range(4):
            d_copy(slot, b // 2, b % 2, 1 - k).wait_recv()

    for step in range(layers):
        TB[step] = tow[step, 1 - x].astype(low)
        p_send(step).start()
        W[step, pcs(y, x, k, z)] = tow[step, x].astype(low)
    pltpu_feature = remote(feat, FP, fs.at[0], fr.at[0], (par, z))
    pltpu_feature.start()
    tail = cls_out + box_out - 2 * CUT
    HB[2] = jnp.zeros((piece, 8, CUT), low)
    for cut, width in ((2, tail), (0, CUT), (1, CUT)):
        part = hed[:, cut * CUT : cut * CUT + width].astype(low)
        HB[cut, :, :, 0:width] = part.reshape(piece, 8, width)

    @pl.when(is_cls)
    def _():
        p_head(2, 4).start()
        W[4, pcs(y, x, k, z)] = HB[0]
        W[5, pcs(y, x, k, z)] = HB[1]

    @pl.when(is_box)
    def _():
        p_head(0, 4).start()
        p_head(1, 5).start()
        W[6, pcs(y, x, k, z)] = HB[2]

    code_copy = remote(CP.at[x], CP.at[x], fs.at[1], fr.at[1], (par, z))
    goal_copy = remote(GP.at[x], GP.at[x], fs.at[2], fr.at[2], (par, z))
    do_z(0)
    do_z(1)

    def n_copy(index, dst, dev):
        return remote(CNT.at[index], CNT.at[dst], ns.at[dst], nr.at[dst], dev)

    r_at = lax.broadcasted_iota(jnp.int32, (rows, cols), 0)
    inside = jnp.zeros((rows, cols), jnp.int32)
    for r in range(rows):
        row = z * rows + r
        here = crops[0, row]
        above = crops[0, jnp.maximum(row - 1, 0)]
        below = crops[0, jnp.minimum(row + 1, 4 * rows - 1)]
        ok = jnp.where((here == above) & (here == below), 1, 0)
        inside = jnp.where(r_at == r, ok, inside)
    CP[x] = jnp.zeros((rows, 16, cols), full)
    picked = jnp.zeros((rows, cols), full)
    for a in range(anchors):
        label = marked[a]
        valid = (label >= 0) & (inside > 0)
        chosen = valid & (lit[a] > 0)
        mark = jnp.where(chosen, label - 200, jnp.where(valid, -100, 0)).astype(full)
        picked = picked + jnp.where(chosen, 1.0, 0.0)
        for r in range(rows):
            CP[x, r, a : a + 1, :] = mark[r : r + 1, :]
    CNT[0] = jnp.broadcast_to(jnp.sum(picked), (8, LANES))
    n_copy(0, 4, (sib, z)).start()

    col = lax.broadcasted_iota(jnp.int32, (cols, CUT), 0)
    first_col = col == 0
    last_col = col == cols - 1

    def move_right(v):
        return jnp.where(first_col, 0.0, pltpu.roll(v, 1, 0))

    def move_left(v):
        return jnp.where(last_col, 0.0, pltpu.roll(v, cols - 1, 0))

    def put_row(layer, cv, row, value):
        at = pl.ds(pl.multiple_of(row * cols, cols), cols)
        A3[layer, cv, at, 0:CUT] = move_right(value).astype(low)
        A3[layer, cv, at, CUT : 2 * CUT] = value.astype(low)
        A3[layer, cv, at, 2 * CUT : 3 * CUT] = move_left(value).astype(low)

    def up_ok():
        return z > 0

    def down_ok():
        return z < 3

    def a_edge(layer, side, cv):
        row = rows if side == 0 else 1
        src = A3.at[layer, cv, pl.ds(row * cols, cols), pl.ds(CUT, CUT)]
        dev = (d, lax.rem(z + 1, 4)) if side == 0 else (d, lax.rem(z + 3, 4))
        return remote(src, HA.at[layer, side, cv], hs.at[layer, side, cv], hr.at[layer, side, cv], dev)

    def send_edges(layer, cv):
        @pl.when(down_ok())
        def _():
            a_edge(layer, 0, cv).start()

        @pl.when(up_ok())
        def _():
            a_edge(layer, 1, cv).start()

    def take_edges(layer, cv):
        @pl.when(up_ok())
        def _():
            a_edge(layer, 0, cv).wait_recv()
            put_row(layer, cv, 0, HA[layer, 0, cv].astype(full))

        @pl.when(down_ok())
        def _():
            a_edge(layer, 1, cv).wait_recv()
            put_row(layer, cv, rows + 1, HA[layer, 1, cv].astype(full))

    def rim_first(body, carry, send):
        carry = lax.fori_loop(0, 2, lambda i, c: body(i * (rows - 1), c), carry)
        send()
        return lax.fori_loop(1, rows - 1, body, carry)

    def g_edge(slot, side, cv):
        src = G.at[slot, cv, pl.ds((rows if side == 0 else 1) * cols, cols)]
        dst = G.at[slot, cv, pl.ds(0 if side == 0 else (rows + 1) * cols, cols)]
        dev = (d, lax.rem(z + 1, 4)) if side == 0 else (d, lax.rem(z + 3, 4))
        return remote(src, dst, gs.at[slot, side, cv], gr.at[slot, side, cv], dev)

    def g_recv(slot, side, cv):
        dst = G.at[slot, cv, pl.ds(0 if side == 0 else (rows + 1) * cols, cols)]
        return remote(dst, dst, gs.at[slot, side, cv], gr.at[slot, side, cv], (d, lax.rem(z + 1, 4)))

    def send_g(slot, cv):
        @pl.when(down_ok())
        def _():
            g_edge(slot, 0, cv).start()

        @pl.when(up_ok())
        def _():
            g_edge(slot, 1, cv).start()

    def take_g(slot, cv):
        @pl.when(up_ok())
        def _():
            g_recv(slot, 0, cv).wait_recv()

        @pl.when(down_ok())
        def _():
            g_recv(slot, 1, cv).wait_recv()

    def fill(layer_src, cv):
        def body(r, carry):
            put_row(0, cv, r + 1, layer_src[pl.ds(pl.multiple_of(r * cols, cols), cols), :].astype(full))
            return carry

        lax.fori_loop(0, rows, body, 0)

    fill(feat, x)
    send_edges(0, x)

    def clear(at, layer_count, slot_count):
        def a_body(layer, carry):
            for cv in range(2):
                A3[layer, cv, at, :] = jnp.zeros((cols, 3 * CUT), low)
            return carry

        def g_body(slot, carry):
            for cv in range(2):
                G[slot, cv, at, :] = jnp.zeros((cols, CUT), low)
            return carry

        lax.fori_loop(0, layer_count, a_body, 0)
        lax.fori_loop(0, slot_count, g_body, 0)

    @pl.when(z == 0)
    def _():
        clear(pl.ds(0, cols), layers + 1, layers + 3)

    @pl.when(z == 3)
    def _():
        clear(pl.ds((rows + 1) * cols, cols), layers + 1, layers + 3)

    BG[...] = jnp.zeros((8, CUT), full)
    GP[x] = jnp.zeros((rows, 40, cols), full)

    def goal_rows(q, carry):
        for r in range(rows):
            GP[x, r, pl.ds(q, 1), :] = goals[q, r : r + 1, :]
        return carry

    lax.fori_loop(0, box_out, goal_rows, 0)
    for q in range(2 * layers + 2):
        bias[q : q + 1, :] = bias_all[q * CUT : (q + 1) * CUT].reshape(1, CUT)
    q = 2 * layers + 2
    bias[q : q + 1, :] = jnp.zeros((1, CUT), full)
    bias[q : q + 1, 0:tail] = bias_all[q * CUT : q * CUT + tail].reshape(1, tail)

    n_copy(0, 4, (sib, z)).wait_recv()
    CNT[1] = CNT[0] + CNT[4]
    n_copy(1, 5, (yn, z)).start()
    do_y(0)
    do_z(2)
    n_copy(1, 5, (yn, z)).wait_recv()
    CNT[2] = CNT[1] + CNT[5]
    n_copy(2, 6, (par, z)).start()
    pltpu_feature.wait_recv()
    fill(FP, 1 - x)
    send_edges(0, 1 - x)
    n_copy(2, 6, (par, z)).wait_recv()
    CNT[3] = CNT[2] + CNT[6]
    for o in (1, 2, 3):
        n_copy(3, 6 + o, (d, zpeer(o))).start()
    do_y(1)
    do_d(0)
    do_z(3)
    code_copy.start()

    @pl.when(is_cls)
    def _():
        goal_copy.start()

    def conv(layer, slot, cv):
        total = None
        for dy in range(3):
            term = jnp.dot(
                A3[layer, cv, pl.ds(dy * cols, px), :],
                W[slot, pl.ds(dy * 96, 96)].reshape(3 * CUT, CUT),
                preferred_element_type=full,
            )
            total = term if total is None else total + term
        return total

    def forward(layer, carry):
        gathered(layer)
        shift = bias[pl.ds(2 * layer + x, 1), :]

        def canvas(cv, carry):
            take_edges(layer, cv)
            Z[layer, cv] = conv(layer, layer, cv)

            def row(r, carry):
                at = pl.ds(pl.multiple_of(r * cols, cols), cols)
                value = Z[layer, cv, at, :] + shift
                Z[layer, cv, at, :] = value
                put_row(layer + 1, cv, r + 1, silu_value(value))
                return carry

            rim_first(row, 0, lambda: send_edges(layer + 1, cv))
            return carry

        lax.fori_loop(0, 2, canvas, 0)
        do_y_when = layer + 2
        do_y(do_y_when)
        do_d(layer + 1)

        @pl.when(layer < 2)
        def _():
            do_z(layer + 4)

        return carry

    lax.fori_loop(0, layers, forward, 0)
    do_d(5)
    for o in (1, 2, 3):
        n_copy(3, 6 + o, (d, zpeer(o))).wait_recv()
    count = CNT[3] + CNT[7] + CNT[8] + CNT[9]
    grad_scale = (1.0 / jnp.maximum(count, 1.0))[0:1, 0:1]
    for cv in range(2):
        take_edges(layers, cv)

    def rd_send(slot, b):
        src = D.at[slot, blk(b // 2, b % 2, 1 - k)]
        return remote(src, RD.at[slot, b], rds.at[slot, b], rdr.at[slot, b], (sib, z))

    def ry_send(slot, xx):
        src = D.at[slot, blk(1 - y, xx, k)]
        return remote(src, RY.at[slot, xx], rys.at[slot, xx], ryr.at[slot, xx], (yn, z))

    def rz_send(slot, xx, o):
        src = D.at[slot, pcs(y, xx, k, zpeer(o))]
        return remote(
            src, RZ.at[slot, xx, o - 1], rzs.at[slot, xx, o - 1], rzr.at[slot, xx, o - 1], (d, zpeer(o))
        )

    def rx_send(b):
        src = D.at[6, blk(b // 2, b % 2, k)]
        return remote(src, RX.at[b], rxs.at[b], rxr.at[b], (par, z))

    def add_into(slot, place, terms):
        units = block // 3

        def body(i, carry):
            here = pl.ds(place + i * units, units)
            there = pl.ds(i * units, units)
            total = D[slot, here].astype(full)
            for ref in terms:
                total = total + ref[there].astype(full)
            D[slot, here] = total.astype(low)
            return carry

        lax.fori_loop(0, 3, body, 0)

    def start_of(yy, xx, kk):
        return ((yy * 2 + xx) * 2 + kk) * block

    def do_rd(slot):
        for b in range(4):
            rd_send(slot, b).start()

    def do_ry(slot, relay=False):
        for xx in range(2):
            b = (1 - y) * 2 + xx
            rd_send(slot, b).wait_recv()
            terms = [RD.at[slot, b]]
            if relay:
                rx_send(b).wait_recv()
                terms.append(RX.at[b])
            add_into(slot, start_of(1 - y, xx, k), terms)
            ry_send(slot, xx).start()

    def do_rx():
        for b in range(4):
            rd_send(6, b).wait_recv()
            add_into(6, start_of(b // 2, b % 2, k), [RD.at[6, b]])
            rx_send(b).start()

    def do_rz(slot, relay=False):
        for xx in range(2):
            b = y * 2 + xx
            rd_send(slot, b).wait_recv()
            terms = [RD.at[slot, b]]
            if relay:
                rx_send(b).wait_recv()
                terms.append(RX.at[b])
            ry_send(slot, xx).wait_recv()
            terms.append(RY.at[slot, xx])
            add_into(slot, start_of(y, xx, k), terms)
            for o in (2, 1, 3):
                rz_send(slot, xx, o).start()

    def piece_sum(slot, xx):
        total = D[slot, pcs(y, xx, k, z)].astype(full)
        for o in (1, 2, 3):
            rz_send(slot, xx, o).wait_recv()
            total = total + RZ[slot, xx, o - 1].astype(full)
        return total

    def rp_send(slot, dst):
        return remote(RP.at[slot], dst, rps.at[slot], rpr.at[slot], (par, z))

    def do_rp(slot, dst_own, dst_other):
        RP[slot] = piece_sum(slot, 1 - x)
        rp_send(slot, dst_other).start()
        dst_own[...] = piece_sum(slot, x)

    def do_rp_layer(layer):
        do_rp(layer, tgrad.at[layer, x], tgrad.at[layer, x])

    def do_rp_head(slot):
        do_rp(slot, hgrad.at[slot - 4], hgrad.at[slot - 4])

    def weight_grad(layer, slot):
        for dy in range(3):
            total = None
            for cv in range(2):
                term = lax.dot_general(
                    A3[layer, cv, pl.ds(dy * cols, px), :],
                    G[slot, cv, pl.ds(cols, px), :],
                    (((0,), (0,)), ((), ())),
                    preferred_element_type=full,
                )
                total = term if total is None else total + term
            D[slot, pl.ds(dy * 96, 96)] = total.astype(low).reshape(96, 8, CUT)

    def input_grad(slot, add):
        def canvas(cv, carry):
            take_g(slot, cv)
            for dx in range(3):
                total = None
                for dy in range(3):
                    term = lax.dot_general(
                        G[slot, cv, pl.ds((2 - dy) * cols, px), :],
                        W[slot, pl.ds((3 * dy + dx) * 32, 32)].reshape(CUT, CUT),
                        (((1,), (1,)), ((), ())),
                        preferred_element_type=full,
                    )
                    total = term if total is None else total + term
                if add:
                    U[dx, cv] = U[dx, cv] + total
                else:
                    U[dx, cv] = total
            return carry

        lax.fori_loop(0, 2, canvas, 0)

    def upstream_row(cv, r):
        at = pl.ds(pl.multiple_of(r * cols, cols), cols)
        return U[1, cv, at, :] + move_left(U[0, cv, at, :]) + move_right(U[2, cv, at, :])

    def fold(value):
        return jnp.sum(value.reshape(cols // 8, 8, CUT), axis=0)

    lane = lax.broadcasted_iota(jnp.int32, (1, CUT), 1)
    lane_tab = lax.broadcasted_iota(jnp.int32, (16, CUT), 1)
    anchor_tab = lax.broadcasted_iota(jnp.int32, (16, CUT), 0)

    def spread_marks(cv, r, table):
        return lax.dot_general(
            CP[cv, r].astype(low), table, (((0,), (0,)), ((), ())), preferred_element_type=full
        )

    box_from = cls_out - 2 * CUT

    def cls_rows(cut, cv, shift):
        channel = lane_tab + cut * CUT
        spread_tab = (
            (channel >= anchor_tab * classes) & (channel < (anchor_tab + 1) * classes) & (channel < cls_out)
        ).astype(full).astype(low)
        here = lane + cut * CUT
        number = here
        for a in range(1, anchors):
            number = number - jnp.where(here >= a * classes, classes, 0)
        number = number.astype(full) - 200.0

        def row(r, carry):
            b_sum, l_sum = carry
            at = pl.ds(pl.multiple_of(r * cols, cols), cols)
            raw = ACC[at, :] + shift
            LS[cut, cv, at, :] = raw.astype(low)
            marks = spread_marks(cv, r, spread_tab)
            hit = marks == number
            seen = marks < -50.0
            s = jnp.where(hit, -raw, raw)
            e = jnp.exp(-jnp.abs(s))
            inv = 1.0 / (1.0 + e)
            other = e * inv
            q = jnp.where(s >= 0.0, inv, other)
            p = jnp.where(s >= 0.0, other, inv)
            soft = jnp.maximum(s, 0.0) + jnp.log1p(e)
            t = jnp.where(seen, jnp.where(hit, focal_alpha, 1.0 - focal_alpha), 0.0) * q * q
            slope = t * (2.0 * p * soft + q) * grad_scale
            g = jnp.where(hit, -slope, slope).astype(low)
            G[4 + cut, cv, pl.ds(pl.multiple_of((r + 1) * cols, cols), cols), :] = g
            return b_sum + fold(g.astype(full)), l_sum + fold(t * soft)

        return row

    def box_rows(cut, cv, shift):
        spot = lane_tab - box_from
        spread_tab = (
            (spot >= anchor_tab * 4) & (spot < (anchor_tab + 1) * 4) & (anchor_tab < anchors)
        ).astype(full).astype(low)
        goal_lane = lax.broadcasted_iota(jnp.int32, (40, LANES), 1) - (box_from - LANES)
        goal_tab = (goal_lane == lax.broadcasted_iota(jnp.int32, (40, LANES), 0)).astype(full)

        def row(r, carry):
            b_sum, l_sum = carry
            at = pl.ds(pl.multiple_of(r * cols, cols), cols)
            raw = ACC[at, :] + shift
            ES[cv, at, :] = raw.astype(low)
            marks = spread_marks(cv, r, spread_tab)
            chosen = marks < -110.0
            want = lax.dot_general(
                GP[cv, r], goal_tab, (((0,), (0,)), ((), ())),
                precision=lax.Precision.HIGHEST, preferred_element_type=full,
            )
            want = jnp.concatenate([jnp.zeros((cols, LANES), full), want], axis=1)
            diff = raw - want
            size = jnp.abs(diff)
            value = jnp.where(
                size < smooth_beta, 0.5 * diff * diff / smooth_beta, size - 0.5 * smooth_beta
            )
            slope = jnp.where(
                size < smooth_beta, diff / smooth_beta, jnp.where(diff > 0.0, 1.0, -1.0)
            )
            g = jnp.where(chosen, slope * grad_scale, 0.0).astype(low)
            G[4 + cut, cv, pl.ds(pl.multiple_of((r + 1) * cols, cols), cols), :] = g
            return b_sum + fold(g.astype(full)), l_sum + fold(jnp.where(chosen, value, 0.0))

        return row

    nothing = jnp.zeros((8, CUT), full)

    def l_copy(cut):
        return remote(LS.at[cut, 1 - x], logits.at[cut], ls.at[cut], lr.at[cut], (par, z))

    def e_copy():
        return remote(ES.at[1 - x], deltas, es.at[0], er.at[0], (par, z))

    U[...] = jnp.zeros(U.shape, full)
    remote(CP.at[1 - x], CP.at[1 - x], fs.at[1], fr.at[1], (par, z)).wait_recv()

    @pl.when(is_box)
    def _():
        remote(GP.at[1 - x], GP.at[1 - x], fs.at[2], fr.at[2], (par, z)).wait_recv()

    def head(cut, carry):
        slot = 4 + cut

        @pl.when(is_cls & (cut == 2))
        def _():
            for b in range(4):
                x_copy(b // 2, b % 2).wait_recv()
                d_copy(6, b // 2, b % 2, k).start()

        gathered(slot)
        shift = bias[pl.ds(2 * layers + cut, 1), :]

        def canvas(cv, carry):
            b_sum, l_sum = carry
            ACC[...] = conv(layers, slot, cv)
            return lax.cond(
                is_cls,
                lambda: rim_first(cls_rows(cut, cv, shift), (b_sum, l_sum), lambda: send_g(slot, cv)),
                lambda: rim_first(box_rows(cut, cv, shift), (b_sum, l_sum), lambda: send_g(slot, cv)),
            )

        b_sum, l_sum = lax.fori_loop(0, 2, canvas, (nothing, nothing))

        @pl.when(is_cls)
        def _():
            l_copy(cut).start()

        @pl.when(is_box)
        def _():
            e_copy().start()

        BG[pl.ds(slot, 1), :] = jnp.sum(b_sum, axis=0, keepdims=True)
        BG[pl.ds(7, 1), :] = BG[pl.ds(7, 1), :] + jnp.sum(l_sum, axis=0, keepdims=True)
        weight_grad(layers, slot)
        do_rd(slot)

        input_grad(slot, True)

        @pl.when(cut < 2)
        def _():
            do_ry(slot)

        @pl.when(cut == 1)
        def _():
            do_rz(4)

        @pl.when(is_cls & (cut == 2))
        def _():
            do_rx()
            do_rz(5)
            do_rp_head(4)

        return carry

    lax.fori_loop(2 * x, 3, head, 0)

    @pl.when(is_cls)
    def _():
        for cut in range(3):
            logits[cut] = LS[cut, 0]

    @pl.when(is_box)
    def _():
        deltas[...] = ES[1]

    def feature_rows(cv, dst):
        def row(r, carry):
            dst[pl.ds(pl.multiple_of(r * cols, cols), cols), :] = upstream_row(cv, r).astype(dst.dtype)
            return carry

        lax.fori_loop(0, rows, row, 0)

    f_copy = remote(FS, FR, fs.at[3], fr.at[3], (par, z))
    def b_copy(src, dst, dev):
        return remote(src, BR.at[dst], bs.at[dst], br.at[dst], dev)

    def backward(j, carry):
        layer = layers - 1 - j

        def canvas(cv, b_sum):
            def row(r, b_sum):
                at = pl.ds(pl.multiple_of(r * cols, cols), cols)
                g = (upstream_row(cv, r) * silu_slope(Z[layer, cv, at, :])).astype(low)
                G[layer, cv, pl.ds(pl.multiple_of((r + 1) * cols, cols), cols), :] = g
                return b_sum + fold(g.astype(full))

            return rim_first(row, b_sum, lambda: send_g(layer, cv))

        b_sum = lax.fori_loop(0, 2, canvas, nothing)
        BG[pl.ds(layer, 1), :] = jnp.sum(b_sum, axis=0, keepdims=True)
        weight_grad(layer, layer)
        do_rd(layer)

        @pl.when(j == 3)
        def _():
            b_copy(BG, 0, (sib, z)).start()

        @pl.when(j == layers - 1)
        def _():
            do_ry(0)

        input_grad(layer, False)

        @pl.when(j == layers - 1)
        def _():
            feature_rows(1 - x, FS)
            f_copy.start()

        @pl.when(j < layers - 1)
        def _():
            do_ry(layer)

        @pl.when(is_cls & (j == 0))
        def _():
            do_rp_head(5)

        @pl.when(j > 0)
        def _():
            do_rz(layer + 1)

        @pl.when(j > 1)
        def _():
            do_rp_layer(layer + 2)

        return carry

    lax.fori_loop(0, layers, backward, 0)

    @pl.when(is_box)
    def _():
        do_ry(6, relay=True)

    b_copy(BG, 0, (sib, z)).wait_recv()
    BR[6] = BG[...] + BR[0]
    b_copy(BR.at[6], 1, (yn, z)).start()
    feature_rows(x, fgrad)
    b_copy(BR.at[6], 1, (yn, z)).wait_recv()
    total = BR[6] + BR[1]
    for zz in range(4):
        @pl.when(z == zz)
        def _():
            BR[7 + zz] = total
            for o in (1, 2, 3):
                remote(
                    BR.at[7 + zz], BR.at[7 + zz], bs.at[1 + o], br.at[1 + o], (d, zpeer(o))
                ).start()
    do_rz(0)
    do_rp_layer(1)

    @pl.when(is_box)
    def _():
        do_rz(6, relay=True)

    for o in (1, 2, 3):
        for zz in range(4):
            @pl.when(zfrom(o) == zz)
            def _():
                remote(
                    BR.at[7 + zz], BR.at[7 + zz], bs.at[1 + o], br.at[1 + o], (d, zpeer(o))
                ).wait_recv()
    total = (BR[7] + BR[8]) + (BR[9] + BR[10])
    BR[5] = total
    last = remote(BR.at[5], bsum.at[x], bs.at[5], br.at[5], (par, z))
    last.start()
    bsum[x] = total
    f_copy.wait_recv()
    fgrad[...] = fgrad[...] + FR[...].astype(full)
    do_rp_layer(0)

    @pl.when(is_box)
    def _():
        do_rp_head(6)

    remote(BR.at[5], bsum.at[1 - x], bs.at[5], br.at[5], (par, z)).wait_recv()
    loss = jnp.sum(bsum[0, 7:8, :] + bsum[1, 7:8, :], axis=1, keepdims=True)
    loss_out[...] = jnp.broadcast_to(loss, (8, LANES)) / jnp.maximum(count, 1.0)

    for layer in range(layers):
        rp_send(layer, tgrad.at[layer, 1 - x]).wait_recv()

    @pl.when(is_cls)
    def _():
        rp_send(6, hgrad.at[2]).wait_recv()
        e_copy().wait_recv()
        for b in range(4):
            rx_send(b).wait_send()
            d_copy(6, b // 2, b % 2, k).wait_send()
        for cut in range(3):
            l_copy(cut).wait_send()
        p_head(2, 4).wait_send()
        goal_copy.wait_send()

    @pl.when(is_box)
    def _():
        for cut in range(2):
            rp_send(4 + cut, hgrad.at[cut]).wait_recv()
        for cut in range(3):
            l_copy(cut).wait_recv()
        for b in range(4):
            x_copy(b // 2, b % 2).wait_send()
            d_copy(6, b // 2, b % 2, k).wait_send()
        e_copy().wait_send()
        p_head(0, 4).wait_send()
        p_head(1, 5).wait_send()

    def close_gather(step, carry):
        for xx in range(2):
            for o in (1, 2, 3):
                z_send(step, xx, o).wait_send()
            y_copy(step, xx, y).wait_send()
        return carry

    lax.fori_loop(0, 6 - x, close_gather, 0)

    def close_slot(slot, carry):
        @pl.when((slot < 4) | is_cls)
        def _():
            for b in range(4):
                d_copy(slot, b // 2, b % 2, k).wait_send()

        return carry

    lax.fori_loop(0, 6 - 2 * x, close_slot, 0)

    def close_layer(layer, carry):
        @pl.when(layer < layers)
        def _():
            p_send(jnp.minimum(layer, layers - 1)).wait_send()

        @pl.when(down_ok())
        def _():
            for cv in range(2):
                a_edge(layer, 0, cv).wait_send()

        @pl.when(up_ok())
        def _():
            for cv in range(2):
                a_edge(layer, 1, cv).wait_send()

        return carry

    lax.fori_loop(0, layers + 1, close_layer, 0)

    def close_grad(slot, carry):
        @pl.when(is_cls | (slot < 4) | (slot == 6))
        def _():
            for b in range(4):
                rd_send(slot, b).wait_send()

            @pl.when(down_ok())
            def _():
                for cv in range(2):
                    g_edge(slot, 0, cv).wait_send()

            @pl.when(up_ok())
            def _():
                for cv in range(2):
                    g_edge(slot, 1, cv).wait_send()

        @pl.when((slot < 4) | (is_cls & (slot < 6)) | (is_box & (slot == 6)))
        def _():
            for xx in range(2):
                ry_send(slot, xx).wait_send()
                for o in (1, 2, 3):
                    rz_send(slot, xx, o).wait_send()
            rp_send(slot, RP.at[slot]).wait_send()

        return carry

    lax.fori_loop(0, layers + 3, close_grad, 0)
    pltpu_feature.wait_send()
    code_copy.wait_send()
    f_copy.wait_send()
    n_copy(0, 4, (sib, z)).wait_send()
    n_copy(1, 5, (yn, z)).wait_send()
    n_copy(2, 6, (par, z)).wait_send()
    b_copy(BG, 0, (sib, z)).wait_send()
    b_copy(BR.at[6], 1, (yn, z)).wait_send()
    for o in (1, 2, 3):
        n_copy(3, 6 + o, (d, zpeer(o))).wait_send()
        remote(BR.at[7], BR.at[7], bs.at[1 + o], br.at[1 + o], (d, zpeer(o))).wait_send()
    last.wait_send()


def finish_kernel(
    step, lg, dl, fg, tg, hg, bsum, loss_in, tw, hw, tm, tv, hm, hv, bw, bm, bv,
    o_lg, o_dl, o_fg, o_tg, o_bg, o_hg, o_tn, o_hn, o_tm, o_tv, o_hm, o_hv, o_tc, o_hc,
    o_loss, o_gb, o_gx, o_wb, o_mb, o_vb,
    TG, TW, TM, TV, TC, HG, HGO, HW, HM, HV, HC, LG, LO, DT, DS, FG,
    t_in, t_out, h_in, h_out, m_sem,
    *, layers, rows, cols, cls_out, box_out,
):
    tail = cls_out - 2 * CUT
    last = tail + box_out

    def t_loads(layer):
        pairs = ((tg, TG), (tw, TW), (tm, TM), (tv, TV))
        return [
            pltpu.make_async_copy(a.at[layer], b.at[layer], t_in.at[layer, i])
            for i, (a, b) in enumerate(pairs)
        ]

    def t_stores(layer):
        pairs = (
            (TG.at[layer, 0], o_tg.at[layer]),
            (TG.at[layer, 1], o_bg.at[layer]),
            (TW.at[layer], o_tn.at[layer]),
            (TM.at[layer], o_tm.at[layer]),
            (TV.at[layer], o_tv.at[layer]),
            (TC.at[layer], o_tc.at[layer]),
        )
        return [pltpu.make_async_copy(a, b, t_out.at[layer, i]) for i, (a, b) in enumerate(pairs)]

    h_loads = [
        pltpu.make_async_copy(a, b, h_in.at[i])
        for i, (a, b) in enumerate(((hg, HG), (hw, HW), (hm, HM), (hv, HV)))
    ]
    h_stores = [
        pltpu.make_async_copy(a, b, h_out.at[i])
        for i, (a, b) in enumerate(((HGO, o_hg), (HW, o_hn), (HM, o_hm), (HV, o_hv), (HC, o_hc)))
    ]
    lg_load = pltpu.make_async_copy(lg, LG, m_sem.at[0])
    lg_store = pltpu.make_async_copy(LO, o_lg, m_sem.at[1])
    fg_load = pltpu.make_async_copy(fg, FG, m_sem.at[2])
    fg_store = pltpu.make_async_copy(FG, o_fg, m_sem.at[3])
    for layer in range(layers):
        for copy in t_loads(layer):
            copy.start()
    for copy in h_loads:
        copy.start()
    fg_load.start()
    lg_load.start()

    steps = jnp.broadcast_to(step[0].astype(full), (8, CUT))
    keep_one = (1.0 - jnp.exp(steps * math.log(beta_one)))[0:1, :]
    keep_two = (1.0 - jnp.exp(steps * math.log(beta_two)))[0:1, :]

    def adam(weight, grad, first, second, decay):
        one, two = keep_one[:, : grad.shape[1]], keep_two[:, : grad.shape[1]]
        first_new = beta_one * first + (1.0 - beta_one) * grad
        second_new = beta_two * second + (1.0 - beta_two) * grad * grad
        first_hat = first_new / one
        second_hat = second_new / two
        weight_new = weight - learn_rate * (
            first_hat / (jnp.sqrt(second_hat) + adam_eps) + decay * weight
        )
        return weight_new, first_new, second_new

    fg_load.wait()
    fg_store.start()

    o_loss[0] = loss_in[0, 0]
    for q in range(2 * layers + 3):
        if q < 2 * layers:
            grad, width = bsum[q % 2, q // 2 : q // 2 + 1, :], CUT
        elif q < 2 * layers + 2:
            grad, width = bsum[0, q - layers : q - layers + 1, :], CUT
        else:
            lane = lax.broadcasted_iota(jnp.int32, (1, CUT), 1)
            boxes = bsum[1, 6:7, :]
            grad, width = jnp.where(lane < tail, bsum[0, 6:7, :], boxes)[:, :last], last
            o_gx[...] = pltpu.roll(boxes, CUT - tail, 1)[:, :box_out].reshape(box_out)
        at = pl.ds(q * CUT, width)
        w_new, m_new, v_new = adam(
            bw[at].reshape(1, width), grad, bm[at].reshape(1, width), bv[at].reshape(1, width), 0.0
        )
        o_wb[at] = w_new.reshape(width)
        o_mb[at] = m_new.reshape(width)
        o_vb[at] = v_new.reshape(width)
        most = min(width, cls_out + 2 * layers * CUT - q * CUT)
        o_gb[pl.ds(q * CUT, most)] = grad[:, :most].reshape(most)
    pick_lane = lax.broadcasted_iota(jnp.int32, (40, LANES), 1) - (tail - LANES)
    pick = (pick_lane == lax.broadcasted_iota(jnp.int32, (40, LANES), 0)).astype(full).astype(low)
    for r in range(rows):
        DT[r] = lax.dot_general(
            pick, dl[r * cols : (r + 1) * cols, LANES:], (((1,), (1,)), ((), ())), preferred_element_type=full
        )

    def turn(q, carry):
        for r in range(rows):
            DS[q, r : r + 1, :] = DT[r, pl.ds(q, 1), :]
        return carry

    lax.fori_loop(0, box_out, turn, 0)
    o_dl[...] = DS[...].astype(low)

    for layer in range(layers):
        for copy in t_loads(layer):
            copy.wait()
        for t in range(2):
            w_new, m_new, v_new = adam(
                TW[layer, t], TG[layer, t], TM[layer, t], TV[layer, t], decay_rate
            )
            TW[layer, t] = w_new
            TM[layer, t] = m_new
            TV[layer, t] = v_new
            TC[layer, t] = w_new.astype(low)
        for copy in t_stores(layer):
            copy.start()
    lg_load.wait()
    for cut, width in ((0, CUT), (1, CUT), (2, tail)):
        LO[:, cut * CUT : cut * CUT + width] = LG[cut][:, :width]
    lg_store.start()
    for copy in h_loads:
        copy.wait()
    for cut, width in ((0, CUT), (1, CUT), (2, last)):
        at = slice(cut * CUT, cut * CUT + width)
        grad = HG[cut][:, :width]
        HGO[:, at] = grad
        w_new, m_new, v_new = adam(HW[:, at], grad, HM[:, at], HV[:, at], decay_rate)
        HW[:, at] = w_new
        HM[:, at] = m_new
        HV[:, at] = v_new
        HC[:, at] = w_new.astype(low)
    for copy in h_stores:
        copy.start()
    for layer in range(layers):
        for copy in t_stores(layer):
            copy.wait()
    for copy in h_stores:
        copy.wait()
    lg_store.wait()
    fg_store.wait()


def fused_shards(
    features,
    crop_ids,
    labels,
    positive,
    box_targets,
    tower_weights,
    head_weights,
    biases,
    tower_m,
    tower_v,
    head_m,
    head_v,
    bias_m,
    bias_v,
    step_count,
):
    canvases, rows, cols, channels = features.shape
    layers = tower_weights.shape[0]
    shard_rows = tower_weights.shape[2]
    anchors = labels.shape[-1]
    head_out = head_weights.shape[1]
    box_out = 4 * anchors
    cls_out = head_out - box_out
    px = rows * cols
    piece = shard_rows // 8
    tow = tower_weights.reshape(layers, 2, piece, 8, channels)
    by_anchor = (0, 3, 1, 2)
    marked = jnp.transpose(labels, by_anchor)[0]
    lit = jnp.transpose(positive, by_anchor)[0]
    goals = jnp.transpose(box_targets, by_anchor)[0]
    units = 32 * piece
    block = 4 * piece
    dma = pltpu.SemaphoreType.DMA
    vm = pl.BlockSpec(memory_space=pltpu.VMEM)
    shape = jax.ShapeDtypeStruct
    logits, deltas, fgrad, tgrad, hgrad, bsum, loss = pl.pallas_call(
        partial(
            mega_kernel,
            rows=rows, cols=cols, layers=layers, cls_out=cls_out, box_out=box_out, anchors=anchors, piece=piece,
        ),
        out_shape=(
            shape((3, px, CUT), low),
            shape((px, CUT), low),
            shape((px, CUT), full),
            shape((layers, 2, piece, 8, CUT), full),
            shape((3, piece, 8, CUT), full),
            shape((2, 8, CUT), full),
            shape((8, LANES), full),
        ),
        in_specs=[vm, pl.BlockSpec(memory_space=pltpu.SMEM)] + [vm] * 6,
        out_specs=[vm] * 7,
        scratch_shapes=[
            pltpu.VMEM((7, units, 8, CUT), low),
            pltpu.VMEM((7, units, 8, CUT), low),
            pltpu.VMEM((7, 4, block, 8, CUT), low),
            pltpu.VMEM((7, 2, block, 8, CUT), low),
            pltpu.VMEM((7, 2, 3, piece, 8, CUT), low),
            pltpu.VMEM((4, block, 8, CUT), low),
            pltpu.VMEM((7, piece, 8, CUT), full),
            pltpu.VMEM((layers + 1, 2, px + 2 * cols, 3 * CUT), low),
            pltpu.VMEM((layers + 1, 2, 2, cols, CUT), low),
            pltpu.VMEM((7, 2, px + 2 * cols, CUT), low),
            pltpu.VMEM((layers, 2, px, CUT), full),
            pltpu.VMEM((3, 2, px, CUT), full),
            pltpu.VMEM((px, CUT), full),
            pltpu.VMEM((px, CUT), low),
            pltpu.VMEM((2, rows, 16, cols), full),
            pltpu.VMEM((2, rows, 40, cols), full),
            pltpu.VMEM((3, 2, px, CUT), low),
            pltpu.VMEM((2, px, CUT), low),
            pltpu.VMEM((px, CUT), low),
            pltpu.VMEM((px, CUT), low),
            pltpu.VMEM((10, 8, LANES), full),
            pltpu.VMEM((8, CUT), full),
            pltpu.VMEM((11, 8, CUT), full),
            pltpu.VMEM((layers, piece, 8, CUT), low),
            pltpu.VMEM((3, piece, 8, CUT), low),
            pltpu.VMEM((16, CUT), full),
            dma((6,)), dma((6,)),
            dma((6, 2, 3)), dma((6, 2, 3)),
            dma((6, 2)), dma((6, 2)),
            dma((7, 4)), dma((7, 4)),
            dma((4,)), dma((4,)),
            dma((4,)), dma((4,)),
            dma((layers + 1, 2, 2)), dma((layers + 1, 2, 2)),
            dma((7, 2, 2)), dma((7, 2, 2)),
            dma((3,)), dma((3,)),
            dma((1,)), dma((1,)),
            dma((7, 4)), dma((7, 4)),
            dma((7, 2)), dma((7, 2)),
            dma((7, 2, 3)), dma((7, 2, 3)),
            dma((4,)), dma((4,)),
            dma((7,)), dma((7,)),
            dma((10,)), dma((10,)),
            dma((6,)), dma((6,)),
        ],
        compiler_params=pltpu.CompilerParams(
            vmem_limit_bytes=60 * 1024 * 1024, collective_id=0, has_side_effects=True
        ),
    )(features.reshape(px, channels), crop_ids, marked, lit, goals, tow, head_weights, biases)

    tower_shape = tower_weights.shape
    head_shape = head_weights.shape
    anys = pl.BlockSpec(memory_space=pl.ANY)
    smem = pl.BlockSpec(memory_space=pltpu.SMEM)
    biases_out = biases.shape[0]
    (
        o_lg, o_dl, o_fg, o_tg, o_bg, o_hg, o_tn, o_hn, o_tm, o_tv, o_hm, o_hv, o_tc, o_hc,
        o_loss, o_gb, o_gx, o_wb, o_mb, o_vb,
    ) = pl.pallas_call(
        partial(
            finish_kernel, layers=layers, rows=rows, cols=cols, cls_out=cls_out, box_out=box_out
        ),
        out_shape=(
            shape((px, cls_out), low),
            shape((box_out, rows, cols), low),
            shape((px, channels), full),
            shape((layers, shard_rows, channels), full),
            shape((layers, shard_rows, channels), full),
            shape(head_shape, full),
            shape(tower_shape, full),
            shape(head_shape, full),
            shape(tower_shape, full),
            shape(tower_shape, full),
            shape(head_shape, full),
            shape(head_shape, full),
            shape(tower_shape, low),
            shape(head_shape, low),
            shape((1,), full),
            shape((biases_out - box_out,), full),
            shape((box_out,), full),
            shape((biases_out,), full),
            shape((biases_out,), full),
            shape((biases_out,), full),
        ),
        in_specs=[smem, anys, vm, anys, anys, anys, vm, vm] + [anys] * 6 + [vm] * 3,
        out_specs=[anys, vm] + [anys] * 12 + [smem] + [vm] * 5,
        scratch_shapes=[
            pltpu.VMEM(tower_shape, full),
            pltpu.VMEM(tower_shape, full),
            pltpu.VMEM(tower_shape, full),
            pltpu.VMEM(tower_shape, full),
            pltpu.VMEM(tower_shape, low),
            pltpu.VMEM((3, shard_rows, CUT), full),
            pltpu.VMEM(head_shape, full),
            pltpu.VMEM(head_shape, full),
            pltpu.VMEM(head_shape, full),
            pltpu.VMEM(head_shape, full),
            pltpu.VMEM(head_shape, low),
            pltpu.VMEM((3, px, CUT), low),
            pltpu.VMEM((px, cls_out), low),
            pltpu.VMEM((rows, 40, cols), full),
            pltpu.VMEM((box_out, rows, cols), full),
            pltpu.VMEM((px, channels), full),
            dma((layers, 4)), dma((layers, 6)), dma((4,)), dma((5,)), dma((4,)),
        ],
        compiler_params=pltpu.CompilerParams(vmem_limit_bytes=60 * 1024 * 1024),
    )(
        step_count, logits, deltas, fgrad, tgrad.reshape(tower_shape), hgrad.reshape(3, shard_rows, CUT), bsum, loss,
        tower_weights, head_weights, tower_m, tower_v, head_m, head_v, biases, bias_m, bias_v,
    )
    field = (canvases, rows, cols, -1)
    return (
        o_lg.reshape(field),
        jnp.transpose(o_dl[None], (0, 2, 3, 1)),
        o_loss.reshape(()),
        o_fg.reshape(field),
        o_tg,
        o_bg,
        o_hg,
        o_gb,
        o_gx,
        o_tn,
        o_hn,
        o_wb,
        o_tm,
        o_tv,
        o_hm,
        o_hv,
        o_mb,
        o_vb,
        o_tc,
        o_hc,
    )


def solution(mesh):
    placed = (
        P("dp", "tower", None, None),
        P("dp", None),
        P("dp", "tower", None, None),
        P("dp", "tower", None, None),
        P("dp", "tower", None, None),
        P(None, None, ("dp", "tower"), None),
        P(("dp", "tower"), None),
        P(),
        P(None, None, ("dp", "tower"), None),
        P(None, None, ("dp", "tower"), None),
        P(("dp", "tower"), None),
        P(("dp", "tower"), None),
        P(),
        P(),
        P(),
    )
    fused = mesh.shape["dp"] == 8 and mesh.shape["tower"] == 4
    return jax.shard_map(
        fused_shards if fused else plain_shards,
        mesh=mesh,
        in_specs=placed,
        out_specs=(
            P("dp", "tower", None, None),
            P("dp", "tower", None, None),
            P(),
            P("dp", "tower", None, None),
            P(None, ("dp", "tower"), None),
            P(None, ("dp", "tower"), None),
            P(("dp", "tower"), None),
            P(),
            P(),
            P(None, None, ("dp", "tower"), None),
            P(("dp", "tower"), None),
            P(),
            P(None, None, ("dp", "tower"), None),
            P(None, None, ("dp", "tower"), None),
            P(("dp", "tower"), None),
            P(("dp", "tower"), None),
            P(),
            P(),
            P(None, None, ("dp", "tower"), None),
            P(("dp", "tower"), None),
        ),
        check_vma=False,
    )
```

```python
import math
from functools import partial

import jax
import jax.numpy as jnp
from jax import lax
from jax.experimental import pallas as pl
from jax.experimental.pallas import tpu as pltpu
from jax.sharding import PartitionSpec as P

beta_one = 0.9
beta_two = 0.999
adam_eps = 1e-08
learn_rate = 0.03
decay_rate = 0.05
focal_alpha = 0.25
smooth_beta = 1.0 / 9.0


def with_halo(shard, sides, width):
    for axis, dim in sides:
        size, length = (lax.axis_size(axis), shard.shape[dim])
        up = [(i, (i + 1) % size) for i in range(size - 1)]
        down = [(j, i) for i, j in up]
        last = lax.slice_in_dim(shard, length - width, length, axis=dim)
        initial = lax.slice_in_dim(shard, 0, width, axis=dim)
        before = lax.ppermute(last, axis, up)
        after = lax.ppermute(initial, axis, down)
        shard = jnp.concatenate([before, shard, after], axis=dim)
    return shard


def act_rim(values):
    return with_halo(values, (("tower", 2),), 1)


def grad_rim(values):
    return with_halo(values, (("tower", 2),), 1)


def pad_cols(values):
    return jnp.pad(values, ((0, 0), (0, 0), (0, 0), (1, 1), (0, 0)))


def silu_value(values):
    return values * jax.nn.sigmoid(values)


def silu_slope(values):
    sig = jax.nn.sigmoid(values)
    return sig * (1.0 + values * (1.0 - sig))


def conv_forward(padded, weight, out_rows, out_cols):
    stacks, canvases, channels = (padded.shape[0], padded.shape[1], padded.shape[-1])
    summed = None
    for row_off in range(3):
        for col_off in range(3):
            tap_index = row_off * 3 + col_off
            window = padded[
                :, :, row_off : row_off + out_rows, col_off : col_off + out_cols, :
            ].reshape(stacks, -1, channels)
            contrib = jnp.einsum(
                "snk,skm->snm",
                window,
                weight[:, tap_index * channels : (tap_index + 1) * channels, :],
                preferred_element_type=jnp.float32,
            )
            summed = contrib if summed is None else summed + contrib
    return summed.reshape(stacks, canvases, out_rows, out_cols, weight.shape[-1])


def conv_input_grad(grad_pad, weight, out_rows, out_cols):
    stacks, canvases, outputs = (grad_pad.shape[0], grad_pad.shape[1], grad_pad.shape[-1])
    channels = weight.shape[1] // 9
    summed = None
    for row_off in range(3):
        for col_off in range(3):
            tap_index = row_off * 3 + col_off
            window = grad_pad[
                :, :, 2 - row_off : 2 - row_off + out_rows, 2 - col_off : 2 - col_off + out_cols, :
            ].reshape(stacks, -1, outputs)
            contrib = jnp.einsum(
                "snm,skm->snk",
                window,
                weight[:, tap_index * channels : (tap_index + 1) * channels, :],
                preferred_element_type=jnp.float32,
            )
            summed = contrib if summed is None else summed + contrib
    return summed.reshape(stacks, canvases, out_rows, out_cols, channels)


def conv_weight_grad(padded, grads):
    stacks, channels = (padded.shape[0], padded.shape[-1])
    out_rows, out_cols = (grads.shape[2], grads.shape[3])
    flat_grads = grads.reshape(stacks, -1, grads.shape[-1])
    pieces = []
    for row_off in range(3):
        for col_off in range(3):
            window = padded[
                :, :, row_off : row_off + out_rows, col_off : col_off + out_cols, :
            ].reshape(stacks, -1, channels)
            pieces.append(
                jnp.einsum("snk,snm->skm", window, flat_grads, preferred_element_type=jnp.float32)
            )
    return jnp.concatenate(pieces, 1)


def adam_update(weight, grad, first, second, step_float, decay):
    first_new = beta_one * first + (1.0 - beta_one) * grad
    second_new = beta_two * second + (1.0 - beta_two) * grad * grad
    first_hat = first_new / (1.0 - jnp.power(beta_one, step_float))
    second_hat = second_new / (1.0 - jnp.power(beta_two, step_float))
    weight_new = weight - learn_rate * (
        first_hat / (jnp.sqrt(second_hat) + adam_eps) + decay * weight
    )
    return (weight_new, first_new, second_new)


def anchor_masks(label_rows, positive_rows, row_flags, classes):
    valid = (label_rows >= 0) & row_flags[:, :, None, None]
    chosen = valid & (positive_rows > 0)
    targets = (
        (label_rows[..., None] == jnp.arange(classes, dtype=jnp.int32)) & chosen[..., None]
    ).astype(jnp.float32)
    return (valid.astype(jnp.float32), chosen.astype(jnp.float32), targets)


def focal_terms(cls_vals, targets, valid_f):
    logit_view = cls_vals.reshape(targets.shape)
    prob = jax.nn.sigmoid(logit_view)
    cross = jax.nn.softplus(logit_view) - targets * logit_view
    prob_true = prob * targets + (1.0 - prob) * (1.0 - targets)
    alpha_weight = focal_alpha * targets + (1.0 - focal_alpha) * (1.0 - targets)
    return jnp.sum(alpha_weight * (1.0 - prob_true) ** 2 * cross * valid_f[..., None])


def smooth_terms(box_vals, goals, chosen_f):
    diff = box_vals.reshape(chosen_f.shape + (4,)) - goals.reshape(chosen_f.shape + (4,))
    abs_diff = jnp.abs(diff)
    smooth = jnp.where(
        abs_diff < smooth_beta, 0.5 * diff * diff / smooth_beta, abs_diff - 0.5 * smooth_beta
    )
    return jnp.sum(smooth * chosen_f[..., None])


def plain_shards(
    features,
    crop_ids,
    labels,
    positive,
    box_targets,
    tower_weights,
    head_weights,
    biases,
    tower_m,
    tower_v,
    head_m,
    head_v,
    bias_m,
    bias_v,
    step_count,
):
    canvases, row_count, col_count, channels = features.shape
    layers = tower_weights.shape[0]
    anchors = labels.shape[-1]
    head_out = head_weights.shape[1]
    box_out = 4 * anchors
    cls_out = head_out - box_out
    classes = cls_out // anchors
    shard = lax.axis_index("tower")
    tower_low, head_stack = (
        lax.all_gather(tower_weights.astype(jnp.bfloat16), ("dp", "tower"), axis=2, tiled=True),
        lax.all_gather(
            head_weights.astype(jnp.bfloat16)[None, None], ("dp", "tower"), axis=2, tiled=True
        ),
    )
    head_low = head_stack[0, 0]
    tower_bias = biases[: 2 * layers * channels].reshape(layers, 2, channels)
    head_bias = biases[2 * layers * channels :]
    cls_weight = head_low[:, :cls_out][None]
    box_weight = head_low[:, cls_out:][None]
    same_rows = crop_ids[:, 1:] == crop_ids[:, :-1]
    edge_true = jnp.ones((crop_ids.shape[0], 1), dtype=jnp.bool_)
    row_ok = jnp.concatenate([edge_true, same_rows], 1) & jnp.concatenate([same_rows, edge_true], 1)
    own_ok = lax.dynamic_slice_in_dim(row_ok, shard * row_count, row_count, 1)
    own_valid, own_chosen, own_targets = anchor_masks(labels, positive, own_ok, classes)
    count_all = lax.psum(jnp.sum(own_chosen), ("dp", "tower"))
    denom = jnp.maximum(count_all, 1.0)
    grad_scale = 1.0 / denom
    kept = []
    preact = []
    current = features[None]
    for layer in range(layers):
        padded = pad_cols(act_rim(current))
        if layer == 0:
            padded = jnp.broadcast_to(padded, (2,) + padded.shape[1:])
        kept.append(padded)
        summed = (
            conv_forward(padded, tower_low[layer], row_count, col_count)
            + tower_bias[layer][:, None, None, None, :]
        )
        preact.append(summed)
        current = silu_value(summed).astype(jnp.bfloat16)
    head_in = pad_cols(act_rim(current))
    kept.append(head_in)
    cls_raw = conv_forward(head_in[0:1], cls_weight, row_count, col_count)[0] + head_bias[:cls_out]
    box_raw = conv_forward(head_in[1:2], box_weight, row_count, col_count)[0] + head_bias[cls_out:]
    focal_value, focal_back = jax.vjp(
        partial(focal_terms, targets=own_targets, valid_f=own_valid), cls_raw
    )
    smooth_value, smooth_back = jax.vjp(
        partial(smooth_terms, goals=box_targets, chosen_f=own_chosen), box_raw
    )
    loss_local = focal_value + smooth_value
    cls_low = focal_back(grad_scale)[0].astype(jnp.bfloat16)
    box_low = smooth_back(grad_scale)[0].astype(jnp.bfloat16)
    head_wgrad = jnp.concatenate(
        [
            conv_weight_grad(head_in[0:1], cls_low[None])[0],
            conv_weight_grad(head_in[1:2], box_low[None])[0],
        ],
        1,
    )
    head_bgrad = jnp.concatenate(
        [
            jnp.sum(cls_low, axis=(0, 1, 2), dtype=jnp.float32),
            jnp.sum(box_low, axis=(0, 1, 2), dtype=jnp.float32),
        ]
    )
    joined = pad_cols(grad_rim(jnp.concatenate([cls_low, box_low], -1)[None]))
    upstream = jnp.concatenate(
        [
            conv_input_grad(joined[..., :cls_out], cls_weight, row_count, col_count),
            conv_input_grad(joined[..., cls_out:], box_weight, row_count, col_count),
        ],
        0,
    )
    tower_grads = [None] * layers
    bias_grads = [None] * layers
    for layer in reversed(range(layers)):
        grad_low = (upstream * silu_slope(preact[layer])).astype(jnp.bfloat16)
        bias_grads[layer] = jnp.sum(grad_low, axis=(1, 2, 3), dtype=jnp.float32)
        tower_grads[layer] = conv_weight_grad(kept[layer], grad_low)
        padded_grad = pad_cols(grad_rim(grad_low))
        upstream = conv_input_grad(padded_grad, tower_low[layer], row_count, col_count)
    feature_grad = upstream[0] + upstream[1]
    tower_shard, head_pair = (
        lax.psum_scatter(
            jnp.stack(tower_grads, 0), ("dp", "tower"), scatter_dimension=2, tiled=True
        ),
        lax.psum_scatter(head_wgrad[None, None], ("dp", "tower"), scatter_dimension=2, tiled=True),
    )
    head_shard = head_pair[0, 0]
    bias_local = jnp.concatenate([jnp.stack(bias_grads, 0).reshape(-1), head_bgrad])
    logits_out = cls_raw.astype(jnp.bfloat16)
    deltas_out = box_raw.astype(jnp.bfloat16)
    bias_grad, loss_total = lax.psum((bias_local, loss_local), ("dp", "tower"))
    loss = loss_total / denom
    step_float = step_count[0].astype(jnp.float32)
    tower_new, tower_m_new, tower_v_new = adam_update(
        tower_weights, tower_shard, tower_m, tower_v, step_float, decay_rate
    )
    head_new, head_m_new, head_v_new = adam_update(
        head_weights, head_shard, head_m, head_v, step_float, decay_rate
    )
    bias_new, bias_m_new, bias_v_new = adam_update(
        biases, bias_grad, bias_m, bias_v, step_float, 0.0
    )
    split_at = bias_grad.shape[0] - box_out
    return (
        logits_out,
        deltas_out,
        loss,
        feature_grad,
        tower_shard[:, 0],
        tower_shard[:, 1],
        head_shard,
        bias_grad[:split_at],
        bias_grad[split_at:],
        tower_new,
        head_new,
        bias_new,
        tower_m_new,
        tower_v_new,
        head_m_new,
        head_v_new,
        bias_m_new,
        bias_v_new,
        tower_new.astype(jnp.bfloat16),
        head_new.astype(jnp.bfloat16),
    )


MESH = pl.DeviceIdType.MESH
low = jnp.bfloat16
full = jnp.float32
LANES = 128
CUT = 256


def mega_kernel(
    feat, crops, marked, lit, goals, tow, hed, bias_all,
    logits, deltas, fgrad, tgrad, hgrad, bsum, loss_out,
    W, D, RD, RY, RZ, RX, RP, A3, HA, G, Z, U, ACC, FP, CP, GP, LS, CNT, BG, BR, TB, HB, bias, MK,
    ps, pr, zs, zr, ys, yr, ds, dr, xs, xr, fs, fr, hs, hr, gs, gr, ls, lr, es, er,
    rds, rdr, rys, ryr, rzs, rzr, rxs, rxr, rps, rpr, ns, nr, bs, br,
    *, rows, cols, layers, cls_out, box_out, anchors, piece,
):
    d = lax.axis_index("dp")
    z = lax.axis_index("tower")
    k = lax.rem(d, 2)
    x = lax.rem(d // 2, 2)
    y = d // 4
    sib = d + 1 - 2 * k
    par = d + 2 - 4 * x
    yn = d + 4 - 8 * y
    is_cls = x == 0
    is_box = x == 1
    block = 4 * piece
    px = rows * cols
    classes = cls_out // anchors

    def remote(src, dst, send, recv, dev):
        return pltpu.make_async_remote_copy(
            src_ref=src, dst_ref=dst, send_sem=send, recv_sem=recv, device_id=dev, device_id_type=MESH
        )

    def blk(yy, xx, kk):
        return pl.ds(((yy * 2 + xx) * 2 + kk) * block, block)

    def pcs(yy, xx, kk, zz):
        return pl.ds(((yy * 2 + xx) * 2 + kk) * block + zz * piece, piece)

    def zpeer(o):
        return lax.rem(z + o, 4)

    def zfrom(o):
        return lax.rem(z + 4 - o, 4)

    barrier = pltpu.get_barrier_semaphore()
    peers = [(sib, z), (par, z), (yn, z), (par, zpeer(1)), (par, zpeer(3))]
    for dev in peers + [(d, zpeer(o)) for o in (1, 2, 3)]:
        pl.semaphore_signal(barrier, inc=1, device_id=dev, device_id_type=MESH)
    pl.semaphore_wait(barrier, 8)

    def f_edge(side, across):
        src = feat.at[pl.ds((rows - 1) * cols if side == 0 else 0, cols)]
        dev = (par if across else d, zpeer(1) if side == 0 else zpeer(3))
        return remote(src, HA.at[0, side, x], hs.at[0, side, across], hr.at[0, side, across], dev)

    def f_edge_in(side, across):
        dst = HA.at[0, side, 1 - x if across else x]
        return remote(dst, dst, hs.at[0, side, across], hr.at[0, side, across], (par, zpeer(1)))

    @pl.when(z < 3)
    def _():
        for across in range(2):
            f_edge(0, across).start()

    @pl.when(z > 0)
    def _():
        for across in range(2):
            f_edge(1, across).start()

    def slot_of(step):
        odd = jnp.where(step == 1, 6, jnp.where(step == 3, 5, 3))
        return jnp.where(is_cls, step, jnp.where(lax.rem(step, 2) == 0, step // 2, odd))

    def p_send(layer):
        theirs = jnp.where(is_cls, jnp.minimum(2 * layer, 5), layer)
        return remote(
            TB.at[layer], W.at[layer, pcs(y, x, k, z)], ps.at[layer], pr.at[theirs], (par, z)
        )

    def p_head(cut, index, theirs):
        return remote(
            HB.at[cut], W.at[4 + cut, pcs(y, x, k, z)], ps.at[index], pr.at[theirs], (par, z)
        )

    def p_recv(step):
        slot = slot_of(step)
        there = W.at[slot, pcs(y, 1 - x, k, z)]
        return remote(there, there, ps.at[step], pr.at[step], (par, z))

    def z_send(step, xx, o):
        here = W.at[slot_of(step), pcs(y, xx, k, z)]
        return remote(here, here, zs.at[step, xx, o - 1], zr.at[step, xx, o - 1], (d, zpeer(o)))

    def z_recv(step, xx, o):
        here = W.at[slot_of(step), pcs(y, xx, k, zfrom(o))]
        return remote(here, here, zs.at[step, xx, o - 1], zr.at[step, xx, o - 1], (d, zpeer(o)))

    def y_copy(step, xx, yy):
        here = W.at[slot_of(step), blk(yy, xx, k)]
        return remote(here, here, ys.at[step, xx], yr.at[step, xx], (yn, z))

    def d_copy(slot, yy, xx, kk):
        here = W.at[slot, blk(yy, xx, kk)]
        return remote(here, here, ds.at[slot, yy * 2 + xx], dr.at[slot, yy * 2 + xx], (sib, z))

    def x_copy(slot, yy, xx):
        here = W.at[slot, blk(yy, xx, k)]
        return remote(here, here, xs.at[slot - 5, yy * 2 + xx], xr.at[slot - 5, yy * 2 + xx], (par, z))

    def has(step):
        return (step < 5) | (is_box & (step < 6))

    def do_z(step):
        @pl.when(has(step))
        def _():
            p_recv(step).wait_recv()
            for xx in range(2):
                for o in (2, 1, 3):
                    z_send(step, xx, o).start()

    def spread(step, yy, xx):
        slot = slot_of(step)

        @pl.when(slot >= 5)
        def _():
            x_copy(slot, yy, xx).start()

        @pl.when(slot != 5)
        def _():
            d_copy(slot, yy, xx, k).start()

    def do_y(step, lead=False):
        @pl.when(has(step))
        def _():
            for xx in range(2):
                for o in (1, 2, 3):
                    z_recv(step, xx, o).wait_recv()
                if lead:
                    if xx == 0:
                        p_recv(step + 1).wait_recv()
                    for o in (2, 1, 3):
                        z_send(step + 1, xx, o).start()
                y_copy(step, xx, y).start()
                spread(step, y, xx)

    def do_d(step):
        @pl.when(has(step))
        def _():
            for xx in range(2):
                y_copy(step, xx, 1 - y).wait_recv()
                spread(step, 1 - y, xx)

    def pump(step, carry=0):
        do_y(step)
        do_d(step - 1)

        @pl.when(step < 5)
        def _():
            do_z(step + 1)

        return carry

    def handed_over(slot):
        for b in range(4):
            x_copy(slot, b // 2, b % 2).wait_recv()
            d_copy(slot, b // 2, b % 2, k).start()

    def gathered(slot):
        for b in range(4):
            d_copy(slot, b // 2, b % 2, 1 - k).wait_recv()

    pltpu_feature = remote(feat, FP, fs.at[0], fr.at[0], (par, z))
    for step in range(layers):
        TB[step] = tow[step, 1 - x].astype(low)
        p_send(step).start()
        if step == 0:
            pltpu_feature.start()
        W[step, pcs(y, x, k, z)] = tow[step, x].astype(low)
    tail = cls_out + box_out - 2 * CUT
    HB[2] = jnp.zeros((piece, 8, CUT), low)
    for cut, width in ((2, tail), (0, CUT), (1, CUT)):
        part = hed[:, cut * CUT : cut * CUT + width].astype(low)
        HB[cut, :, :, 0:width] = part.reshape(piece, 8, width)

    @pl.when(is_cls)
    def _():
        p_head(2, 4, 1).start()
        p_head(1, 5, 3).start()
        W[4, pcs(y, x, k, z)] = HB[0]

    @pl.when(is_box)
    def _():
        p_head(0, 4, 4).start()
        W[5, pcs(y, x, k, z)] = HB[1]
        W[6, pcs(y, x, k, z)] = HB[2]

    code_copy = remote(CP.at[x], CP.at[x], fs.at[1], fr.at[1], (par, z))
    goal_copy = remote(GP.at[x], GP.at[x], fs.at[2], fr.at[2], (par, z))
    do_z(0)

    def n_copy(index, dst, dev):
        return remote(CNT.at[index], CNT.at[dst], ns.at[dst], nr.at[dst], dev)

    col = lax.broadcasted_iota(jnp.int32, (cols, CUT), 0)
    first_col = col == 0
    last_col = col == cols - 1

    def move_right(v):
        return jnp.where(first_col, 0.0, pltpu.roll(v, 1, 0))

    def move_left(v):
        return jnp.where(last_col, 0.0, pltpu.roll(v, cols - 1, 0))

    def put_row(layer, cv, row, value):
        at = pl.ds(pl.multiple_of(row * cols, cols), cols)
        A3[layer, cv, at, 0:CUT] = move_right(value).astype(low)
        A3[layer, cv, at, CUT : 2 * CUT] = value.astype(low)
        A3[layer, cv, at, 2 * CUT : 3 * CUT] = move_left(value).astype(low)

    def up_ok():
        return z > 0

    def down_ok():
        return z < 3

    def a_edge(layer, side, cv):
        row = rows if side == 0 else 1
        src = A3.at[layer, cv, pl.ds(row * cols, cols), pl.ds(CUT, CUT)]
        dev = (d, lax.rem(z + 1, 4)) if side == 0 else (d, lax.rem(z + 3, 4))
        return remote(src, HA.at[layer, side, cv], hs.at[layer, side, cv], hr.at[layer, side, cv], dev)

    def send_edges(layer, cv):
        @pl.when(down_ok())
        def _():
            a_edge(layer, 0, cv).start()

        @pl.when(up_ok())
        def _():
            a_edge(layer, 1, cv).start()

    def first_edges():
        for side, there in ((0, z > 0), (1, z < 3)):
            @pl.when(there)
            def _():
                for across in range(2):
                    f_edge_in(side, across).wait_recv()
                    cv = 1 - x if across else x
                    put_row(0, cv, 0 if side == 0 else rows + 1, HA[0, side, cv].astype(full))

    def take_edges(layer, cv):
        @pl.when(up_ok())
        def _():
            a_edge(layer, 0, cv).wait_recv()
            put_row(layer, cv, 0, HA[layer, 0, cv].astype(full))

        @pl.when(down_ok())
        def _():
            a_edge(layer, 1, cv).wait_recv()
            put_row(layer, cv, rows + 1, HA[layer, 1, cv].astype(full))

    def rim_first(body, carry, send):
        carry = lax.fori_loop(0, 2, lambda i, c: body(i * (rows - 1), c), carry)
        send()
        return lax.fori_loop(1, rows - 1, body, carry)

    def g_edge(slot, side, cv):
        src = G.at[slot, cv, pl.ds((rows if side == 0 else 1) * cols, cols)]
        dst = G.at[slot, cv, pl.ds(0 if side == 0 else (rows + 1) * cols, cols)]
        dev = (d, lax.rem(z + 1, 4)) if side == 0 else (d, lax.rem(z + 3, 4))
        return remote(src, dst, gs.at[slot, side, cv], gr.at[slot, side, cv], dev)

    def g_recv(slot, side, cv):
        dst = G.at[slot, cv, pl.ds(0 if side == 0 else (rows + 1) * cols, cols)]
        return remote(dst, dst, gs.at[slot, side, cv], gr.at[slot, side, cv], (d, lax.rem(z + 1, 4)))

    def send_g(slot, cv):
        @pl.when(down_ok())
        def _():
            g_edge(slot, 0, cv).start()

        @pl.when(up_ok())
        def _():
            g_edge(slot, 1, cv).start()

    def take_g(slot, cv):
        @pl.when(up_ok())
        def _():
            g_recv(slot, 0, cv).wait_recv()

        @pl.when(down_ok())
        def _():
            g_recv(slot, 1, cv).wait_recv()

    def fill(layer_src, cv):
        def body(r, carry):
            put_row(0, cv, r + 1, layer_src[pl.ds(pl.multiple_of(r * cols, cols), cols), :].astype(full))
            return carry

        lax.fori_loop(0, rows, body, 0)

    fill(feat, x)
    do_y(0, lead=True)

    r_at = lax.broadcasted_iota(jnp.int32, (rows, cols), 0)
    inside = jnp.zeros((rows, cols), jnp.int32)
    for r in range(rows):
        row = z * rows + r
        here = crops[0, row]
        above = crops[0, jnp.maximum(row - 1, 0)]
        below = crops[0, jnp.minimum(row + 1, 4 * rows - 1)]
        ok = jnp.where((here == above) & (here == below), 1, 0)
        inside = jnp.where(r_at == r, ok, inside)
    CP[x] = jnp.zeros((rows, 16, cols), full)
    picked = jnp.zeros((rows, cols), full)
    for a in range(anchors):
        label = marked[a]
        valid = (label >= 0) & (inside > 0)
        chosen = valid & (lit[a] > 0)
        mark = jnp.where(chosen, label - 200, jnp.where(valid, -100, 0)).astype(full)
        picked = picked + jnp.where(chosen, 1.0, 0.0)
        for r in range(rows):
            CP[x, r, a : a + 1, :] = mark[r : r + 1, :]
    CNT[0] = jnp.broadcast_to(jnp.sum(picked), (8, LANES))
    n_copy(0, 4, (sib, z)).start()

    code_copy.start()
    pltpu_feature.wait_recv()
    fill(FP, 1 - x)
    first_edges()
    pump(1)

    def clear(at, layer_count, slot_count):
        def a_body(layer, carry):
            for cv in range(2):
                A3[layer, cv, at, :] = jnp.zeros((cols, 3 * CUT), low)
            return carry

        def g_body(slot, carry):
            for cv in range(2):
                G[slot, cv, at, :] = jnp.zeros((cols, CUT), low)
            return carry

        lax.fori_loop(0, layer_count, a_body, 0)
        lax.fori_loop(0, slot_count, g_body, 0)

    @pl.when(z == 0)
    def _():
        clear(pl.ds(0, cols), layers + 1, layers + 3)

    @pl.when(z == 3)
    def _():
        clear(pl.ds((rows + 1) * cols, cols), layers + 1, layers + 3)

    BG[...] = jnp.zeros((8, CUT), full)
    GP[x] = jnp.zeros((rows, 40, cols), full)

    def goal_rows(q, carry):
        for r in range(rows):
            GP[x, r, pl.ds(q, 1), :] = goals[q, r : r + 1, :]
        return carry

    lax.fori_loop(0, box_out, goal_rows, 0)
    for q in range(2 * layers + 2):
        bias[q : q + 1, :] = bias_all[q * CUT : (q + 1) * CUT].reshape(1, CUT)
    q = 2 * layers + 2
    bias[q : q + 1, :] = jnp.zeros((1, CUT), full)
    bias[q : q + 1, 0:tail] = bias_all[q * CUT : q * CUT + tail].reshape(1, tail)

    U[...] = jnp.zeros(U.shape, full)

    @pl.when(is_cls)
    def _():
        goal_copy.start()

    n_copy(0, 4, (sib, z)).wait_recv()
    CNT[1] = CNT[0] + CNT[4]
    n_copy(1, 5, (yn, z)).start()

    lane_tab = lax.broadcasted_iota(jnp.int32, (16, CUT), 1)
    anchor_tab = lax.broadcasted_iota(jnp.int32, (16, CUT), 0)

    def write_marks():
        remote(CP.at[1 - x], CP.at[1 - x], fs.at[1], fr.at[1], (par, z)).wait_recv()
        spot = lane_tab - (cls_out - 2 * CUT)
        box_tab = jnp.where(
            (spot >= anchor_tab * 4) & (spot < (anchor_tab + 1) * 4) & (anchor_tab < anchors), 1.0, 0.0
        )
        tables = []
        for cut in range(3):
            channel = lane_tab + cut * CUT
            table = jnp.where(
                (channel >= anchor_tab * classes) & (channel < (anchor_tab + 1) * classes) & (channel < cls_out),
                1.0,
                0.0,
            )
            if cut == 2:
                side = x.astype(full)
                table = table * (1.0 - side) + box_tab * side
            tables.append(table.astype(low))

        def row(r, carry):
            at = pl.ds(pl.multiple_of(r * cols, cols), cols)
            for cv in range(2):
                codes = CP[cv, r].astype(low)
                for cut in range(3):
                    MK[cut, cv, at, :] = lax.dot_general(
                        codes, tables[cut], (((0,), (0,)), ((), ())), preferred_element_type=full
                    ).astype(low)
            return carry

        lax.fori_loop(0, rows, row, 0)

    def conv(layer, slot, cv):
        total = None
        for dy in range(3):
            term = jnp.dot(
                A3[layer, cv, pl.ds(dy * cols, px), :],
                W[slot, pl.ds(dy * 96, 96)].reshape(3 * CUT, CUT),
                preferred_element_type=full,
            )
            total = term if total is None else total + term
        return total

    def forward(layer, carry):
        gathered(layer)
        shift = bias[pl.ds(2 * layer + x, 1), :]

        def canvas(cv, carry):
            @pl.when(layer > 0)
            def _():
                take_edges(layer, cv)

            Z[layer, cv] = conv(layer, layer, cv)

            def row(r, carry):
                at = pl.ds(pl.multiple_of(r * cols, cols), cols)
                value = Z[layer, cv, at, :] + shift
                Z[layer, cv, at, :] = value
                put_row(layer + 1, cv, r + 1, silu_value(value))
                return carry

            rim_first(row, 0, lambda: send_edges(layer + 1, cv))
            return carry

        lax.fori_loop(0, 2, canvas, 0)
        first = jnp.where(is_cls, layer + 2, 2 * layer + 2)
        after = jnp.where(is_cls, jnp.minimum(layer + 3, 5), jnp.minimum(2 * layer + 4, 7))
        lax.fori_loop(first, after, pump, 0)

        @pl.when(layer == 0)
        def _():
            n_copy(1, 5, (yn, z)).wait_recv()
            CNT[2] = CNT[1] + CNT[5]
            n_copy(2, 6, (par, z)).start()

        @pl.when(layer == 1)
        def _():
            write_marks()
            n_copy(2, 6, (par, z)).wait_recv()
            CNT[3] = CNT[2] + CNT[6]
            for o in (1, 2, 3):
                n_copy(3, 6 + o, (d, zpeer(o))).start()

        return carry

    lax.fori_loop(0, layers, forward, 0)
    for o in (1, 2, 3):
        n_copy(3, 6 + o, (d, zpeer(o))).wait_recv()
    count = CNT[3] + CNT[7] + CNT[8] + CNT[9]
    grad_scale = (1.0 / jnp.maximum(count, 1.0))[0:1, 0:1]

    @pl.when(is_cls)
    def _():
        handed_over(6)

    for cv in range(2):
        take_edges(layers, cv)

    def rd_send(slot, b):
        src = D.at[slot, blk(b // 2, b % 2, 1 - k)]
        return remote(src, RD.at[slot, b], rds.at[slot, b], rdr.at[slot, b], (sib, z))

    def ry_send(slot, xx):
        src = D.at[slot, blk(1 - y, xx, k)]
        return remote(src, RY.at[slot, xx], rys.at[slot, xx], ryr.at[slot, xx], (yn, z))

    def rz_send(slot, xx, o):
        src = D.at[slot, pcs(y, xx, k, zpeer(o))]
        return remote(
            src, RZ.at[slot, xx, o - 1], rzs.at[slot, xx, o - 1], rzr.at[slot, xx, o - 1], (d, zpeer(o))
        )

    def rx_send(slot, b):
        src = D.at[slot, blk(b // 2, b % 2, k)]
        return remote(src, RX.at[b], rxs.at[b], rxr.at[b], (par, z))

    def add_into(slot, place, terms, own=True):
        units = block // 3

        def body(i, carry):
            here = pl.ds(place + i * units, units)
            there = pl.ds(i * units, units)
            total = D[slot, here].astype(full) if own else None
            for ref in terms:
                term = ref[there].astype(full)
                total = term if total is None else total + term
            D[slot, here] = total.astype(low)
            return carry

        lax.fori_loop(0, 3, body, 0)

    def start_of(yy, xx, kk):
        return ((yy * 2 + xx) * 2 + kk) * block

    def do_rd(slot):
        for b in range(4):
            rd_send(slot, b).start()

    def here_terms(slot, b, own, relay):
        terms = []
        if own:
            rd_send(slot, b).wait_recv()
            terms.append(RD.at[slot, b])
        if relay:
            rx_send(slot, b).wait_recv()
            terms.append(RX.at[b])
        return terms

    def do_ry(slot, own=True, relay=False, halves=(0, 1)):
        for xx in halves:
            terms = here_terms(slot, (1 - y) * 2 + xx, own, relay)
            add_into(slot, start_of(1 - y, xx, k), terms, own)
            ry_send(slot, xx).start()

    def do_rx(slot):
        for b in range(4):
            rd_send(slot, b).wait_recv()
            add_into(slot, start_of(b // 2, b % 2, k), [RD.at[slot, b]])
            rx_send(slot, b).start()

    def do_rz(slot, own=True, relay=False):
        for xx in range(2):
            terms = here_terms(slot, y * 2 + xx, own, relay)
            ry_send(slot, xx).wait_recv()
            terms.append(RY.at[slot, xx])
            add_into(slot, start_of(y, xx, k), terms, own)
            for o in (2, 1, 3):
                rz_send(slot, xx, o).start()

    def piece_sum(slot, xx):
        total = D[slot, pcs(y, xx, k, z)].astype(full)
        for o in (1, 2, 3):
            rz_send(slot, xx, o).wait_recv()
            total = total + RZ[slot, xx, o - 1].astype(full)
        return total

    def rp_send(slot, dst):
        return remote(RP.at[slot], dst, rps.at[slot], rpr.at[slot], (par, z))

    def do_rp(slot, dst_own, dst_other):
        RP[slot] = piece_sum(slot, 1 - x)
        rp_send(slot, dst_other).start()
        dst_own[...] = piece_sum(slot, x)

    def do_rp_layer(layer):
        do_rp(layer, tgrad.at[layer, x], tgrad.at[layer, x])

    def do_rp_head(slot):
        do_rp(slot, hgrad.at[slot - 4], hgrad.at[slot - 4])

    def weight_grad(layer, slot):
        for dy in range(3):
            total = None
            for cv in range(2):
                term = lax.dot_general(
                    A3[layer, cv, pl.ds(dy * cols, px), :],
                    G[slot, cv, pl.ds(cols, px), :],
                    (((0,), (0,)), ((), ())),
                    preferred_element_type=full,
                )
                total = term if total is None else total + term
            D[slot, pl.ds(dy * 96, 96)] = total.astype(low).reshape(96, 8, CUT)

    def input_grad(slot, add):
        def canvas(cv, carry):
            take_g(slot, cv)
            for dx in range(3):
                total = None
                for dy in range(3):
                    term = lax.dot_general(
                        G[slot, cv, pl.ds((2 - dy) * cols, px), :],
                        W[slot, pl.ds((3 * dy + dx) * 32, 32)].reshape(CUT, CUT),
                        (((1,), (1,)), ((), ())),
                        preferred_element_type=full,
                    )
                    total = term if total is None else total + term
                if add:
                    U[dx, cv] = U[dx, cv] + total
                else:
                    U[dx, cv] = total
            return carry

        lax.fori_loop(0, 2, canvas, 0)

    def upstream_row(cv, r):
        at = pl.ds(pl.multiple_of(r * cols, cols), cols)
        return U[1, cv, at, :] + move_left(U[0, cv, at, :]) + move_right(U[2, cv, at, :])

    def fold(value):
        return jnp.sum(value.reshape(cols // 8, 8, CUT), axis=0)

    lane = lax.broadcasted_iota(jnp.int32, (1, CUT), 1)
    box_from = cls_out - 2 * CUT

    def log_one_plus(e):
        return jnp.where(e < 0.015625, e * (1.0 + e * (e * (1.0 / 3.0) - 0.5)), jnp.log(1.0 + e))

    def cls_rows(cut, cv, shift):
        here = lane + cut * CUT
        number = here
        for a in range(1, anchors):
            number = number - jnp.where(here >= a * classes, classes, 0)
        number = number.astype(full) - 200.0

        def row(r, carry):
            b_sum, l_sum = carry
            at = pl.ds(pl.multiple_of(r * cols, cols), cols)
            raw = ACC[at, :] + shift
            LS[cut, cv, at, :] = raw.astype(low)
            marks = MK[cut, cv, at, :].astype(full)
            hit = marks == number
            seen = marks < -50.0
            s = jnp.where(hit, -raw, raw)
            e = jnp.exp(-jnp.abs(s))
            inv = 1.0 / (1.0 + e)
            other = e * inv
            q = jnp.where(s >= 0.0, inv, other)
            p = jnp.where(s >= 0.0, other, inv)
            soft = jnp.maximum(s, 0.0) + log_one_plus(e)
            t = jnp.where(seen, jnp.where(hit, focal_alpha, 1.0 - focal_alpha), 0.0) * q * q
            slope = t * (2.0 * p * soft + q) * grad_scale
            g = jnp.where(hit, -slope, slope).astype(low)
            G[4 + cut, cv, pl.ds(pl.multiple_of((r + 1) * cols, cols), cols), :] = g
            return b_sum + fold(g.astype(full)), l_sum + fold(t * soft)

        return row

    def box_rows(cut, cv, shift):
        goal_lane = lax.broadcasted_iota(jnp.int32, (40, LANES), 1) - (box_from - LANES)
        goal_tab = (goal_lane == lax.broadcasted_iota(jnp.int32, (40, LANES), 0)).astype(full)

        def row(r, carry):
            b_sum, l_sum = carry
            at = pl.ds(pl.multiple_of(r * cols, cols), cols)
            raw = ACC[at, :] + shift
            LS[0, cv, at, :] = raw.astype(low)
            marks = MK[cut, cv, at, :].astype(full)
            chosen = marks < -110.0
            want = lax.dot_general(
                GP[cv, r], goal_tab, (((0,), (0,)), ((), ())),
                precision=lax.Precision.HIGHEST, preferred_element_type=full,
            )
            want = jnp.concatenate([jnp.zeros((cols, LANES), full), want], axis=1)
            diff = raw - want
            size = jnp.abs(diff)
            value = jnp.where(
                size < smooth_beta, 0.5 * diff * diff / smooth_beta, size - 0.5 * smooth_beta
            )
            slope = jnp.where(
                size < smooth_beta, diff / smooth_beta, jnp.where(diff > 0.0, 1.0, -1.0)
            )
            g = jnp.where(chosen, slope * grad_scale, 0.0).astype(low)
            G[4 + cut, cv, pl.ds(pl.multiple_of((r + 1) * cols, cols), cols), :] = g
            return b_sum + fold(g.astype(full)), l_sum + fold(jnp.where(chosen, value, 0.0))

        return row

    nothing = jnp.zeros((8, CUT), full)

    def l_copy(cut):
        return remote(LS.at[cut, 1 - x], logits.at[cut], ls.at[cut], lr.at[cut], (par, z))

    def e_copy():
        return remote(LS.at[0, 1 - x], deltas, es.at[0], er.at[0], (par, z))

    @pl.when(is_box)
    def _():
        remote(GP.at[1 - x], GP.at[1 - x], fs.at[2], fr.at[2], (par, z)).wait_recv()

    def head(i, carry):
        cut = 2 - i
        slot = 4 + cut
        gathered(slot)
        shift = bias[pl.ds(2 * layers + cut, 1), :]

        def canvas(cv, carry):
            b_sum, l_sum = carry
            ACC[...] = conv(layers, slot, cv)
            return lax.cond(
                is_cls,
                lambda: rim_first(cls_rows(cut, cv, shift), (b_sum, l_sum), lambda: send_g(slot, cv)),
                lambda: rim_first(box_rows(cut, cv, shift), (b_sum, l_sum), lambda: send_g(slot, cv)),
            )

        b_sum, l_sum = lax.fori_loop(0, 2, canvas, (nothing, nothing))

        @pl.when(is_box)
        def _():
            e_copy().start()

        BG[pl.ds(slot, 1), :] = jnp.sum(b_sum, axis=0, keepdims=True)
        BG[pl.ds(7, 1), :] = BG[pl.ds(7, 1), :] + jnp.sum(l_sum, axis=0, keepdims=True)
        weight_grad(layers, slot)
        do_rd(slot)

        input_grad(slot, True)

        @pl.when(is_cls & (i == 0))
        def _():
            do_d(4)
            handed_over(5)

        @pl.when(is_cls & (i == 0))
        def _():
            do_rx(slot)

        @pl.when(i > 0)
        def _():
            do_ry(slot)

        @pl.when(i == 2)
        def _():
            do_rz(5)

        return carry

    lax.fori_loop(0, 3 - 2 * x, head, 0)

    @pl.when(is_cls)
    def _():
        for cut in range(3):
            l_copy(cut).start()
            logits[cut] = LS[cut, 0]

    @pl.when(is_box)
    def _():
        deltas[...] = LS[0, 1]

    def feature_rows(cv, dst):
        def row(r, carry):
            dst[pl.ds(pl.multiple_of(r * cols, cols), cols), :] = upstream_row(cv, r).astype(dst.dtype)
            return carry

        lax.fori_loop(0, rows, row, 0)

    FS = MK.at[0, 0]
    f_copy = remote(FS, FP, fs.at[3], fr.at[3], (par, z))
    def b_copy(src, dst, dev):
        return remote(src, BR.at[dst], bs.at[dst], br.at[dst], dev)

    def backward(j, carry):
        layer = layers - 1 - j

        def canvas(cv, b_sum):
            def row(r, b_sum):
                at = pl.ds(pl.multiple_of(r * cols, cols), cols)
                g = (upstream_row(cv, r) * silu_slope(Z[layer, cv, at, :])).astype(low)
                G[layer, cv, pl.ds(pl.multiple_of((r + 1) * cols, cols), cols), :] = g
                return b_sum + fold(g.astype(full))

            return rim_first(row, b_sum, lambda: send_g(layer, cv))

        b_sum = lax.fori_loop(0, 2, canvas, nothing)
        BG[pl.ds(layer, 1), :] = jnp.sum(b_sum, axis=0, keepdims=True)
        weight_grad(layer, layer)
        do_rd(layer)

        @pl.when(j == 3)
        def _():
            b_copy(BG, 0, (sib, z)).start()

        @pl.when(j == layers - 1)
        def _():
            do_ry(0, halves=(0,))

        input_grad(layer, False)

        @pl.when(j == layers - 1)
        def _():
            do_ry(0, halves=(1,))
            feature_rows(1 - x, FS)
            f_copy.start()

        @pl.when(j < layers - 1)
        def _():
            do_ry(layer)

        @pl.when(is_cls | (j > 0))
        def _():
            do_rz(layer + 1)

        @pl.when(is_cls & (j == 0))
        def _():
            do_rp_head(5)

        @pl.when(is_cls & (j == 1))
        def _():
            do_rp_head(4)

        @pl.when(j > 1)
        def _():
            do_rp_layer(layer + 2)

        @pl.when(is_box & (j == 0))
        def _():
            do_ry(6, relay=True)

        @pl.when(is_box & (j == 1))
        def _():
            do_rz(6, relay=True)

        @pl.when(is_box & (j == 2))
        def _():
            do_rp_head(6)

        return carry

    lax.fori_loop(0, layers, backward, 0)

    b_copy(BG, 0, (sib, z)).wait_recv()
    BR[6] = BG[...] + BR[0]
    b_copy(BR.at[6], 1, (yn, z)).start()
    feature_rows(x, fgrad)
    b_copy(BR.at[6], 1, (yn, z)).wait_recv()
    total = BR[6] + BR[1]
    for zz in range(4):
        @pl.when(z == zz)
        def _():
            BR[7 + zz] = total
            for o in (1, 2, 3):
                remote(
                    BR.at[7 + zz], BR.at[7 + zz], bs.at[1 + o], br.at[1 + o], (d, zpeer(o))
                ).start()
    do_rz(0)
    do_rp_layer(1)

    for o in (1, 2, 3):
        for zz in range(4):
            @pl.when(zfrom(o) == zz)
            def _():
                remote(
                    BR.at[7 + zz], BR.at[7 + zz], bs.at[1 + o], br.at[1 + o], (d, zpeer(o))
                ).wait_recv()
    total = (BR[7] + BR[8]) + (BR[9] + BR[10])
    BR[5] = total
    last = remote(BR.at[5], bsum.at[x], bs.at[5], br.at[5], (par, z))
    last.start()
    bsum[x] = total
    f_copy.wait_recv()
    fgrad[...] = fgrad[...] + FP[...].astype(full)
    do_rp_layer(0)

    remote(BR.at[5], bsum.at[1 - x], bs.at[5], br.at[5], (par, z)).wait_recv()
    loss = jnp.sum(bsum[0, 7:8, :] + bsum[1, 7:8, :], axis=1, keepdims=True)
    loss_out[...] = jnp.broadcast_to(loss, (8, LANES)) / jnp.maximum(count, 1.0)

    for layer in range(layers):
        rp_send(layer, tgrad.at[layer, 1 - x]).wait_recv()

    @pl.when(is_cls)
    def _():
        e_copy().wait_recv()
        rp_send(6, hgrad.at[2]).wait_recv()
        for b in range(4):
            rx_send(6, b).wait_send()
            d_copy(5, b // 2, b % 2, k).wait_send()
            d_copy(6, b // 2, b % 2, k).wait_send()
        for cut in range(3):
            l_copy(cut).wait_send()
        p_head(2, 4, 1).wait_send()
        p_head(1, 5, 3).wait_send()
        goal_copy.wait_send()

    @pl.when(is_box)
    def _():
        for cut in range(2):
            rp_send(4 + cut, hgrad.at[cut]).wait_recv()
        for cut in range(3):
            l_copy(cut).wait_recv()
        for b in range(4):
            x_copy(5, b // 2, b % 2).wait_send()
            x_copy(6, b // 2, b % 2).wait_send()
            d_copy(6, b // 2, b % 2, k).wait_send()
        e_copy().wait_send()
        p_head(0, 4, 4).wait_send()

    def close_gather(step, carry):
        for xx in range(2):
            for o in (1, 2, 3):
                z_send(step, xx, o).wait_send()
            y_copy(step, xx, y).wait_send()
        return carry

    lax.fori_loop(0, 5 + x, close_gather, 0)

    def close_slot(slot, carry):
        for b in range(4):
            d_copy(slot, b // 2, b % 2, k).wait_send()

        return carry

    lax.fori_loop(0, 5 - x, close_slot, 0)

    def close_layer(layer, carry):
        @pl.when(layer < layers)
        def _():
            p_send(jnp.minimum(layer, layers - 1)).wait_send()

        @pl.when(down_ok() & (layer > 0))
        def _():
            for cv in range(2):
                a_edge(layer, 0, cv).wait_send()

        @pl.when(up_ok() & (layer > 0))
        def _():
            for cv in range(2):
                a_edge(layer, 1, cv).wait_send()

        return carry

    lax.fori_loop(0, layers + 1, close_layer, 0)

    def close_grad(slot, carry):
        @pl.when(is_cls | (slot < 4) | (slot == 6))
        def _():
            for b in range(4):
                rd_send(slot, b).wait_send()

            @pl.when(down_ok())
            def _():
                for cv in range(2):
                    g_edge(slot, 0, cv).wait_send()

            @pl.when(up_ok())
            def _():
                for cv in range(2):
                    g_edge(slot, 1, cv).wait_send()

        @pl.when((slot < 4) | (is_cls & (slot < 6)) | (is_box & (slot == 6)))
        def _():
            for xx in range(2):
                ry_send(slot, xx).wait_send()
                for o in (1, 2, 3):
                    rz_send(slot, xx, o).wait_send()
            rp_send(slot, RP.at[slot]).wait_send()

        return carry

    lax.fori_loop(0, layers + 3, close_grad, 0)
    pltpu_feature.wait_send()

    @pl.when(z < 3)
    def _():
        for across in range(2):
            f_edge(0, across).wait_send()

    @pl.when(z > 0)
    def _():
        for across in range(2):
            f_edge(1, across).wait_send()

    code_copy.wait_send()
    f_copy.wait_send()
    n_copy(0, 4, (sib, z)).wait_send()
    n_copy(1, 5, (yn, z)).wait_send()
    n_copy(2, 6, (par, z)).wait_send()
    b_copy(BG, 0, (sib, z)).wait_send()
    b_copy(BR.at[6], 1, (yn, z)).wait_send()
    for o in (1, 2, 3):
        n_copy(3, 6 + o, (d, zpeer(o))).wait_send()
        remote(BR.at[7], BR.at[7], bs.at[1 + o], br.at[1 + o], (d, zpeer(o))).wait_send()
    last.wait_send()


def finish_kernel(
    step, lg, dl, fg, tg, hg, bsum, loss_in, tw, hw, tm, tv, hm, hv, bw, bm, bv,
    o_lg, o_dl, o_fg, o_tg, o_bg, o_hg, o_tn, o_hn, o_tm, o_tv, o_hm, o_hv, o_tc, o_hc,
    o_loss, o_gb, o_gx, o_wb, o_mb, o_vb,
    TW, TM, TV, TC, HGO, HW, HM, HV, HC, LO, DT, DS, t_out, h_out, m_sem,
    *, layers, rows, cols, cls_out, box_out,
):
    tail = cls_out - 2 * CUT
    last = tail + box_out

    def t_stores(layer):
        pairs = (
            (tg.at[layer, 0], o_tg.at[layer]),
            (tg.at[layer, 1], o_bg.at[layer]),
            (TW.at[layer], o_tn.at[layer]),
            (TM.at[layer], o_tm.at[layer]),
            (TV.at[layer], o_tv.at[layer]),
            (TC.at[layer], o_tc.at[layer]),
        )
        return [pltpu.make_async_copy(a, b, t_out.at[layer, i]) for i, (a, b) in enumerate(pairs)]

    h_stores = [
        pltpu.make_async_copy(a, b, h_out.at[i])
        for i, (a, b) in enumerate(((HGO, o_hg), (HW, o_hn), (HM, o_hm), (HV, o_hv), (HC, o_hc)))
    ]
    lg_store = pltpu.make_async_copy(LO, o_lg, m_sem.at[0])
    fg_store = pltpu.make_async_copy(fg, o_fg, m_sem.at[1])
    fg_store.start()
    for cut, width in ((0, CUT), (1, CUT), (2, tail)):
        LO[:, cut * CUT : cut * CUT + width] = lg[cut][:, :width]
    lg_store.start()

    steps = jnp.broadcast_to(step[0].astype(full), (8, CUT))
    keep_one = (1.0 - jnp.exp(steps * math.log(beta_one)))[0:1, :]
    keep_two = (1.0 - jnp.exp(steps * math.log(beta_two)))[0:1, :]

    def adam(weight, grad, first, second, decay):
        one, two = keep_one[:, : grad.shape[1]], keep_two[:, : grad.shape[1]]
        first_new = beta_one * first + (1.0 - beta_one) * grad
        second_new = beta_two * second + (1.0 - beta_two) * grad * grad
        first_hat = first_new / one
        second_hat = second_new / two
        weight_new = weight - learn_rate * (
            first_hat / (jnp.sqrt(second_hat) + adam_eps) + decay * weight
        )
        return weight_new, first_new, second_new

    for layer in range(layers):
        for t in range(2):
            w_new, m_new, v_new = adam(
                tw[layer, t], tg[layer, t], tm[layer, t], tv[layer, t], decay_rate
            )
            TW[layer, t] = w_new
            TM[layer, t] = m_new
            TV[layer, t] = v_new
            TC[layer, t] = w_new.astype(low)
        for copy in t_stores(layer):
            copy.start()
    for cut, width in ((0, CUT), (1, CUT), (2, last)):
        at = slice(cut * CUT, cut * CUT + width)
        grad = hg[cut][:, :width]
        HGO[:, at] = grad
        w_new, m_new, v_new = adam(hw[:, at], grad, hm[:, at], hv[:, at], decay_rate)
        HW[:, at] = w_new
        HM[:, at] = m_new
        HV[:, at] = v_new
        HC[:, at] = w_new.astype(low)
    for copy in h_stores:
        copy.start()
    o_loss[0] = loss_in[0, 0]
    for q in range(2 * layers + 3):
        if q < 2 * layers:
            grad, width = bsum[q % 2, q // 2 : q // 2 + 1, :], CUT
        elif q < 2 * layers + 2:
            grad, width = bsum[0, q - layers : q - layers + 1, :], CUT
        else:
            lane = lax.broadcasted_iota(jnp.int32, (1, CUT), 1)
            boxes = bsum[1, 6:7, :]
            grad, width = jnp.where(lane < tail, bsum[0, 6:7, :], boxes)[:, :last], last
            o_gx[...] = pltpu.roll(boxes, CUT - tail, 1)[:, :box_out].reshape(box_out)
        at = pl.ds(q * CUT, width)
        w_new, m_new, v_new = adam(
            bw[at].reshape(1, width), grad, bm[at].reshape(1, width), bv[at].reshape(1, width), 0.0
        )
        o_wb[at] = w_new.reshape(width)
        o_mb[at] = m_new.reshape(width)
        o_vb[at] = v_new.reshape(width)
        most = min(width, cls_out + 2 * layers * CUT - q * CUT)
        o_gb[pl.ds(q * CUT, most)] = grad[:, :most].reshape(most)
    pick_lane = lax.broadcasted_iota(jnp.int32, (40, LANES), 1) - (tail - LANES)
    pick = (pick_lane == lax.broadcasted_iota(jnp.int32, (40, LANES), 0)).astype(full).astype(low)
    for r in range(rows):
        DT[r] = lax.dot_general(
            pick, dl[r * cols : (r + 1) * cols, LANES:], (((1,), (1,)), ((), ())), preferred_element_type=full
        )

    def turn(q, carry):
        for r in range(rows):
            DS[q, r : r + 1, :] = DT[r, pl.ds(q, 1), :]
        return carry

    lax.fori_loop(0, box_out, turn, 0)
    o_dl[...] = DS[...].astype(low)

    for layer in range(layers):
        for copy in t_stores(layer):
            copy.wait()
    for copy in h_stores:
        copy.wait()
    lg_store.wait()
    fg_store.wait()


def fused_shards(
    features,
    crop_ids,
    labels,
    positive,
    box_targets,
    tower_weights,
    head_weights,
    biases,
    tower_m,
    tower_v,
    head_m,
    head_v,
    bias_m,
    bias_v,
    step_count,
):
    canvases, rows, cols, channels = features.shape
    layers = tower_weights.shape[0]
    shard_rows = tower_weights.shape[2]
    anchors = labels.shape[-1]
    head_out = head_weights.shape[1]
    box_out = 4 * anchors
    cls_out = head_out - box_out
    px = rows * cols
    piece = shard_rows // 8
    tow = tower_weights.reshape(layers, 2, piece, 8, channels)
    by_anchor = (0, 3, 1, 2)
    marked = jnp.transpose(labels, by_anchor)[0]
    lit = jnp.transpose(positive, by_anchor)[0]
    goals = jnp.transpose(box_targets, by_anchor)[0]
    units = 32 * piece
    block = 4 * piece
    dma = pltpu.SemaphoreType.DMA
    vm = pl.BlockSpec(memory_space=pltpu.VMEM)
    shape = jax.ShapeDtypeStruct
    logits, deltas, fgrad, tgrad, hgrad, bsum, loss = pl.pallas_call(
        partial(
            mega_kernel,
            rows=rows, cols=cols, layers=layers, cls_out=cls_out, box_out=box_out, anchors=anchors, piece=piece,
        ),
        out_shape=(
            shape((3, px, CUT), low),
            shape((px, CUT), low),
            shape((px, CUT), full),
            shape((layers, 2, piece, 8, CUT), full),
            shape((3, piece, 8, CUT), full),
            shape((2, 8, CUT), full),
            shape((8, LANES), full),
        ),
        in_specs=[vm, pl.BlockSpec(memory_space=pltpu.SMEM)] + [vm] * 6,
        out_specs=[vm] * 7,
        scratch_shapes=[
            pltpu.VMEM((7, units, 8, CUT), low),
            pltpu.VMEM((7, units, 8, CUT), low),
            pltpu.VMEM((7, 4, block, 8, CUT), low),
            pltpu.VMEM((7, 2, block, 8, CUT), low),
            pltpu.VMEM((7, 2, 3, piece, 8, CUT), low),
            pltpu.VMEM((4, block, 8, CUT), low),
            pltpu.VMEM((7, piece, 8, CUT), full),
            pltpu.VMEM((layers + 1, 2, px + 2 * cols, 3 * CUT), low),
            pltpu.VMEM((layers + 1, 2, 2, cols, CUT), low),
            pltpu.VMEM((7, 2, px + 2 * cols, CUT), low),
            pltpu.VMEM((layers, 2, px, CUT), full),
            pltpu.VMEM((3, 2, px, CUT), full),
            pltpu.VMEM((px, CUT), full),
            pltpu.VMEM((px, CUT), low),
            pltpu.VMEM((2, rows, 16, cols), full),
            pltpu.VMEM((2, rows, 40, cols), full),
            pltpu.VMEM((3, 2, px, CUT), low),
            pltpu.VMEM((10, 8, LANES), full),
            pltpu.VMEM((8, CUT), full),
            pltpu.VMEM((11, 8, CUT), full),
            pltpu.VMEM((layers, piece, 8, CUT), low),
            pltpu.VMEM((3, piece, 8, CUT), low),
            pltpu.VMEM((16, CUT), full),
            pltpu.VMEM((3, 2, px, CUT), low),
            dma((6,)), dma((6,)),
            dma((6, 2, 3)), dma((6, 2, 3)),
            dma((6, 2)), dma((6, 2)),
            dma((7, 4)), dma((7, 4)),
            dma((2, 4)), dma((2, 4)),
            dma((4,)), dma((4,)),
            dma((layers + 1, 2, 2)), dma((layers + 1, 2, 2)),
            dma((7, 2, 2)), dma((7, 2, 2)),
            dma((3,)), dma((3,)),
            dma((1,)), dma((1,)),
            dma((7, 4)), dma((7, 4)),
            dma((7, 2)), dma((7, 2)),
            dma((7, 2, 3)), dma((7, 2, 3)),
            dma((4,)), dma((4,)),
            dma((7,)), dma((7,)),
            dma((10,)), dma((10,)),
            dma((6,)), dma((6,)),
        ],
        compiler_params=pltpu.CompilerParams(
            vmem_limit_bytes=60 * 1024 * 1024, collective_id=0, has_side_effects=True
        ),
    )(features.reshape(px, channels), crop_ids, marked, lit, goals, tow, head_weights, biases)

    tower_shape = tower_weights.shape
    head_shape = head_weights.shape
    anys = pl.BlockSpec(memory_space=pl.ANY)
    smem = pl.BlockSpec(memory_space=pltpu.SMEM)
    biases_out = biases.shape[0]
    (
        o_lg, o_dl, o_fg, o_tg, o_bg, o_hg, o_tn, o_hn, o_tm, o_tv, o_hm, o_hv, o_tc, o_hc,
        o_loss, o_gb, o_gx, o_wb, o_mb, o_vb,
    ) = pl.pallas_call(
        partial(
            finish_kernel, layers=layers, rows=rows, cols=cols, cls_out=cls_out, box_out=box_out
        ),
        out_shape=(
            shape((px, cls_out), low),
            shape((box_out, rows, cols), low),
            shape((px, channels), full),
            shape((layers, shard_rows, channels), full),
            shape((layers, shard_rows, channels), full),
            shape(head_shape, full),
            shape(tower_shape, full),
            shape(head_shape, full),
            shape(tower_shape, full),
            shape(tower_shape, full),
            shape(head_shape, full),
            shape(head_shape, full),
            shape(tower_shape, low),
            shape(head_shape, low),
            shape((1,), full),
            shape((biases_out - box_out,), full),
            shape((box_out,), full),
            shape((biases_out,), full),
            shape((biases_out,), full),
            shape((biases_out,), full),
        ),
        in_specs=[smem] + [vm] * 16,
        out_specs=[anys, vm] + [anys] * 12 + [smem] + [vm] * 5,
        scratch_shapes=[
            pltpu.VMEM(tower_shape, full),
            pltpu.VMEM(tower_shape, full),
            pltpu.VMEM(tower_shape, full),
            pltpu.VMEM(tower_shape, low),
            pltpu.VMEM(head_shape, full),
            pltpu.VMEM(head_shape, full),
            pltpu.VMEM(head_shape, full),
            pltpu.VMEM(head_shape, full),
            pltpu.VMEM(head_shape, low),
            pltpu.VMEM((px, cls_out), low),
            pltpu.VMEM((rows, 40, cols), full),
            pltpu.VMEM((box_out, rows, cols), full),
            dma((layers, 6)), dma((5,)), dma((2,)),
        ],
        compiler_params=pltpu.CompilerParams(vmem_limit_bytes=60 * 1024 * 1024),
    )(
        step_count, logits, deltas, fgrad, tgrad.reshape(tower_shape), hgrad.reshape(3, shard_rows, CUT), bsum, loss,
        tower_weights, head_weights, tower_m, tower_v, head_m, head_v, biases, bias_m, bias_v,
    )
    field = (canvases, rows, cols, -1)
    return (
        o_lg.reshape(field),
        jnp.transpose(o_dl[None], (0, 2, 3, 1)),
        o_loss.reshape(()),
        o_fg.reshape(field),
        o_tg,
        o_bg,
        o_hg,
        o_gb,
        o_gx,
        o_tn,
        o_hn,
        o_wb,
        o_tm,
        o_tv,
        o_hm,
        o_hv,
        o_mb,
        o_vb,
        o_tc,
        o_hc,
    )


def solution(mesh):
    placed = (
        P("dp", "tower", None, None),
        P("dp", None),
        P("dp", "tower", None, None),
        P("dp", "tower", None, None),
        P("dp", "tower", None, None),
        P(None, None, ("dp", "tower"), None),
        P(("dp", "tower"), None),
        P(),
        P(None, None, ("dp", "tower"), None),
        P(None, None, ("dp", "tower"), None),
        P(("dp", "tower"), None),
        P(("dp", "tower"), None),
        P(),
        P(),
        P(),
    )
    fused = mesh.shape["dp"] == 8 and mesh.shape["tower"] == 4
    return jax.shard_map(
        fused_shards if fused else plain_shards,
        mesh=mesh,
        in_specs=placed,
        out_specs=(
            P("dp", "tower", None, None),
            P("dp", "tower", None, None),
            P(),
            P("dp", "tower", None, None),
            P(None, ("dp", "tower"), None),
            P(None, ("dp", "tower"), None),
            P(("dp", "tower"), None),
            P(),
            P(),
            P(None, None, ("dp", "tower"), None),
            P(("dp", "tower"), None),
            P(),
            P(None, None, ("dp", "tower"), None),
            P(None, None, ("dp", "tower"), None),
            P(("dp", "tower"), None),
            P(("dp", "tower"), None),
            P(),
            P(),
            P(None, None, ("dp", "tower"), None),
            P(("dp", "tower"), None),
        ),
        check_vma=False,
    )
```

```python
import math
from functools import partial

import jax
import jax.numpy as jnp
from jax import lax
from jax.experimental import pallas as pl
from jax.experimental.pallas import tpu as pltpu
from jax.sharding import PartitionSpec as P

beta_one = 0.9
beta_two = 0.999
adam_eps = 1e-08
learn_rate = 0.03
decay_rate = 0.05
focal_alpha = 0.25
smooth_beta = 1.0 / 9.0


def with_halo(shard, sides, width):
    for axis, dim in sides:
        size, length = (lax.axis_size(axis), shard.shape[dim])
        up = [(i, (i + 1) % size) for i in range(size - 1)]
        down = [(j, i) for i, j in up]
        last = lax.slice_in_dim(shard, length - width, length, axis=dim)
        initial = lax.slice_in_dim(shard, 0, width, axis=dim)
        before = lax.ppermute(last, axis, up)
        after = lax.ppermute(initial, axis, down)
        shard = jnp.concatenate([before, shard, after], axis=dim)
    return shard


def act_rim(values):
    return with_halo(values, (("tower", 2),), 1)


def grad_rim(values):
    return with_halo(values, (("tower", 2),), 1)


def pad_cols(values):
    return jnp.pad(values, ((0, 0), (0, 0), (0, 0), (1, 1), (0, 0)))


def silu_value(values):
    return values * jax.nn.sigmoid(values)


def silu_slope(values):
    sig = jax.nn.sigmoid(values)
    return sig * (1.0 + values * (1.0 - sig))


def conv_forward(padded, weight, out_rows, out_cols):
    stacks, canvases, channels = (padded.shape[0], padded.shape[1], padded.shape[-1])
    summed = None
    for row_off in range(3):
        for col_off in range(3):
            tap_index = row_off * 3 + col_off
            window = padded[
                :, :, row_off : row_off + out_rows, col_off : col_off + out_cols, :
            ].reshape(stacks, -1, channels)
            contrib = jnp.einsum(
                "snk,skm->snm",
                window,
                weight[:, tap_index * channels : (tap_index + 1) * channels, :],
                preferred_element_type=jnp.float32,
            )
            summed = contrib if summed is None else summed + contrib
    return summed.reshape(stacks, canvases, out_rows, out_cols, weight.shape[-1])


def conv_input_grad(grad_pad, weight, out_rows, out_cols):
    stacks, canvases, outputs = (grad_pad.shape[0], grad_pad.shape[1], grad_pad.shape[-1])
    channels = weight.shape[1] // 9
    summed = None
    for row_off in range(3):
        for col_off in range(3):
            tap_index = row_off * 3 + col_off
            window = grad_pad[
                :, :, 2 - row_off : 2 - row_off + out_rows, 2 - col_off : 2 - col_off + out_cols, :
            ].reshape(stacks, -1, outputs)
            contrib = jnp.einsum(
                "snm,skm->snk",
                window,
                weight[:, tap_index * channels : (tap_index + 1) * channels, :],
                preferred_element_type=jnp.float32,
            )
            summed = contrib if summed is None else summed + contrib
    return summed.reshape(stacks, canvases, out_rows, out_cols, channels)


def conv_weight_grad(padded, grads):
    stacks, channels = (padded.shape[0], padded.shape[-1])
    out_rows, out_cols = (grads.shape[2], grads.shape[3])
    flat_grads = grads.reshape(stacks, -1, grads.shape[-1])
    pieces = []
    for row_off in range(3):
        for col_off in range(3):
            window = padded[
                :, :, row_off : row_off + out_rows, col_off : col_off + out_cols, :
            ].reshape(stacks, -1, channels)
            pieces.append(
                jnp.einsum("snk,snm->skm", window, flat_grads, preferred_element_type=jnp.float32)
            )
    return jnp.concatenate(pieces, 1)


def adam_update(weight, grad, first, second, step_float, decay):
    first_new = beta_one * first + (1.0 - beta_one) * grad
    second_new = beta_two * second + (1.0 - beta_two) * grad * grad
    first_hat = first_new / (1.0 - jnp.power(beta_one, step_float))
    second_hat = second_new / (1.0 - jnp.power(beta_two, step_float))
    weight_new = weight - learn_rate * (
        first_hat / (jnp.sqrt(second_hat) + adam_eps) + decay * weight
    )
    return (weight_new, first_new, second_new)


def anchor_masks(label_rows, positive_rows, row_flags, classes):
    valid = (label_rows >= 0) & row_flags[:, :, None, None]
    chosen = valid & (positive_rows > 0)
    targets = (
        (label_rows[..., None] == jnp.arange(classes, dtype=jnp.int32)) & chosen[..., None]
    ).astype(jnp.float32)
    return (valid.astype(jnp.float32), chosen.astype(jnp.float32), targets)


def focal_terms(cls_vals, targets, valid_f):
    logit_view = cls_vals.reshape(targets.shape)
    prob = jax.nn.sigmoid(logit_view)
    cross = jax.nn.softplus(logit_view) - targets * logit_view
    prob_true = prob * targets + (1.0 - prob) * (1.0 - targets)
    alpha_weight = focal_alpha * targets + (1.0 - focal_alpha) * (1.0 - targets)
    return jnp.sum(alpha_weight * (1.0 - prob_true) ** 2 * cross * valid_f[..., None])


def smooth_terms(box_vals, goals, chosen_f):
    diff = box_vals.reshape(chosen_f.shape + (4,)) - goals.reshape(chosen_f.shape + (4,))
    abs_diff = jnp.abs(diff)
    smooth = jnp.where(
        abs_diff < smooth_beta, 0.5 * diff * diff / smooth_beta, abs_diff - 0.5 * smooth_beta
    )
    return jnp.sum(smooth * chosen_f[..., None])


def plain_shards(
    features,
    crop_ids,
    labels,
    positive,
    box_targets,
    tower_weights,
    head_weights,
    biases,
    tower_m,
    tower_v,
    head_m,
    head_v,
    bias_m,
    bias_v,
    step_count,
):
    canvases, row_count, col_count, channels = features.shape
    layers = tower_weights.shape[0]
    anchors = labels.shape[-1]
    head_out = head_weights.shape[1]
    box_out = 4 * anchors
    cls_out = head_out - box_out
    classes = cls_out // anchors
    shard = lax.axis_index("tower")
    tower_low, head_stack = (
        lax.all_gather(tower_weights.astype(jnp.bfloat16), ("dp", "tower"), axis=2, tiled=True),
        lax.all_gather(
            head_weights.astype(jnp.bfloat16)[None, None], ("dp", "tower"), axis=2, tiled=True
        ),
    )
    head_low = head_stack[0, 0]
    tower_bias = biases[: 2 * layers * channels].reshape(layers, 2, channels)
    head_bias = biases[2 * layers * channels :]
    cls_weight = head_low[:, :cls_out][None]
    box_weight = head_low[:, cls_out:][None]
    same_rows = crop_ids[:, 1:] == crop_ids[:, :-1]
    edge_true = jnp.ones((crop_ids.shape[0], 1), dtype=jnp.bool_)
    row_ok = jnp.concatenate([edge_true, same_rows], 1) & jnp.concatenate([same_rows, edge_true], 1)
    own_ok = lax.dynamic_slice_in_dim(row_ok, shard * row_count, row_count, 1)
    own_valid, own_chosen, own_targets = anchor_masks(labels, positive, own_ok, classes)
    count_all = lax.psum(jnp.sum(own_chosen), ("dp", "tower"))
    denom = jnp.maximum(count_all, 1.0)
    grad_scale = 1.0 / denom
    kept = []
    preact = []
    current = features[None]
    for layer in range(layers):
        padded = pad_cols(act_rim(current))
        if layer == 0:
            padded = jnp.broadcast_to(padded, (2,) + padded.shape[1:])
        kept.append(padded)
        summed = (
            conv_forward(padded, tower_low[layer], row_count, col_count)
            + tower_bias[layer][:, None, None, None, :]
        )
        preact.append(summed)
        current = silu_value(summed).astype(jnp.bfloat16)
    head_in = pad_cols(act_rim(current))
    kept.append(head_in)
    cls_raw = conv_forward(head_in[0:1], cls_weight, row_count, col_count)[0] + head_bias[:cls_out]
    box_raw = conv_forward(head_in[1:2], box_weight, row_count, col_count)[0] + head_bias[cls_out:]
    focal_value, focal_back = jax.vjp(
        partial(focal_terms, targets=own_targets, valid_f=own_valid), cls_raw
    )
    smooth_value, smooth_back = jax.vjp(
        partial(smooth_terms, goals=box_targets, chosen_f=own_chosen), box_raw
    )
    loss_local = focal_value + smooth_value
    cls_low = focal_back(grad_scale)[0].astype(jnp.bfloat16)
    box_low = smooth_back(grad_scale)[0].astype(jnp.bfloat16)
    head_wgrad = jnp.concatenate(
        [
            conv_weight_grad(head_in[0:1], cls_low[None])[0],
            conv_weight_grad(head_in[1:2], box_low[None])[0],
        ],
        1,
    )
    head_bgrad = jnp.concatenate(
        [
            jnp.sum(cls_low, axis=(0, 1, 2), dtype=jnp.float32),
            jnp.sum(box_low, axis=(0, 1, 2), dtype=jnp.float32),
        ]
    )
    joined = pad_cols(grad_rim(jnp.concatenate([cls_low, box_low], -1)[None]))
    upstream = jnp.concatenate(
        [
            conv_input_grad(joined[..., :cls_out], cls_weight, row_count, col_count),
            conv_input_grad(joined[..., cls_out:], box_weight, row_count, col_count),
        ],
        0,
    )
    tower_grads = [None] * layers
    bias_grads = [None] * layers
    for layer in reversed(range(layers)):
        grad_low = (upstream * silu_slope(preact[layer])).astype(jnp.bfloat16)
        bias_grads[layer] = jnp.sum(grad_low, axis=(1, 2, 3), dtype=jnp.float32)
        tower_grads[layer] = conv_weight_grad(kept[layer], grad_low)
        padded_grad = pad_cols(grad_rim(grad_low))
        upstream = conv_input_grad(padded_grad, tower_low[layer], row_count, col_count)
    feature_grad = upstream[0] + upstream[1]
    tower_shard, head_pair = (
        lax.psum_scatter(
            jnp.stack(tower_grads, 0), ("dp", "tower"), scatter_dimension=2, tiled=True
        ),
        lax.psum_scatter(head_wgrad[None, None], ("dp", "tower"), scatter_dimension=2, tiled=True),
    )
    head_shard = head_pair[0, 0]
    bias_local = jnp.concatenate([jnp.stack(bias_grads, 0).reshape(-1), head_bgrad])
    logits_out = cls_raw.astype(jnp.bfloat16)
    deltas_out = box_raw.astype(jnp.bfloat16)
    bias_grad, loss_total = lax.psum((bias_local, loss_local), ("dp", "tower"))
    loss = loss_total / denom
    step_float = step_count[0].astype(jnp.float32)
    tower_new, tower_m_new, tower_v_new = adam_update(
        tower_weights, tower_shard, tower_m, tower_v, step_float, decay_rate
    )
    head_new, head_m_new, head_v_new = adam_update(
        head_weights, head_shard, head_m, head_v, step_float, decay_rate
    )
    bias_new, bias_m_new, bias_v_new = adam_update(
        biases, bias_grad, bias_m, bias_v, step_float, 0.0
    )
    split_at = bias_grad.shape[0] - box_out
    return (
        logits_out,
        deltas_out,
        loss,
        feature_grad,
        tower_shard[:, 0],
        tower_shard[:, 1],
        head_shard,
        bias_grad[:split_at],
        bias_grad[split_at:],
        tower_new,
        head_new,
        bias_new,
        tower_m_new,
        tower_v_new,
        head_m_new,
        head_v_new,
        bias_m_new,
        bias_v_new,
        tower_new.astype(jnp.bfloat16),
        head_new.astype(jnp.bfloat16),
    )


MESH = pl.DeviceIdType.MESH
low = jnp.bfloat16
full = jnp.float32
LANES = 128
CUT = 256


def mega_kernel(
    feat, crops, marked, lit, goals, tow, hed, bias_all,
    logits, deltas, fgrad, tgrad, hgrad, bsum, loss_out,
    W, D, RD, RY, RZ, RX, RP, A3, HA, G, Z, U, ACC, FP, CP, GP, LS, CNT, BG, BR, TB, HB, bias, MK,
    ps, pr, zs, zr, ys, yr, ds, dr, xs, xr, fs, fr, hs, hr, gs, gr, ls, lr, es, er,
    rds, rdr, rys, ryr, rzs, rzr, rxs, rxr, rps, rpr, ns, nr, bs, br,
    *, rows, cols, layers, cls_out, box_out, anchors, piece,
):
    d = lax.axis_index("dp")
    z = lax.axis_index("tower")
    k = lax.rem(d, 2)
    x = lax.rem(d // 2, 2)
    y = d // 4
    sib = d + 1 - 2 * k
    par = d + 2 - 4 * x
    yn = d + 4 - 8 * y
    is_cls = x == 0
    is_box = x == 1
    block = 4 * piece
    px = rows * cols
    classes = cls_out // anchors

    def remote(src, dst, send, recv, dev):
        return pltpu.make_async_remote_copy(
            src_ref=src, dst_ref=dst, send_sem=send, recv_sem=recv, device_id=dev, device_id_type=MESH
        )

    def blk(yy, xx, kk):
        return pl.ds(((yy * 2 + xx) * 2 + kk) * block, block)

    def pcs(yy, xx, kk, zz):
        return pl.ds(((yy * 2 + xx) * 2 + kk) * block + zz * piece, piece)

    def zpeer(o):
        return lax.rem(z + o, 4)

    def zfrom(o):
        return lax.rem(z + 4 - o, 4)

    barrier = pltpu.get_barrier_semaphore()
    peers = [(sib, z), (par, z), (yn, z), (par, zpeer(1)), (par, zpeer(3))]
    for dev in peers + [(d, zpeer(o)) for o in (1, 2, 3)]:
        pl.semaphore_signal(barrier, inc=1, device_id=dev, device_id_type=MESH)
    pl.semaphore_wait(barrier, 8)

    def f_edge(side, across):
        src = feat.at[pl.ds((rows - 1) * cols if side == 0 else 0, cols)]
        dev = (par if across else d, zpeer(1) if side == 0 else zpeer(3))
        return remote(src, HA.at[0, side, x], hs.at[0, side, across], hr.at[0, side, across], dev)

    def f_edge_in(side, across):
        dst = HA.at[0, side, 1 - x if across else x]
        return remote(dst, dst, hs.at[0, side, across], hr.at[0, side, across], (par, zpeer(1)))

    @pl.when(z < 3)
    def _():
        for across in range(2):
            f_edge(0, across).start()

    @pl.when(z > 0)
    def _():
        for across in range(2):
            f_edge(1, across).start()

    def slot_of(step):
        odd = jnp.where(step == 1, 5, jnp.where(step == 3, 6, 3))
        return jnp.where(is_cls, step, jnp.where(lax.rem(step, 2) == 0, step // 2, odd))

    def p_send(layer):
        theirs = jnp.where(is_cls, jnp.minimum(2 * layer, 5), layer)
        return remote(
            TB.at[layer], W.at[layer, pcs(y, x, k, z)], ps.at[layer], pr.at[theirs], (par, z)
        )

    def p_head(cut, index, theirs):
        return remote(
            HB.at[cut], W.at[4 + cut, pcs(y, x, k, z)], ps.at[index], pr.at[theirs], (par, z)
        )

    def p_recv(step):
        slot = slot_of(step)
        there = W.at[slot, pcs(y, 1 - x, k, z)]
        return remote(there, there, ps.at[step], pr.at[step], (par, z))

    def z_send(step, xx, o):
        here = W.at[slot_of(step), pcs(y, xx, k, z)]
        return remote(here, here, zs.at[step, xx, o - 1], zr.at[step, xx, o - 1], (d, zpeer(o)))

    def z_recv(step, xx, o):
        here = W.at[slot_of(step), pcs(y, xx, k, zfrom(o))]
        return remote(here, here, zs.at[step, xx, o - 1], zr.at[step, xx, o - 1], (d, zpeer(o)))

    def y_copy(step, xx, yy):
        here = W.at[slot_of(step), blk(yy, xx, k)]
        return remote(here, here, ys.at[step, xx], yr.at[step, xx], (yn, z))

    def d_copy(slot, yy, xx, kk):
        here = W.at[slot, blk(yy, xx, kk)]
        return remote(here, here, ds.at[slot, yy * 2 + xx], dr.at[slot, yy * 2 + xx], (sib, z))

    def x_copy(slot, yy, xx):
        here = W.at[slot, blk(yy, xx, k)]
        return remote(here, here, xs.at[slot - 5, yy * 2 + xx], xr.at[slot - 5, yy * 2 + xx], (par, z))

    def has(step):
        return (step < 5) | (is_box & (step < 6))

    def do_z(step):
        @pl.when(has(step))
        def _():
            p_recv(step).wait_recv()
            for xx in range(2):
                for o in (2, 1, 3):
                    z_send(step, xx, o).start()

    def spread(step, yy, xx):
        slot = slot_of(step)

        @pl.when(slot >= 5)
        def _():
            x_copy(slot, yy, xx).start()

        @pl.when(slot != 5)
        def _():
            d_copy(slot, yy, xx, k).start()

    def do_y(step, lead=False):
        @pl.when(has(step))
        def _():
            for xx in range(2):
                for o in (1, 2, 3):
                    z_recv(step, xx, o).wait_recv()
                if lead:
                    if xx == 0:
                        p_recv(step + 1).wait_recv()
                    for o in (2, 1, 3):
                        z_send(step + 1, xx, o).start()
                y_copy(step, xx, y).start()
                spread(step, y, xx)

    def do_d(step):
        @pl.when(has(step))
        def _():
            for xx in range(2):
                y_copy(step, xx, 1 - y).wait_recv()
                spread(step, 1 - y, xx)

    def pump(step, carry=0):
        do_y(step)
        do_d(step - 1)

        @pl.when(step < 5)
        def _():
            do_z(step + 1)

        return carry

    def handed_over(slot):
        for b in range(4):
            x_copy(slot, b // 2, b % 2).wait_recv()
            d_copy(slot, b // 2, b % 2, k).start()

    def gathered(slot):
        for b in range(4):
            d_copy(slot, b // 2, b % 2, 1 - k).wait_recv()

    pltpu_feature = remote(feat, FP, fs.at[0], fr.at[0], (par, z))
    for step in range(layers):
        TB[step] = tow[step, 1 - x].astype(low)
        p_send(step).start()
        W[step, pcs(y, x, k, z)] = tow[step, x].astype(low)
    tail = cls_out + box_out - 2 * CUT
    HB[2] = jnp.zeros((piece, 8, CUT), low)
    for cut, width in ((2, tail), (0, CUT), (1, CUT)):
        part = hed[:, cut * CUT : cut * CUT + width].astype(low)
        HB[cut, :, :, 0:width] = part.reshape(piece, 8, width)

    @pl.when(is_cls)
    def _():
        p_head(2, 4, 3).start()
        p_head(1, 5, 1).start()
        W[4, pcs(y, x, k, z)] = HB[0]

    @pl.when(is_box)
    def _():
        p_head(0, 4, 4).start()
        W[5, pcs(y, x, k, z)] = HB[1]
        W[6, pcs(y, x, k, z)] = HB[2]

    pltpu_feature.start()
    code_copy = remote(CP.at[x], CP.at[x], fs.at[1], fr.at[1], (par, z))
    goal_copy = remote(GP.at[x], GP.at[x], fs.at[2], fr.at[2], (par, z))
    do_z(0)

    def n_copy(index, dst, dev):
        return remote(CNT.at[index], CNT.at[dst], ns.at[dst], nr.at[dst], dev)

    col = lax.broadcasted_iota(jnp.int32, (cols, CUT), 0)
    first_col = col == 0
    last_col = col == cols - 1

    def move_right(v):
        return jnp.where(first_col, 0.0, pltpu.roll(v, 1, 0))

    def move_left(v):
        return jnp.where(last_col, 0.0, pltpu.roll(v, cols - 1, 0))

    def put_row(layer, cv, row, value):
        at = pl.ds(pl.multiple_of(row * cols, cols), cols)
        A3[layer, cv, at, 0:CUT] = move_right(value).astype(low)
        A3[layer, cv, at, CUT : 2 * CUT] = value.astype(low)
        A3[layer, cv, at, 2 * CUT : 3 * CUT] = move_left(value).astype(low)

    def up_ok():
        return z > 0

    def down_ok():
        return z < 3

    def a_edge(layer, side, cv):
        row = rows if side == 0 else 1
        src = A3.at[layer, cv, pl.ds(row * cols, cols), pl.ds(CUT, CUT)]
        dev = (d, lax.rem(z + 1, 4)) if side == 0 else (d, lax.rem(z + 3, 4))
        return remote(src, HA.at[layer, side, cv], hs.at[layer, side, cv], hr.at[layer, side, cv], dev)

    def send_edges(layer, cv):
        @pl.when(down_ok())
        def _():
            a_edge(layer, 0, cv).start()

        @pl.when(up_ok())
        def _():
            a_edge(layer, 1, cv).start()

    def first_edges():
        for side, there in ((0, z > 0), (1, z < 3)):
            @pl.when(there)
            def _():
                for across in range(2):
                    f_edge_in(side, across).wait_recv()
                    cv = 1 - x if across else x
                    put_row(0, cv, 0 if side == 0 else rows + 1, HA[0, side, cv].astype(full))

    def take_edges(layer, cv):
        @pl.when(up_ok())
        def _():
            a_edge(layer, 0, cv).wait_recv()
            put_row(layer, cv, 0, HA[layer, 0, cv].astype(full))

        @pl.when(down_ok())
        def _():
            a_edge(layer, 1, cv).wait_recv()
            put_row(layer, cv, rows + 1, HA[layer, 1, cv].astype(full))

    def rim_first(body, carry, send):
        carry = lax.fori_loop(0, 2, lambda i, c: body(i * (rows - 1), c), carry)
        send()
        return lax.fori_loop(1, rows - 1, body, carry)

    def g_edge(slot, side, cv):
        src = G.at[slot, cv, pl.ds((rows if side == 0 else 1) * cols, cols)]
        dst = G.at[slot, cv, pl.ds(0 if side == 0 else (rows + 1) * cols, cols)]
        dev = (d, lax.rem(z + 1, 4)) if side == 0 else (d, lax.rem(z + 3, 4))
        return remote(src, dst, gs.at[slot, side, cv], gr.at[slot, side, cv], dev)

    def g_recv(slot, side, cv):
        dst = G.at[slot, cv, pl.ds(0 if side == 0 else (rows + 1) * cols, cols)]
        return remote(dst, dst, gs.at[slot, side, cv], gr.at[slot, side, cv], (d, lax.rem(z + 1, 4)))

    def send_g(slot, cv):
        @pl.when(down_ok())
        def _():
            g_edge(slot, 0, cv).start()

        @pl.when(up_ok())
        def _():
            g_edge(slot, 1, cv).start()

    def take_g(slot, cv):
        @pl.when(up_ok())
        def _():
            g_recv(slot, 0, cv).wait_recv()

        @pl.when(down_ok())
        def _():
            g_recv(slot, 1, cv).wait_recv()

    def fill(layer_src, cv):
        def body(r, carry):
            put_row(0, cv, r + 1, layer_src[pl.ds(pl.multiple_of(r * cols, cols), cols), :].astype(full))
            return carry

        lax.fori_loop(0, rows, body, 0)

    fill(feat, x)
    do_y(0, lead=True)

    r_at = lax.broadcasted_iota(jnp.int32, (rows, cols), 0)
    inside = jnp.zeros((rows, cols), jnp.int32)
    for r in range(rows):
        row = z * rows + r
        here = crops[0, row]
        above = crops[0, jnp.maximum(row - 1, 0)]
        below = crops[0, jnp.minimum(row + 1, 4 * rows - 1)]
        ok = jnp.where((here == above) & (here == below), 1, 0)
        inside = jnp.where(r_at == r, ok, inside)
    CP[x] = jnp.zeros((rows, 16, cols), full)
    picked = jnp.zeros((rows, cols), full)
    for a in range(anchors):
        label = marked[a]
        valid = (label >= 0) & (inside > 0)
        chosen = valid & (lit[a] > 0)
        mark = jnp.where(chosen, label - 200, jnp.where(valid, -100, 0)).astype(full)
        picked = picked + jnp.where(chosen, 1.0, 0.0)
        for r in range(rows):
            CP[x, r, a : a + 1, :] = mark[r : r + 1, :]
    CNT[0] = jnp.broadcast_to(jnp.sum(picked), (8, LANES))
    n_copy(0, 4, (sib, z)).start()

    code_copy.start()
    pltpu_feature.wait_recv()
    fill(FP, 1 - x)
    first_edges()
    pump(1)

    def clear(at, layer_count, slot_count):
        def a_body(layer, carry):
            for cv in range(2):
                A3[layer, cv, at, :] = jnp.zeros((cols, 3 * CUT), low)
            return carry

        def g_body(slot, carry):
            for cv in range(2):
                G[slot, cv, at, :] = jnp.zeros((cols, CUT), low)
            return carry

        lax.fori_loop(0, layer_count, a_body, 0)
        lax.fori_loop(0, slot_count, g_body, 0)

    @pl.when(z == 0)
    def _():
        clear(pl.ds(0, cols), layers + 1, layers + 3)

    @pl.when(z == 3)
    def _():
        clear(pl.ds((rows + 1) * cols, cols), layers + 1, layers + 3)

    BG[...] = jnp.zeros((8, CUT), full)
    GP[x] = jnp.zeros((rows, 40, cols), full)

    def goal_rows(q, carry):
        for r in range(rows):
            GP[x, r, pl.ds(q, 1), :] = goals[q, r : r + 1, :]
        return carry

    lax.fori_loop(0, box_out, goal_rows, 0)
    for q in range(2 * layers + 2):
        bias[q : q + 1, :] = bias_all[q * CUT : (q + 1) * CUT].reshape(1, CUT)
    q = 2 * layers + 2
    bias[q : q + 1, :] = jnp.zeros((1, CUT), full)
    bias[q : q + 1, 0:tail] = bias_all[q * CUT : q * CUT + tail].reshape(1, tail)

    U[...] = jnp.zeros(U.shape, full)

    @pl.when(is_cls)
    def _():
        goal_copy.start()

    n_copy(0, 4, (sib, z)).wait_recv()
    CNT[1] = CNT[0] + CNT[4]
    n_copy(1, 5, (yn, z)).start()

    lane_tab = lax.broadcasted_iota(jnp.int32, (16, CUT), 1)
    anchor_tab = lax.broadcasted_iota(jnp.int32, (16, CUT), 0)

    def write_marks():
        remote(CP.at[1 - x], CP.at[1 - x], fs.at[1], fr.at[1], (par, z)).wait_recv()
        spot = lane_tab - (cls_out - 2 * CUT)
        box_tab = jnp.where(
            (spot >= anchor_tab * 4) & (spot < (anchor_tab + 1) * 4) & (anchor_tab < anchors), 1.0, 0.0
        )
        tables = []
        for cut in range(3):
            channel = lane_tab + cut * CUT
            table = jnp.where(
                (channel >= anchor_tab * classes) & (channel < (anchor_tab + 1) * classes) & (channel < cls_out),
                1.0,
                0.0,
            )
            if cut == 2:
                side = x.astype(full)
                table = table * (1.0 - side) + box_tab * side
            tables.append(table.astype(low))

        def row(r, carry):
            at = pl.ds(pl.multiple_of(r * cols, cols), cols)
            for cv in range(2):
                codes = CP[cv, r].astype(low)
                for cut in range(3):
                    MK[cut, cv, at, :] = lax.dot_general(
                        codes, tables[cut], (((0,), (0,)), ((), ())), preferred_element_type=full
                    ).astype(low)
            return carry

        lax.fori_loop(0, rows, row, 0)

    def conv(layer, slot, cv):
        total = None
        for dy in range(3):
            term = jnp.dot(
                A3[layer, cv, pl.ds(dy * cols, px), :],
                W[slot, pl.ds(dy * 96, 96)].reshape(3 * CUT, CUT),
                preferred_element_type=full,
            )
            total = term if total is None else total + term
        return total

    def forward(layer, carry):
        gathered(layer)
        shift = bias[pl.ds(2 * layer + x, 1), :]

        def canvas(cv, carry):
            @pl.when(layer > 0)
            def _():
                take_edges(layer, cv)

            Z[layer, cv] = conv(layer, layer, cv)

            def row(r, carry):
                at = pl.ds(pl.multiple_of(r * cols, cols), cols)
                value = Z[layer, cv, at, :] + shift
                Z[layer, cv, at, :] = value
                put_row(layer + 1, cv, r + 1, silu_value(value))
                return carry

            rim_first(row, 0, lambda: send_edges(layer + 1, cv))
            return carry

        lax.fori_loop(0, 2, canvas, 0)
        first = jnp.where(is_cls, layer + 2, 2 * layer + 2)
        after = jnp.where(is_cls, jnp.minimum(layer + 3, 5), jnp.minimum(2 * layer + 4, 7))
        lax.fori_loop(first, after, pump, 0)

        @pl.when(layer == 0)
        def _():
            n_copy(1, 5, (yn, z)).wait_recv()
            CNT[2] = CNT[1] + CNT[5]
            n_copy(2, 6, (par, z)).start()

        @pl.when(layer == 1)
        def _():
            write_marks()
            n_copy(2, 6, (par, z)).wait_recv()
            CNT[3] = CNT[2] + CNT[6]
            for o in (1, 2, 3):
                n_copy(3, 6 + o, (d, zpeer(o))).start()

        return carry

    lax.fori_loop(0, layers, forward, 0)
    for o in (1, 2, 3):
        n_copy(3, 6 + o, (d, zpeer(o))).wait_recv()
    count = CNT[3] + CNT[7] + CNT[8] + CNT[9]
    grad_scale = (1.0 / jnp.maximum(count, 1.0))[0:1, 0:1]

    @pl.when(is_cls)
    def _():
        handed_over(5)

    for cv in range(2):
        take_edges(layers, cv)

    def rd_send(slot, b):
        src = D.at[slot, blk(b // 2, b % 2, 1 - k)]
        return remote(src, RD.at[slot, b], rds.at[slot, b], rdr.at[slot, b], (sib, z))

    def ry_send(slot, xx):
        src = D.at[slot, blk(1 - y, xx, k)]
        return remote(src, RY.at[slot, xx], rys.at[slot, xx], ryr.at[slot, xx], (yn, z))

    def rz_send(slot, xx, o):
        src = D.at[slot, pcs(y, xx, k, zpeer(o))]
        return remote(
            src, RZ.at[slot, xx, o - 1], rzs.at[slot, xx, o - 1], rzr.at[slot, xx, o - 1], (d, zpeer(o))
        )

    def rx_send(slot, b):
        src = D.at[slot, blk(b // 2, b % 2, k)]
        return remote(src, RX.at[b], rxs.at[b], rxr.at[b], (par, z))

    def add_into(slot, place, terms, own=True):
        units = block // 3

        def body(i, carry):
            here = pl.ds(place + i * units, units)
            there = pl.ds(i * units, units)
            total = D[slot, here].astype(full) if own else None
            for ref in terms:
                term = ref[there].astype(full)
                total = term if total is None else total + term
            D[slot, here] = total.astype(low)
            return carry

        lax.fori_loop(0, 3, body, 0)

    def start_of(yy, xx, kk):
        return ((yy * 2 + xx) * 2 + kk) * block

    def do_rd(slot):
        for b in range(4):
            rd_send(slot, b).start()

    def here_terms(slot, b, own, relay):
        terms = []
        if own:
            rd_send(slot, b).wait_recv()
            terms.append(RD.at[slot, b])
        if relay:
            rx_send(slot, b).wait_recv()
            terms.append(RX.at[b])
        return terms

    def do_ry(slot, own=True, relay=False, halves=(0, 1)):
        for xx in halves:
            terms = here_terms(slot, (1 - y) * 2 + xx, own, relay)
            add_into(slot, start_of(1 - y, xx, k), terms, own)
            ry_send(slot, xx).start()

    def do_rx(slot):
        for b in range(4):
            rd_send(slot, b).wait_recv()
            add_into(slot, start_of(b // 2, b % 2, k), [RD.at[slot, b]])
            rx_send(slot, b).start()

    def do_rz(slot, own=True, relay=False):
        for xx in range(2):
            terms = here_terms(slot, y * 2 + xx, own, relay)
            ry_send(slot, xx).wait_recv()
            terms.append(RY.at[slot, xx])
            add_into(slot, start_of(y, xx, k), terms, own)
            for o in (2, 1, 3):
                rz_send(slot, xx, o).start()

    def piece_sum(slot, xx):
        total = D[slot, pcs(y, xx, k, z)].astype(full)
        for o in (1, 2, 3):
            rz_send(slot, xx, o).wait_recv()
            total = total + RZ[slot, xx, o - 1].astype(full)
        return total

    def rp_send(slot, dst):
        return remote(RP.at[slot], dst, rps.at[slot], rpr.at[slot], (par, z))

    def do_rp(slot, dst_own, dst_other):
        RP[slot] = piece_sum(slot, 1 - x)
        rp_send(slot, dst_other).start()
        dst_own[...] = piece_sum(slot, x)

    def do_rp_layer(layer):
        do_rp(layer, tgrad.at[layer, x], tgrad.at[layer, x])

    def do_rp_head(slot):
        do_rp(slot, hgrad.at[slot - 4], hgrad.at[slot - 4])

    def weight_grad(layer, slot):
        for dy in range(3):
            total = None
            for cv in range(2):
                term = lax.dot_general(
                    A3[layer, cv, pl.ds(dy * cols, px), :],
                    G[slot, cv, pl.ds(cols, px), :],
                    (((0,), (0,)), ((), ())),
                    preferred_element_type=full,
                )
                total = term if total is None else total + term
            D[slot, pl.ds(dy * 96, 96)] = total.astype(low).reshape(96, 8, CUT)

    def input_grad(slot, add):
        def canvas(cv, carry):
            take_g(slot, cv)
            for dx in range(3):
                total = None
                for dy in range(3):
                    term = lax.dot_general(
                        G[slot, cv, pl.ds((2 - dy) * cols, px), :],
                        W[slot, pl.ds((3 * dy + dx) * 32, 32)].reshape(CUT, CUT),
                        (((1,), (1,)), ((), ())),
                        preferred_element_type=full,
                    )
                    total = term if total is None else total + term
                if add:
                    U[dx, cv] = U[dx, cv] + total
                else:
                    U[dx, cv] = total
            return carry

        lax.fori_loop(0, 2, canvas, 0)

    def upstream_row(cv, r):
        at = pl.ds(pl.multiple_of(r * cols, cols), cols)
        return U[1, cv, at, :] + move_left(U[0, cv, at, :]) + move_right(U[2, cv, at, :])

    def fold(value):
        return jnp.sum(value.reshape(cols // 8, 8, CUT), axis=0)

    lane = lax.broadcasted_iota(jnp.int32, (1, CUT), 1)
    box_from = cls_out - 2 * CUT

    def log_one_plus(e):
        return jnp.where(e < 0.015625, e * (1.0 + e * (e * (1.0 / 3.0) - 0.5)), jnp.log(1.0 + e))

    def cls_rows(cut, cv, shift):
        here = lane + cut * CUT
        number = here
        for a in range(1, anchors):
            number = number - jnp.where(here >= a * classes, classes, 0)
        number = number.astype(full) - 200.0

        def row(r, carry):
            b_sum, l_sum = carry
            at = pl.ds(pl.multiple_of(r * cols, cols), cols)
            raw = ACC[at, :] + shift
            LS[cut, cv, at, :] = raw.astype(low)
            marks = MK[cut, cv, at, :].astype(full)
            hit = marks == number
            seen = marks < -50.0
            s = jnp.where(hit, -raw, raw)
            e = jnp.exp(-jnp.abs(s))
            inv = 1.0 / (1.0 + e)
            other = e * inv
            q = jnp.where(s >= 0.0, inv, other)
            p = jnp.where(s >= 0.0, other, inv)
            soft = jnp.maximum(s, 0.0) + log_one_plus(e)
            t = jnp.where(seen, jnp.where(hit, focal_alpha, 1.0 - focal_alpha), 0.0) * q * q
            slope = t * (2.0 * p * soft + q) * grad_scale
            g = jnp.where(hit, -slope, slope).astype(low)
            G[4 + cut, cv, pl.ds(pl.multiple_of((r + 1) * cols, cols), cols), :] = g
            return b_sum + fold(g.astype(full)), l_sum + fold(t * soft)

        return row

    def box_rows(cut, cv, shift):
        goal_lane = lax.broadcasted_iota(jnp.int32, (40, LANES), 1) - (box_from - LANES)
        goal_tab = (goal_lane == lax.broadcasted_iota(jnp.int32, (40, LANES), 0)).astype(full)

        def row(r, carry):
            b_sum, l_sum = carry
            at = pl.ds(pl.multiple_of(r * cols, cols), cols)
            raw = ACC[at, :] + shift
            LS[0, cv, at, :] = raw.astype(low)
            marks = MK[cut, cv, at, :].astype(full)
            chosen = marks < -110.0
            want = lax.dot_general(
                GP[cv, r], goal_tab, (((0,), (0,)), ((), ())),
                precision=lax.Precision.HIGHEST, preferred_element_type=full,
            )
            want = jnp.concatenate([jnp.zeros((cols, LANES), full), want], axis=1)
            diff = raw - want
            size = jnp.abs(diff)
            value = jnp.where(
                size < smooth_beta, 0.5 * diff * diff / smooth_beta, size - 0.5 * smooth_beta
            )
            slope = jnp.where(
                size < smooth_beta, diff / smooth_beta, jnp.where(diff > 0.0, 1.0, -1.0)
            )
            g = jnp.where(chosen, slope * grad_scale, 0.0).astype(low)
            G[4 + cut, cv, pl.ds(pl.multiple_of((r + 1) * cols, cols), cols), :] = g
            return b_sum + fold(g.astype(full)), l_sum + fold(jnp.where(chosen, value, 0.0))

        return row

    nothing = jnp.zeros((8, CUT), full)

    def l_copy(cut):
        return remote(LS.at[cut, 1 - x], logits.at[cut], ls.at[cut], lr.at[cut], (par, z))

    def e_copy():
        return remote(LS.at[0, 1 - x], deltas, es.at[0], er.at[0], (par, z))

    @pl.when(is_box)
    def _():
        remote(GP.at[1 - x], GP.at[1 - x], fs.at[2], fr.at[2], (par, z)).wait_recv()

    def head(i, carry):
        cut = jnp.where(i == 2, 0, i + 1)
        slot = 4 + cut
        gathered(slot)
        shift = bias[pl.ds(2 * layers + cut, 1), :]

        def canvas(cv, carry):
            b_sum, l_sum = carry
            ACC[...] = conv(layers, slot, cv)
            return lax.cond(
                is_cls,
                lambda: rim_first(cls_rows(cut, cv, shift), (b_sum, l_sum), lambda: send_g(slot, cv)),
                lambda: rim_first(box_rows(cut, cv, shift), (b_sum, l_sum), lambda: send_g(slot, cv)),
            )

        b_sum, l_sum = lax.fori_loop(0, 2, canvas, (nothing, nothing))

        @pl.when(is_box)
        def _():
            e_copy().start()

        BG[pl.ds(slot, 1), :] = jnp.sum(b_sum, axis=0, keepdims=True)
        BG[pl.ds(7, 1), :] = BG[pl.ds(7, 1), :] + jnp.sum(l_sum, axis=0, keepdims=True)
        weight_grad(layers, slot)
        do_rd(slot)

        @pl.when(is_cls & (i == 2))
        def _():
            do_rz(5)

        input_grad(slot, True)

        @pl.when(is_cls & (i == 0))
        def _():
            do_d(4)
            handed_over(6)

        @pl.when(is_cls & (i == 1))
        def _():
            do_rx(6)

        @pl.when(i != 1)
        def _():
            do_ry(slot)

        return carry

    lax.fori_loop(x, 3 - x, head, 0)

    @pl.when(is_cls)
    def _():
        for cut in range(3):
            l_copy(cut).start()
            logits[cut] = LS[cut, 0]

    @pl.when(is_box)
    def _():
        deltas[...] = LS[0, 1]

    def feature_rows(cv, dst):
        def row(r, carry):
            dst[pl.ds(pl.multiple_of(r * cols, cols), cols), :] = upstream_row(cv, r).astype(dst.dtype)
            return carry

        lax.fori_loop(0, rows, row, 0)

    FS = MK.at[0, 0]
    f_copy = remote(FS, FP, fs.at[3], fr.at[3], (par, z))
    def b_copy(src, dst, dev):
        return remote(src, BR.at[dst], bs.at[dst], br.at[dst], dev)

    def backward(j, carry):
        layer = layers - 1 - j

        def canvas(cv, b_sum):
            def row(r, b_sum):
                at = pl.ds(pl.multiple_of(r * cols, cols), cols)
                g = (upstream_row(cv, r) * silu_slope(Z[layer, cv, at, :])).astype(low)
                G[layer, cv, pl.ds(pl.multiple_of((r + 1) * cols, cols), cols), :] = g
                return b_sum + fold(g.astype(full))

            return rim_first(row, b_sum, lambda: send_g(layer, cv))

        b_sum = lax.fori_loop(0, 2, canvas, nothing)
        BG[pl.ds(layer, 1), :] = jnp.sum(b_sum, axis=0, keepdims=True)
        weight_grad(layer, layer)
        do_rd(layer)

        @pl.when(j == 3)
        def _():
            b_copy(BG, 0, (sib, z)).start()

        @pl.when(is_cls | (j > 0))
        def _():
            do_rz(layer + 1)

        @pl.when(j == layers - 1)
        def _():
            do_ry(0, halves=(0,))

        input_grad(layer, False)

        @pl.when(j == layers - 1)
        def _():
            do_ry(0, halves=(1,))
            feature_rows(1 - x, FS)
            f_copy.start()

        @pl.when(j < layers - 1)
        def _():
            do_ry(layer)

        @pl.when(is_cls & (j == 0))
        def _():
            do_rp_head(5)

        @pl.when(is_cls & (j == 1))
        def _():
            do_rp_head(4)

        @pl.when(j > 1)
        def _():
            do_rp_layer(layer + 2)

        @pl.when(is_box & (j == 1))
        def _():
            do_ry(6, relay=True)

        @pl.when(is_box & (j == 2))
        def _():
            do_rz(6, relay=True)

        @pl.when(is_box & (j == 3))
        def _():
            do_rp_head(6)

        return carry

    lax.fori_loop(0, layers, backward, 0)

    b_copy(BG, 0, (sib, z)).wait_recv()
    BR[6] = BG[...] + BR[0]
    b_copy(BR.at[6], 1, (yn, z)).start()
    feature_rows(x, fgrad)
    b_copy(BR.at[6], 1, (yn, z)).wait_recv()
    total = BR[6] + BR[1]
    for zz in range(4):
        @pl.when(z == zz)
        def _():
            BR[7 + zz] = total
            for o in (1, 2, 3):
                remote(
                    BR.at[7 + zz], BR.at[7 + zz], bs.at[1 + o], br.at[1 + o], (d, zpeer(o))
                ).start()
    do_rz(0)
    do_rp_layer(1)

    for o in (1, 2, 3):
        for zz in range(4):
            @pl.when(zfrom(o) == zz)
            def _():
                remote(
                    BR.at[7 + zz], BR.at[7 + zz], bs.at[1 + o], br.at[1 + o], (d, zpeer(o))
                ).wait_recv()
    total = (BR[7] + BR[8]) + (BR[9] + BR[10])
    BR[5] = total
    last = remote(BR.at[5], bsum.at[x], bs.at[5], br.at[5], (par, z))
    last.start()
    bsum[x] = total
    f_copy.wait_recv()
    fgrad[...] = fgrad[...] + FP[...].astype(full)
    do_rp_layer(0)

    remote(BR.at[5], bsum.at[1 - x], bs.at[5], br.at[5], (par, z)).wait_recv()
    loss = jnp.sum(bsum[0, 7:8, :] + bsum[1, 7:8, :], axis=1, keepdims=True)
    loss_out[...] = jnp.broadcast_to(loss, (8, LANES)) / jnp.maximum(count, 1.0)

    for layer in range(layers):
        rp_send(layer, tgrad.at[layer, 1 - x]).wait_recv()

    @pl.when(is_cls)
    def _():
        e_copy().wait_recv()
        rp_send(6, hgrad.at[2]).wait_recv()
        for b in range(4):
            rx_send(6, b).wait_send()
            d_copy(5, b // 2, b % 2, k).wait_send()
            d_copy(6, b // 2, b % 2, k).wait_send()
        for cut in range(3):
            l_copy(cut).wait_send()
        p_head(2, 4, 3).wait_send()
        p_head(1, 5, 1).wait_send()
        goal_copy.wait_send()

    @pl.when(is_box)
    def _():
        for cut in range(2):
            rp_send(4 + cut, hgrad.at[cut]).wait_recv()
        for cut in range(3):
            l_copy(cut).wait_recv()
        for b in range(4):
            x_copy(5, b // 2, b % 2).wait_send()
            x_copy(6, b // 2, b % 2).wait_send()
            d_copy(6, b // 2, b % 2, k).wait_send()
        e_copy().wait_send()
        p_head(0, 4, 4).wait_send()

    def close_gather(step, carry):
        for xx in range(2):
            for o in (1, 2, 3):
                z_send(step, xx, o).wait_send()
            y_copy(step, xx, y).wait_send()
        return carry

    lax.fori_loop(0, 5 + x, close_gather, 0)

    def close_slot(slot, carry):
        for b in range(4):
            d_copy(slot, b // 2, b % 2, k).wait_send()

        return carry

    lax.fori_loop(0, 5 - x, close_slot, 0)

    def close_layer(layer, carry):
        @pl.when(layer < layers)
        def _():
            p_send(jnp.minimum(layer, layers - 1)).wait_send()

        @pl.when(down_ok() & (layer > 0))
        def _():
            for cv in range(2):
                a_edge(layer, 0, cv).wait_send()

        @pl.when(up_ok() & (layer > 0))
        def _():
            for cv in range(2):
                a_edge(layer, 1, cv).wait_send()

        return carry

    lax.fori_loop(0, layers + 1, close_layer, 0)

    def close_grad(slot, carry):
        @pl.when(is_cls | (slot < 4) | (slot == 6))
        def _():
            for b in range(4):
                rd_send(slot, b).wait_send()

            @pl.when(down_ok())
            def _():
                for cv in range(2):
                    g_edge(slot, 0, cv).wait_send()

            @pl.when(up_ok())
            def _():
                for cv in range(2):
                    g_edge(slot, 1, cv).wait_send()

        @pl.when((slot < 4) | (is_cls & (slot < 6)) | (is_box & (slot == 6)))
        def _():
            for xx in range(2):
                ry_send(slot, xx).wait_send()
                for o in (1, 2, 3):
                    rz_send(slot, xx, o).wait_send()
            rp_send(slot, RP.at[slot]).wait_send()

        return carry

    lax.fori_loop(0, layers + 3, close_grad, 0)
    pltpu_feature.wait_send()

    @pl.when(z < 3)
    def _():
        for across in range(2):
            f_edge(0, across).wait_send()

    @pl.when(z > 0)
    def _():
        for across in range(2):
            f_edge(1, across).wait_send()

    code_copy.wait_send()
    f_copy.wait_send()
    n_copy(0, 4, (sib, z)).wait_send()
    n_copy(1, 5, (yn, z)).wait_send()
    n_copy(2, 6, (par, z)).wait_send()
    b_copy(BG, 0, (sib, z)).wait_send()
    b_copy(BR.at[6], 1, (yn, z)).wait_send()
    for o in (1, 2, 3):
        n_copy(3, 6 + o, (d, zpeer(o))).wait_send()
        remote(BR.at[7], BR.at[7], bs.at[1 + o], br.at[1 + o], (d, zpeer(o))).wait_send()
    last.wait_send()


def finish_kernel(
    step, lg, dl, fg, tg, hg, bsum, loss_in, tw, hw, tm, tv, hm, hv, bw, bm, bv,
    o_lg, o_dl, o_fg, o_tg, o_bg, o_hg, o_tn, o_hn, o_tm, o_tv, o_hm, o_hv, o_tc, o_hc,
    o_loss, o_gb, o_gx, o_wb, o_mb, o_vb,
    TW, TM, TV, TC, HGO, HW, HM, HV, HC, LO, DT, DS, t_out, h_out, m_sem,
    *, layers, rows, cols, cls_out, box_out,
):
    tail = cls_out - 2 * CUT
    last = tail + box_out

    def t_stores(layer):
        pairs = (
            (tg.at[layer, 0], o_tg.at[layer]),
            (tg.at[layer, 1], o_bg.at[layer]),
            (TW.at[layer], o_tn.at[layer]),
            (TM.at[layer], o_tm.at[layer]),
            (TV.at[layer], o_tv.at[layer]),
            (TC.at[layer], o_tc.at[layer]),
        )
        return [pltpu.make_async_copy(a, b, t_out.at[layer, i]) for i, (a, b) in enumerate(pairs)]

    h_stores = [
        pltpu.make_async_copy(a, b, h_out.at[i])
        for i, (a, b) in enumerate(((HGO, o_hg), (HW, o_hn), (HM, o_hm), (HV, o_hv), (HC, o_hc)))
    ]
    lg_store = pltpu.make_async_copy(LO, o_lg, m_sem.at[0])
    fg_store = pltpu.make_async_copy(fg, o_fg, m_sem.at[1])
    fg_store.start()
    for cut, width in ((0, CUT), (1, CUT), (2, tail)):
        LO[:, cut * CUT : cut * CUT + width] = lg[cut][:, :width]
    lg_store.start()

    steps = jnp.broadcast_to(step[0].astype(full), (8, CUT))
    keep_one = (1.0 - jnp.exp(steps * math.log(beta_one)))[0:1, :]
    keep_two = (1.0 - jnp.exp(steps * math.log(beta_two)))[0:1, :]

    def adam(weight, grad, first, second, decay):
        one, two = keep_one[:, : grad.shape[1]], keep_two[:, : grad.shape[1]]
        first_new = beta_one * first + (1.0 - beta_one) * grad
        second_new = beta_two * second + (1.0 - beta_two) * grad * grad
        first_hat = first_new / one
        second_hat = second_new / two
        weight_new = weight - learn_rate * (
            first_hat / (jnp.sqrt(second_hat) + adam_eps) + decay * weight
        )
        return weight_new, first_new, second_new

    for layer in range(layers):
        for t in range(2):
            w_new, m_new, v_new = adam(
                tw[layer, t], tg[layer, t], tm[layer, t], tv[layer, t], decay_rate
            )
            TW[layer, t] = w_new
            TM[layer, t] = m_new
            TV[layer, t] = v_new
            TC[layer, t] = w_new.astype(low)
        for copy in t_stores(layer):
            copy.start()
    for cut, width in ((0, CUT), (1, CUT), (2, last)):
        at = slice(cut * CUT, cut * CUT + width)
        grad = hg[cut][:, :width]
        HGO[:, at] = grad
        w_new, m_new, v_new = adam(hw[:, at], grad, hm[:, at], hv[:, at], decay_rate)
        HW[:, at] = w_new
        HM[:, at] = m_new
        HV[:, at] = v_new
        HC[:, at] = w_new.astype(low)
    for copy in h_stores:
        copy.start()
    o_loss[0] = loss_in[0, 0]
    for q in range(2 * layers + 3):
        if q < 2 * layers:
            grad, width = bsum[q % 2, q // 2 : q // 2 + 1, :], CUT
        elif q < 2 * layers + 2:
            grad, width = bsum[0, q - layers : q - layers + 1, :], CUT
        else:
            lane = lax.broadcasted_iota(jnp.int32, (1, CUT), 1)
            boxes = bsum[1, 6:7, :]
            grad, width = jnp.where(lane < tail, bsum[0, 6:7, :], boxes)[:, :last], last
            o_gx[...] = pltpu.roll(boxes, CUT - tail, 1)[:, :box_out].reshape(box_out)
        at = pl.ds(q * CUT, width)
        w_new, m_new, v_new = adam(
            bw[at].reshape(1, width), grad, bm[at].reshape(1, width), bv[at].reshape(1, width), 0.0
        )
        o_wb[at] = w_new.reshape(width)
        o_mb[at] = m_new.reshape(width)
        o_vb[at] = v_new.reshape(width)
        most = min(width, cls_out + 2 * layers * CUT - q * CUT)
        o_gb[pl.ds(q * CUT, most)] = grad[:, :most].reshape(most)
    pick_lane = lax.broadcasted_iota(jnp.int32, (40, LANES), 1) - (tail - LANES)
    pick = (pick_lane == lax.broadcasted_iota(jnp.int32, (40, LANES), 0)).astype(full).astype(low)
    for r in range(rows):
        DT[r] = lax.dot_general(
            pick, dl[r * cols : (r + 1) * cols, LANES:], (((1,), (1,)), ((), ())), preferred_element_type=full
        )

    def turn(q, carry):
        for r in range(rows):
            DS[q, r : r + 1, :] = DT[r, pl.ds(q, 1), :]
        return carry

    lax.fori_loop(0, box_out, turn, 0)
    o_dl[...] = DS[...].astype(low)

    for layer in range(layers):
        for copy in t_stores(layer):
            copy.wait()
    for copy in h_stores:
        copy.wait()
    lg_store.wait()
    fg_store.wait()


def fused_shards(
    features,
    crop_ids,
    labels,
    positive,
    box_targets,
    tower_weights,
    head_weights,
    biases,
    tower_m,
    tower_v,
    head_m,
    head_v,
    bias_m,
    bias_v,
    step_count,
):
    canvases, rows, cols, channels = features.shape
    layers = tower_weights.shape[0]
    shard_rows = tower_weights.shape[2]
    anchors = labels.shape[-1]
    head_out = head_weights.shape[1]
    box_out = 4 * anchors
    cls_out = head_out - box_out
    px = rows * cols
    piece = shard_rows // 8
    tow = tower_weights.reshape(layers, 2, piece, 8, channels)
    by_anchor = (0, 3, 1, 2)
    marked = jnp.transpose(labels, by_anchor)[0]
    lit = jnp.transpose(positive, by_anchor)[0]
    goals = jnp.transpose(box_targets, by_anchor)[0]
    units = 32 * piece
    block = 4 * piece
    dma = pltpu.SemaphoreType.DMA
    vm = pl.BlockSpec(memory_space=pltpu.VMEM)
    shape = jax.ShapeDtypeStruct
    logits, deltas, fgrad, tgrad, hgrad, bsum, loss = pl.pallas_call(
        partial(
            mega_kernel,
            rows=rows, cols=cols, layers=layers, cls_out=cls_out, box_out=box_out, anchors=anchors, piece=piece,
        ),
        out_shape=(
            shape((3, px, CUT), low),
            shape((px, CUT), low),
            shape((px, CUT), full),
            shape((layers, 2, piece, 8, CUT), full),
            shape((3, piece, 8, CUT), full),
            shape((2, 8, CUT), full),
            shape((8, LANES), full),
        ),
        in_specs=[vm, pl.BlockSpec(memory_space=pltpu.SMEM)] + [vm] * 6,
        out_specs=[vm] * 7,
        scratch_shapes=[
            pltpu.VMEM((7, units, 8, CUT), low),
            pltpu.VMEM((7, units, 8, CUT), low),
            pltpu.VMEM((7, 4, block, 8, CUT), low),
            pltpu.VMEM((7, 2, block, 8, CUT), low),
            pltpu.VMEM((7, 2, 3, piece, 8, CUT), low),
            pltpu.VMEM((4, block, 8, CUT), low),
            pltpu.VMEM((7, piece, 8, CUT), full),
            pltpu.VMEM((layers + 1, 2, px + 2 * cols, 3 * CUT), low),
            pltpu.VMEM((layers + 1, 2, 2, cols, CUT), low),
            pltpu.VMEM((7, 2, px + 2 * cols, CUT), low),
            pltpu.VMEM((layers, 2, px, CUT), full),
            pltpu.VMEM((3, 2, px, CUT), full),
            pltpu.VMEM((px, CUT), full),
            pltpu.VMEM((px, CUT), low),
            pltpu.VMEM((2, rows, 16, cols), full),
            pltpu.VMEM((2, rows, 40, cols), full),
            pltpu.VMEM((3, 2, px, CUT), low),
            pltpu.VMEM((10, 8, LANES), full),
            pltpu.VMEM((8, CUT), full),
            pltpu.VMEM((11, 8, CUT), full),
            pltpu.VMEM((layers, piece, 8, CUT), low),
            pltpu.VMEM((3, piece, 8, CUT), low),
            pltpu.VMEM((16, CUT), full),
            pltpu.VMEM((3, 2, px, CUT), low),
            dma((6,)), dma((6,)),
            dma((6, 2, 3)), dma((6, 2, 3)),
            dma((6, 2)), dma((6, 2)),
            dma((7, 4)), dma((7, 4)),
            dma((2, 4)), dma((2, 4)),
            dma((4,)), dma((4,)),
            dma((layers + 1, 2, 2)), dma((layers + 1, 2, 2)),
            dma((7, 2, 2)), dma((7, 2, 2)),
            dma((3,)), dma((3,)),
            dma((1,)), dma((1,)),
            dma((7, 4)), dma((7, 4)),
            dma((7, 2)), dma((7, 2)),
            dma((7, 2, 3)), dma((7, 2, 3)),
            dma((4,)), dma((4,)),
            dma((7,)), dma((7,)),
            dma((10,)), dma((10,)),
            dma((6,)), dma((6,)),
        ],
        compiler_params=pltpu.CompilerParams(
            vmem_limit_bytes=60 * 1024 * 1024, collective_id=0, has_side_effects=True
        ),
    )(features.reshape(px, channels), crop_ids, marked, lit, goals, tow, head_weights, biases)

    tower_shape = tower_weights.shape
    head_shape = head_weights.shape
    anys = pl.BlockSpec(memory_space=pl.ANY)
    smem = pl.BlockSpec(memory_space=pltpu.SMEM)
    biases_out = biases.shape[0]
    (
        o_lg, o_dl, o_fg, o_tg, o_bg, o_hg, o_tn, o_hn, o_tm, o_tv, o_hm, o_hv, o_tc, o_hc,
        o_loss, o_gb, o_gx, o_wb, o_mb, o_vb,
    ) = pl.pallas_call(
        partial(
            finish_kernel, layers=layers, rows=rows, cols=cols, cls_out=cls_out, box_out=box_out
        ),
        out_shape=(
            shape((px, cls_out), low),
            shape((box_out, rows, cols), low),
            shape((px, channels), full),
            shape((layers, shard_rows, channels), full),
            shape((layers, shard_rows, channels), full),
            shape(head_shape, full),
            shape(tower_shape, full),
            shape(head_shape, full),
            shape(tower_shape, full),
            shape(tower_shape, full),
            shape(head_shape, full),
            shape(head_shape, full),
            shape(tower_shape, low),
            shape(head_shape, low),
            shape((1,), full),
            shape((biases_out - box_out,), full),
            shape((box_out,), full),
            shape((biases_out,), full),
            shape((biases_out,), full),
            shape((biases_out,), full),
        ),
        in_specs=[smem] + [vm] * 16,
        out_specs=[anys, vm] + [anys] * 12 + [smem] + [vm] * 5,
        scratch_shapes=[
            pltpu.VMEM(tower_shape, full),
            pltpu.VMEM(tower_shape, full),
            pltpu.VMEM(tower_shape, full),
            pltpu.VMEM(tower_shape, low),
            pltpu.VMEM(head_shape, full),
            pltpu.VMEM(head_shape, full),
            pltpu.VMEM(head_shape, full),
            pltpu.VMEM(head_shape, full),
            pltpu.VMEM(head_shape, low),
            pltpu.VMEM((px, cls_out), low),
            pltpu.VMEM((rows, 40, cols), full),
            pltpu.VMEM((box_out, rows, cols), full),
            dma((layers, 6)), dma((5,)), dma((2,)),
        ],
        compiler_params=pltpu.CompilerParams(vmem_limit_bytes=60 * 1024 * 1024),
    )(
        step_count, logits, deltas, fgrad, tgrad.reshape(tower_shape), hgrad.reshape(3, shard_rows, CUT), bsum, loss,
        tower_weights, head_weights, tower_m, tower_v, head_m, head_v, biases, bias_m, bias_v,
    )
    field = (canvases, rows, cols, -1)
    return (
        o_lg.reshape(field),
        jnp.transpose(o_dl[None], (0, 2, 3, 1)),
        o_loss.reshape(()),
        o_fg.reshape(field),
        o_tg,
        o_bg,
        o_hg,
        o_gb,
        o_gx,
        o_tn,
        o_hn,
        o_wb,
        o_tm,
        o_tv,
        o_hm,
        o_hv,
        o_mb,
        o_vb,
        o_tc,
        o_hc,
    )


def solution(mesh):
    placed = (
        P("dp", "tower", None, None),
        P("dp", None),
        P("dp", "tower", None, None),
        P("dp", "tower", None, None),
        P("dp", "tower", None, None),
        P(None, None, ("dp", "tower"), None),
        P(("dp", "tower"), None),
        P(),
        P(None, None, ("dp", "tower"), None),
        P(None, None, ("dp", "tower"), None),
        P(("dp", "tower"), None),
        P(("dp", "tower"), None),
        P(),
        P(),
        P(),
    )
    fused = mesh.shape["dp"] == 8 and mesh.shape["tower"] == 4
    return jax.shard_map(
        fused_shards if fused else plain_shards,
        mesh=mesh,
        in_specs=placed,
        out_specs=(
            P("dp", "tower", None, None),
            P("dp", "tower", None, None),
            P(),
            P("dp", "tower", None, None),
            P(None, ("dp", "tower"), None),
            P(None, ("dp", "tower"), None),
            P(("dp", "tower"), None),
            P(),
            P(),
            P(None, None, ("dp", "tower"), None),
            P(("dp", "tower"), None),
            P(),
            P(None, None, ("dp", "tower"), None),
            P(None, None, ("dp", "tower"), None),
            P(("dp", "tower"), None),
            P(("dp", "tower"), None),
            P(),
            P(),
            P(None, None, ("dp", "tower"), None),
            P(("dp", "tower"), None),
        ),
        check_vma=False,
    )
```

```python
import math
from functools import partial

import jax
import jax.numpy as jnp
from jax import lax
from jax.experimental import pallas as pl
from jax.experimental.pallas import tpu as pltpu
from jax.sharding import PartitionSpec as P

beta_one = 0.9
beta_two = 0.999
adam_eps = 1e-08
learn_rate = 0.03
decay_rate = 0.05
focal_alpha = 0.25
smooth_beta = 1.0 / 9.0


def with_halo(shard, sides, width):
    for axis, dim in sides:
        size, length = (lax.axis_size(axis), shard.shape[dim])
        up = [(i, (i + 1) % size) for i in range(size - 1)]
        down = [(j, i) for i, j in up]
        last = lax.slice_in_dim(shard, length - width, length, axis=dim)
        initial = lax.slice_in_dim(shard, 0, width, axis=dim)
        before = lax.ppermute(last, axis, up)
        after = lax.ppermute(initial, axis, down)
        shard = jnp.concatenate([before, shard, after], axis=dim)
    return shard


def act_rim(values):
    return with_halo(values, (("tower", 2),), 1)


def grad_rim(values):
    return with_halo(values, (("tower", 2),), 1)


def pad_cols(values):
    return jnp.pad(values, ((0, 0), (0, 0), (0, 0), (1, 1), (0, 0)))


def silu_value(values):
    return values * jax.nn.sigmoid(values)


def silu_slope(values):
    sig = jax.nn.sigmoid(values)
    return sig * (1.0 + values * (1.0 - sig))


def conv_forward(padded, weight, out_rows, out_cols):
    stacks, canvases, channels = (padded.shape[0], padded.shape[1], padded.shape[-1])
    summed = None
    for row_off in range(3):
        for col_off in range(3):
            tap_index = row_off * 3 + col_off
            window = padded[
                :, :, row_off : row_off + out_rows, col_off : col_off + out_cols, :
            ].reshape(stacks, -1, channels)
            contrib = jnp.einsum(
                "snk,skm->snm",
                window,
                weight[:, tap_index * channels : (tap_index + 1) * channels, :],
                preferred_element_type=jnp.float32,
            )
            summed = contrib if summed is None else summed + contrib
    return summed.reshape(stacks, canvases, out_rows, out_cols, weight.shape[-1])


def conv_input_grad(grad_pad, weight, out_rows, out_cols):
    stacks, canvases, outputs = (grad_pad.shape[0], grad_pad.shape[1], grad_pad.shape[-1])
    channels = weight.shape[1] // 9
    summed = None
    for row_off in range(3):
        for col_off in range(3):
            tap_index = row_off * 3 + col_off
            window = grad_pad[
                :, :, 2 - row_off : 2 - row_off + out_rows, 2 - col_off : 2 - col_off + out_cols, :
            ].reshape(stacks, -1, outputs)
            contrib = jnp.einsum(
                "snm,skm->snk",
                window,
                weight[:, tap_index * channels : (tap_index + 1) * channels, :],
                preferred_element_type=jnp.float32,
            )
            summed = contrib if summed is None else summed + contrib
    return summed.reshape(stacks, canvases, out_rows, out_cols, channels)


def conv_weight_grad(padded, grads):
    stacks, channels = (padded.shape[0], padded.shape[-1])
    out_rows, out_cols = (grads.shape[2], grads.shape[3])
    flat_grads = grads.reshape(stacks, -1, grads.shape[-1])
    pieces = []
    for row_off in range(3):
        for col_off in range(3):
            window = padded[
                :, :, row_off : row_off + out_rows, col_off : col_off + out_cols, :
            ].reshape(stacks, -1, channels)
            pieces.append(
                jnp.einsum("snk,snm->skm", window, flat_grads, preferred_element_type=jnp.float32)
            )
    return jnp.concatenate(pieces, 1)


def adam_update(weight, grad, first, second, step_float, decay):
    first_new = beta_one * first + (1.0 - beta_one) * grad
    second_new = beta_two * second + (1.0 - beta_two) * grad * grad
    first_hat = first_new / (1.0 - jnp.power(beta_one, step_float))
    second_hat = second_new / (1.0 - jnp.power(beta_two, step_float))
    weight_new = weight - learn_rate * (
        first_hat / (jnp.sqrt(second_hat) + adam_eps) + decay * weight
    )
    return (weight_new, first_new, second_new)


def anchor_masks(label_rows, positive_rows, row_flags, classes):
    valid = (label_rows >= 0) & row_flags[:, :, None, None]
    chosen = valid & (positive_rows > 0)
    targets = (
        (label_rows[..., None] == jnp.arange(classes, dtype=jnp.int32)) & chosen[..., None]
    ).astype(jnp.float32)
    return (valid.astype(jnp.float32), chosen.astype(jnp.float32), targets)


def focal_terms(cls_vals, targets, valid_f):
    logit_view = cls_vals.reshape(targets.shape)
    prob = jax.nn.sigmoid(logit_view)
    cross = jax.nn.softplus(logit_view) - targets * logit_view
    prob_true = prob * targets + (1.0 - prob) * (1.0 - targets)
    alpha_weight = focal_alpha * targets + (1.0 - focal_alpha) * (1.0 - targets)
    return jnp.sum(alpha_weight * (1.0 - prob_true) ** 2 * cross * valid_f[..., None])


def smooth_terms(box_vals, goals, chosen_f):
    diff = box_vals.reshape(chosen_f.shape + (4,)) - goals.reshape(chosen_f.shape + (4,))
    abs_diff = jnp.abs(diff)
    smooth = jnp.where(
        abs_diff < smooth_beta, 0.5 * diff * diff / smooth_beta, abs_diff - 0.5 * smooth_beta
    )
    return jnp.sum(smooth * chosen_f[..., None])


def plain_shards(
    features,
    crop_ids,
    labels,
    positive,
    box_targets,
    tower_weights,
    head_weights,
    biases,
    tower_m,
    tower_v,
    head_m,
    head_v,
    bias_m,
    bias_v,
    step_count,
):
    canvases, row_count, col_count, channels = features.shape
    layers = tower_weights.shape[0]
    anchors = labels.shape[-1]
    head_out = head_weights.shape[1]
    box_out = 4 * anchors
    cls_out = head_out - box_out
    classes = cls_out // anchors
    shard = lax.axis_index("tower")
    tower_low, head_stack = (
        lax.all_gather(tower_weights.astype(jnp.bfloat16), ("dp", "tower"), axis=2, tiled=True),
        lax.all_gather(
            head_weights.astype(jnp.bfloat16)[None, None], ("dp", "tower"), axis=2, tiled=True
        ),
    )
    head_low = head_stack[0, 0]
    tower_bias = biases[: 2 * layers * channels].reshape(layers, 2, channels)
    head_bias = biases[2 * layers * channels :]
    cls_weight = head_low[:, :cls_out][None]
    box_weight = head_low[:, cls_out:][None]
    same_rows = crop_ids[:, 1:] == crop_ids[:, :-1]
    edge_true = jnp.ones((crop_ids.shape[0], 1), dtype=jnp.bool_)
    row_ok = jnp.concatenate([edge_true, same_rows], 1) & jnp.concatenate([same_rows, edge_true], 1)
    own_ok = lax.dynamic_slice_in_dim(row_ok, shard * row_count, row_count, 1)
    own_valid, own_chosen, own_targets = anchor_masks(labels, positive, own_ok, classes)
    count_all = lax.psum(jnp.sum(own_chosen), ("dp", "tower"))
    denom = jnp.maximum(count_all, 1.0)
    grad_scale = 1.0 / denom
    kept = []
    preact = []
    current = features[None]
    for layer in range(layers):
        padded = pad_cols(act_rim(current))
        if layer == 0:
            padded = jnp.broadcast_to(padded, (2,) + padded.shape[1:])
        kept.append(padded)
        summed = (
            conv_forward(padded, tower_low[layer], row_count, col_count)
            + tower_bias[layer][:, None, None, None, :]
        )
        preact.append(summed)
        current = silu_value(summed).astype(jnp.bfloat16)
    head_in = pad_cols(act_rim(current))
    kept.append(head_in)
    cls_raw = conv_forward(head_in[0:1], cls_weight, row_count, col_count)[0] + head_bias[:cls_out]
    box_raw = conv_forward(head_in[1:2], box_weight, row_count, col_count)[0] + head_bias[cls_out:]
    focal_value, focal_back = jax.vjp(
        partial(focal_terms, targets=own_targets, valid_f=own_valid), cls_raw
    )
    smooth_value, smooth_back = jax.vjp(
        partial(smooth_terms, goals=box_targets, chosen_f=own_chosen), box_raw
    )
    loss_local = focal_value + smooth_value
    cls_low = focal_back(grad_scale)[0].astype(jnp.bfloat16)
    box_low = smooth_back(grad_scale)[0].astype(jnp.bfloat16)
    head_wgrad = jnp.concatenate(
        [
            conv_weight_grad(head_in[0:1], cls_low[None])[0],
            conv_weight_grad(head_in[1:2], box_low[None])[0],
        ],
        1,
    )
    head_bgrad = jnp.concatenate(
        [
            jnp.sum(cls_low, axis=(0, 1, 2), dtype=jnp.float32),
            jnp.sum(box_low, axis=(0, 1, 2), dtype=jnp.float32),
        ]
    )
    joined = pad_cols(grad_rim(jnp.concatenate([cls_low, box_low], -1)[None]))
    upstream = jnp.concatenate(
        [
            conv_input_grad(joined[..., :cls_out], cls_weight, row_count, col_count),
            conv_input_grad(joined[..., cls_out:], box_weight, row_count, col_count),
        ],
        0,
    )
    tower_grads = [None] * layers
    bias_grads = [None] * layers
    for layer in reversed(range(layers)):
        grad_low = (upstream * silu_slope(preact[layer])).astype(jnp.bfloat16)
        bias_grads[layer] = jnp.sum(grad_low, axis=(1, 2, 3), dtype=jnp.float32)
        tower_grads[layer] = conv_weight_grad(kept[layer], grad_low)
        padded_grad = pad_cols(grad_rim(grad_low))
        upstream = conv_input_grad(padded_grad, tower_low[layer], row_count, col_count)
    feature_grad = upstream[0] + upstream[1]
    tower_shard, head_pair = (
        lax.psum_scatter(
            jnp.stack(tower_grads, 0), ("dp", "tower"), scatter_dimension=2, tiled=True
        ),
        lax.psum_scatter(head_wgrad[None, None], ("dp", "tower"), scatter_dimension=2, tiled=True),
    )
    head_shard = head_pair[0, 0]
    bias_local = jnp.concatenate([jnp.stack(bias_grads, 0).reshape(-1), head_bgrad])
    logits_out = cls_raw.astype(jnp.bfloat16)
    deltas_out = box_raw.astype(jnp.bfloat16)
    bias_grad, loss_total = lax.psum((bias_local, loss_local), ("dp", "tower"))
    loss = loss_total / denom
    step_float = step_count[0].astype(jnp.float32)
    tower_new, tower_m_new, tower_v_new = adam_update(
        tower_weights, tower_shard, tower_m, tower_v, step_float, decay_rate
    )
    head_new, head_m_new, head_v_new = adam_update(
        head_weights, head_shard, head_m, head_v, step_float, decay_rate
    )
    bias_new, bias_m_new, bias_v_new = adam_update(
        biases, bias_grad, bias_m, bias_v, step_float, 0.0
    )
    split_at = bias_grad.shape[0] - box_out
    return (
        logits_out,
        deltas_out,
        loss,
        feature_grad,
        tower_shard[:, 0],
        tower_shard[:, 1],
        head_shard,
        bias_grad[:split_at],
        bias_grad[split_at:],
        tower_new,
        head_new,
        bias_new,
        tower_m_new,
        tower_v_new,
        head_m_new,
        head_v_new,
        bias_m_new,
        bias_v_new,
        tower_new.astype(jnp.bfloat16),
        head_new.astype(jnp.bfloat16),
    )


MESH = pl.DeviceIdType.MESH
low = jnp.bfloat16
full = jnp.float32
LANES = 128
CUT = 256


def mega_kernel(
    feat, crops, marked, lit, goals, tow, hed, bias_all,
    logits, deltas, fgrad, tgrad, hgrad, bsum, loss_out,
    W, D, RD, RY, RZ, RX, RP, A3, HA, G, Z, U, ACC, FP, CP, GP, LS, CNT, BG, BR, TB, HB, bias, MK,
    ps, pr, zs, zr, ys, yr, ds, dr, xs, xr, fs, fr, hs, hr, gs, gr, ls, lr, es, er,
    rds, rdr, rys, ryr, rzs, rzr, rxs, rxr, rps, rpr, ns, nr, bs, br,
    *, rows, cols, layers, cls_out, box_out, anchors, piece,
):
    d = lax.axis_index("dp")
    z = lax.axis_index("tower")
    k = lax.rem(d, 2)
    x = lax.rem(d // 2, 2)
    y = d // 4
    sib = d + 1 - 2 * k
    par = d + 2 - 4 * x
    yn = d + 4 - 8 * y
    is_cls = x == 0
    is_box = x == 1
    block = 4 * piece
    px = rows * cols
    classes = cls_out // anchors

    def remote(src, dst, send, recv, dev):
        return pltpu.make_async_remote_copy(
            src_ref=src, dst_ref=dst, send_sem=send, recv_sem=recv, device_id=dev, device_id_type=MESH
        )

    def blk(yy, xx, kk):
        return pl.ds(((yy * 2 + xx) * 2 + kk) * block, block)

    def pcs(yy, xx, kk, zz):
        return pl.ds(((yy * 2 + xx) * 2 + kk) * block + zz * piece, piece)

    def zpeer(o):
        return lax.rem(z + o, 4)

    def zfrom(o):
        return lax.rem(z + 4 - o, 4)

    barrier = pltpu.get_barrier_semaphore()
    peers = [(sib, z), (par, z), (yn, z), (par, zpeer(1)), (par, zpeer(3))]
    for dev in peers + [(d, zpeer(o)) for o in (1, 2, 3)]:
        pl.semaphore_signal(barrier, inc=1, device_id=dev, device_id_type=MESH)
    pl.semaphore_wait(barrier, 8)

    def f_edge(side, across):
        src = feat.at[pl.ds((rows - 1) * cols if side == 0 else 0, cols)]
        dev = (par if across else d, zpeer(1) if side == 0 else zpeer(3))
        return remote(src, HA.at[0, side, x], hs.at[0, side, across], hr.at[0, side, across], dev)

    def f_edge_in(side, across):
        dst = HA.at[0, side, 1 - x if across else x]
        return remote(dst, dst, hs.at[0, side, across], hr.at[0, side, across], (par, zpeer(1)))

    @pl.when(z < 3)
    def _():
        for across in range(2):
            f_edge(0, across).start()

    @pl.when(z > 0)
    def _():
        for across in range(2):
            f_edge(1, across).start()

    def slot_of(step):
        odd = jnp.where(step == 1, 5, jnp.where(step == 3, 6, 3))
        return jnp.where(is_cls, step, jnp.where(lax.rem(step, 2) == 0, step // 2, odd))

    def p_send(layer):
        theirs = jnp.where(is_cls, jnp.minimum(2 * layer, 5), layer)
        return remote(
            TB.at[layer], W.at[layer, pcs(y, x, k, z)], ps.at[layer], pr.at[theirs], (par, z)
        )

    def p_head(cut, index, theirs):
        return remote(
            HB.at[cut], W.at[4 + cut, pcs(y, x, k, z)], ps.at[index], pr.at[theirs], (par, z)
        )

    def p_recv(step):
        slot = slot_of(step)
        there = W.at[slot, pcs(y, 1 - x, k, z)]
        return remote(there, there, ps.at[step], pr.at[step], (par, z))

    def z_send(step, xx, o):
        here = W.at[slot_of(step), pcs(y, xx, k, z)]
        return remote(here, here, zs.at[step, xx, o - 1], zr.at[step, xx, o - 1], (d, zpeer(o)))

    def z_recv(step, xx, o):
        here = W.at[slot_of(step), pcs(y, xx, k, zfrom(o))]
        return remote(here, here, zs.at[step, xx, o - 1], zr.at[step, xx, o - 1], (d, zpeer(o)))

    def y_copy(step, xx, yy):
        here = W.at[slot_of(step), blk(yy, xx, k)]
        return remote(here, here, ys.at[step, xx], yr.at[step, xx], (yn, z))

    def d_copy(slot, yy, xx, kk):
        here = W.at[slot, blk(yy, xx, kk)]
        return remote(here, here, ds.at[slot, yy * 2 + xx], dr.at[slot, yy * 2 + xx], (sib, z))

    def x_copy(slot, yy, xx):
        here = W.at[slot, blk(yy, xx, k)]
        return remote(here, here, xs.at[slot - 5, yy * 2 + xx], xr.at[slot - 5, yy * 2 + xx], (par, z))

    def has(step):
        return (step < 5) | (is_box & (step < 6))

    def do_z(step):
        @pl.when(has(step))
        def _():
            p_recv(step).wait_recv()
            for xx in range(2):
                for o in (2, 1, 3):
                    z_send(step, xx, o).start()

    def spread(step, yy, xx):
        slot = slot_of(step)

        @pl.when(slot >= 5)
        def _():
            x_copy(slot, yy, xx).start()

        @pl.when(slot != 5)
        def _():
            d_copy(slot, yy, xx, k).start()

    def do_y(step, lead=False):
        @pl.when(has(step))
        def _():
            for xx in range(2):
                for o in (1, 2, 3):
                    z_recv(step, xx, o).wait_recv()
                if lead:
                    if xx == 0:
                        p_recv(step + 1).wait_recv()
                    for o in (2, 1, 3):
                        z_send(step + 1, xx, o).start()
                y_copy(step, xx, y).start()
                spread(step, y, xx)

    def do_d(step):
        @pl.when(has(step))
        def _():
            for xx in range(2):
                y_copy(step, xx, 1 - y).wait_recv()
                spread(step, 1 - y, xx)

    def pump(step, carry=0):
        do_y(step)
        do_d(step - 1)

        @pl.when(step < 5)
        def _():
            do_z(step + 1)

        return carry

    def handed_over(slot):
        for b in range(4):
            x_copy(slot, b // 2, b % 2).wait_recv()
            d_copy(slot, b // 2, b % 2, k).start()

    def gathered(slot):
        for b in range(4):
            d_copy(slot, b // 2, b % 2, 1 - k).wait_recv()

    pltpu_feature = remote(feat, FP, fs.at[0], fr.at[0], (par, z))
    for step in range(layers):
        TB[step] = tow[step, 1 - x].astype(low)
        p_send(step).start()
        W[step, pcs(y, x, k, z)] = tow[step, x].astype(low)
    tail = cls_out + box_out - 2 * CUT
    HB[2] = jnp.zeros((piece, 8, CUT), low)
    for cut, width in ((2, tail), (0, CUT), (1, CUT)):
        part = hed[:, cut * CUT : cut * CUT + width].astype(low)
        HB[cut, :, :, 0:width] = part.reshape(piece, 8, width)

    @pl.when(is_cls)
    def _():
        p_head(2, 4, 3).start()
        p_head(1, 5, 1).start()
        W[4, pcs(y, x, k, z)] = HB[0]

    @pl.when(is_box)
    def _():
        p_head(0, 4, 4).start()
        W[5, pcs(y, x, k, z)] = HB[1]
        W[6, pcs(y, x, k, z)] = HB[2]

    pltpu_feature.start()
    code_copy = remote(CP.at[x], CP.at[x], fs.at[1], fr.at[1], (par, z))
    goal_copy = remote(GP.at[x], GP.at[x], fs.at[2], fr.at[2], (par, z))
    do_z(0)

    def n_copy(index, dst, dev):
        return remote(CNT.at[index], CNT.at[dst], ns.at[dst], nr.at[dst], dev)

    col = lax.broadcasted_iota(jnp.int32, (cols, CUT), 0)
    first_col = col == 0
    last_col = col == cols - 1

    def move_right(v):
        return jnp.where(first_col, 0.0, pltpu.roll(v, 1, 0))

    def move_left(v):
        return jnp.where(last_col, 0.0, pltpu.roll(v, cols - 1, 0))

    def put_row(layer, cv, row, value):
        at = pl.ds(pl.multiple_of(row * cols, cols), cols)
        A3[layer, cv, at, 0:CUT] = move_right(value).astype(low)
        A3[layer, cv, at, CUT : 2 * CUT] = value.astype(low)
        A3[layer, cv, at, 2 * CUT : 3 * CUT] = move_left(value).astype(low)

    def up_ok():
        return z > 0

    def down_ok():
        return z < 3

    def a_edge(layer, side, cv):
        row = rows if side == 0 else 1
        src = A3.at[layer, cv, pl.ds(row * cols, cols), pl.ds(CUT, CUT)]
        dev = (d, lax.rem(z + 1, 4)) if side == 0 else (d, lax.rem(z + 3, 4))
        return remote(src, HA.at[layer, side, cv], hs.at[layer, side, cv], hr.at[layer, side, cv], dev)

    def send_edges(layer, cv):
        @pl.when(down_ok())
        def _():
            a_edge(layer, 0, cv).start()

        @pl.when(up_ok())
        def _():
            a_edge(layer, 1, cv).start()

    def first_edges():
        for side, there in ((0, z > 0), (1, z < 3)):
            @pl.when(there)
            def _():
                for across in range(2):
                    f_edge_in(side, across).wait_recv()
                    cv = 1 - x if across else x
                    put_row(0, cv, 0 if side == 0 else rows + 1, HA[0, side, cv].astype(full))

    def take_edges(layer, cv):
        @pl.when(up_ok())
        def _():
            a_edge(layer, 0, cv).wait_recv()
            put_row(layer, cv, 0, HA[layer, 0, cv].astype(full))

        @pl.when(down_ok())
        def _():
            a_edge(layer, 1, cv).wait_recv()
            put_row(layer, cv, rows + 1, HA[layer, 1, cv].astype(full))

    def rim_first(body, carry, send):
        carry = lax.fori_loop(0, 2, lambda i, c: body(i * (rows - 1), c), carry)
        send()
        return lax.fori_loop(1, rows - 1, body, carry, unroll=3)

    def g_edge(slot, side, cv):
        src = G.at[slot, cv, pl.ds((rows if side == 0 else 1) * cols, cols)]
        dst = G.at[slot, cv, pl.ds(0 if side == 0 else (rows + 1) * cols, cols)]
        dev = (d, lax.rem(z + 1, 4)) if side == 0 else (d, lax.rem(z + 3, 4))
        return remote(src, dst, gs.at[slot, side, cv], gr.at[slot, side, cv], dev)

    def g_recv(slot, side, cv):
        dst = G.at[slot, cv, pl.ds(0 if side == 0 else (rows + 1) * cols, cols)]
        return remote(dst, dst, gs.at[slot, side, cv], gr.at[slot, side, cv], (d, lax.rem(z + 1, 4)))

    def send_g(slot, cv):
        @pl.when(down_ok())
        def _():
            g_edge(slot, 0, cv).start()

        @pl.when(up_ok())
        def _():
            g_edge(slot, 1, cv).start()

    def take_g(slot, cv):
        @pl.when(up_ok())
        def _():
            g_recv(slot, 0, cv).wait_recv()

        @pl.when(down_ok())
        def _():
            g_recv(slot, 1, cv).wait_recv()

    def fill(layer_src, cv):
        def body(r, carry):
            put_row(0, cv, r + 1, layer_src[pl.ds(pl.multiple_of(r * cols, cols), cols), :].astype(full))
            return carry

        lax.fori_loop(0, rows, body, 0)

    fill(feat, x)
    do_y(0, lead=True)

    r_at = lax.broadcasted_iota(jnp.int32, (rows, cols), 0)
    inside = jnp.zeros((rows, cols), jnp.int32)
    for r in range(rows):
        row = z * rows + r
        here = crops[0, row]
        above = crops[0, jnp.maximum(row - 1, 0)]
        below = crops[0, jnp.minimum(row + 1, 4 * rows - 1)]
        ok = jnp.where((here == above) & (here == below), 1, 0)
        inside = jnp.where(r_at == r, ok, inside)
    CP[x] = jnp.zeros((rows, 16, cols), full)
    picked = jnp.zeros((rows, cols), full)
    for a in range(anchors):
        label = marked[a]
        valid = (label >= 0) & (inside > 0)
        chosen = valid & (lit[a] > 0)
        mark = jnp.where(chosen, label - 200, jnp.where(valid, -100, 0)).astype(full)
        picked = picked + jnp.where(chosen, 1.0, 0.0)
        for r in range(rows):
            CP[x, r, a : a + 1, :] = mark[r : r + 1, :]
    CNT[0] = jnp.broadcast_to(jnp.sum(picked), (8, LANES))
    n_copy(0, 4, (sib, z)).start()

    code_copy.start()
    pltpu_feature.wait_recv()
    fill(FP, 1 - x)
    pump(1)
    first_edges()

    def clear(at, layer_count, slot_count):
        def a_body(layer, carry):
            for cv in range(2):
                A3[layer, cv, at, :] = jnp.zeros((cols, 3 * CUT), low)
            return carry

        def g_body(slot, carry):
            for cv in range(2):
                G[slot, cv, at, :] = jnp.zeros((cols, CUT), low)
            return carry

        lax.fori_loop(0, layer_count, a_body, 0)
        lax.fori_loop(0, slot_count, g_body, 0)

    @pl.when(z == 0)
    def _():
        clear(pl.ds(0, cols), layers + 1, layers + 3)

    @pl.when(z == 3)
    def _():
        clear(pl.ds((rows + 1) * cols, cols), layers + 1, layers + 3)

    BG[...] = jnp.zeros((8, CUT), full)
    GP[x] = jnp.zeros((rows, 40, cols), full)

    def goal_rows(q, carry):
        for r in range(rows):
            GP[x, r, pl.ds(q, 1), :] = goals[q, r : r + 1, :]
        return carry

    lax.fori_loop(0, box_out, goal_rows, 0)
    for q in range(2 * layers + 2):
        bias[q : q + 1, :] = bias_all[q * CUT : (q + 1) * CUT].reshape(1, CUT)
    q = 2 * layers + 2
    bias[q : q + 1, :] = jnp.zeros((1, CUT), full)
    bias[q : q + 1, 0:tail] = bias_all[q * CUT : q * CUT + tail].reshape(1, tail)

    U[...] = jnp.zeros(U.shape, full)

    @pl.when(is_cls)
    def _():
        goal_copy.start()

    n_copy(0, 4, (sib, z)).wait_recv()
    CNT[1] = CNT[0] + CNT[4]
    n_copy(1, 5, (yn, z)).start()

    lane_tab = lax.broadcasted_iota(jnp.int32, (16, CUT), 1)
    anchor_tab = lax.broadcasted_iota(jnp.int32, (16, CUT), 0)

    def write_marks():
        remote(CP.at[1 - x], CP.at[1 - x], fs.at[1], fr.at[1], (par, z)).wait_recv()
        spot = lane_tab - (cls_out - 2 * CUT)
        box_tab = jnp.where(
            (spot >= anchor_tab * 4) & (spot < (anchor_tab + 1) * 4) & (anchor_tab < anchors), 1.0, 0.0
        )
        tables = []
        for cut in range(3):
            channel = lane_tab + cut * CUT
            table = jnp.where(
                (channel >= anchor_tab * classes) & (channel < (anchor_tab + 1) * classes) & (channel < cls_out),
                1.0,
                0.0,
            )
            if cut == 2:
                side = x.astype(full)
                table = table * (1.0 - side) + box_tab * side
            tables.append(table.astype(low))

        def row(r, carry):
            at = pl.ds(pl.multiple_of(r * cols, cols), cols)
            for cv in range(2):
                codes = CP[cv, r].astype(low)
                for cut in range(3):
                    MK[cut, cv, at, :] = lax.dot_general(
                        codes, tables[cut], (((0,), (0,)), ((), ())), preferred_element_type=full
                    ).astype(low)
            return carry

        lax.fori_loop(0, rows, row, 0)

    def conv(layer, slot, cv):
        total = None
        for dy in range(3):
            term = jnp.dot(
                A3[layer, cv, pl.ds(dy * cols, px), :],
                W[slot, pl.ds(dy * 96, 96)].reshape(3 * CUT, CUT),
                preferred_element_type=full,
            )
            total = term if total is None else total + term
        return total

    def forward(layer, carry):
        gathered(layer)
        shift = bias[pl.ds(2 * layer + x, 1), :]

        def canvas(cv, carry):
            @pl.when(layer > 0)
            def _():
                take_edges(layer, cv)

            Z[layer, cv] = conv(layer, layer, cv)

            def row(r, carry):
                at = pl.ds(pl.multiple_of(r * cols, cols), cols)
                value = Z[layer, cv, at, :] + shift
                Z[layer, cv, at, :] = value
                put_row(layer + 1, cv, r + 1, silu_value(value))
                return carry

            rim_first(row, 0, lambda: send_edges(layer + 1, cv))
            return carry

        lax.fori_loop(0, 2, canvas, 0)
        first = jnp.where(is_cls, layer + 2, 2 * layer + 2)
        after = jnp.where(is_cls, jnp.minimum(layer + 3, 5), jnp.minimum(2 * layer + 4, 7))
        lax.fori_loop(first, after, pump, 0)

        @pl.when(layer == 0)
        def _():
            n_copy(1, 5, (yn, z)).wait_recv()
            CNT[2] = CNT[1] + CNT[5]
            n_copy(2, 6, (par, z)).start()

        @pl.when(layer == 1)
        def _():
            write_marks()
            n_copy(2, 6, (par, z)).wait_recv()
            CNT[3] = CNT[2] + CNT[6]
            for o in (1, 2, 3):
                n_copy(3, 6 + o, (d, zpeer(o))).start()

        return carry

    lax.fori_loop(0, layers, forward, 0)
    for o in (1, 2, 3):
        n_copy(3, 6 + o, (d, zpeer(o))).wait_recv()
    count = CNT[3] + CNT[7] + CNT[8] + CNT[9]
    grad_scale = (1.0 / jnp.maximum(count, 1.0))[0:1, 0:1]

    @pl.when(is_cls)
    def _():
        handed_over(5)

    for cv in range(2):
        take_edges(layers, cv)

    def rd_send(slot, b):
        src = D.at[slot, blk(b // 2, b % 2, 1 - k)]
        return remote(src, RD.at[slot, b], rds.at[slot, b], rdr.at[slot, b], (sib, z))

    def ry_send(slot, xx):
        src = D.at[slot, blk(1 - y, xx, k)]
        return remote(src, RY.at[slot, xx], rys.at[slot, xx], ryr.at[slot, xx], (yn, z))

    def rz_send(slot, xx, o):
        src = D.at[slot, pcs(y, xx, k, zpeer(o))]
        return remote(
            src, RZ.at[slot, xx, o - 1], rzs.at[slot, xx, o - 1], rzr.at[slot, xx, o - 1], (d, zpeer(o))
        )

    def rx_send(slot, b):
        src = D.at[slot, blk(b // 2, b % 2, k)]
        return remote(src, RX.at[b], rxs.at[b], rxr.at[b], (par, z))

    def add_into(slot, place, terms, own=True):
        units = block // 3

        def body(i, carry):
            here = pl.ds(place + i * units, units)
            there = pl.ds(i * units, units)
            total = D[slot, here].astype(full) if own else None
            for ref in terms:
                term = ref[there].astype(full)
                total = term if total is None else total + term
            D[slot, here] = total.astype(low)
            return carry

        lax.fori_loop(0, 3, body, 0)

    def start_of(yy, xx, kk):
        return ((yy * 2 + xx) * 2 + kk) * block

    def do_rd(slot):
        for b in range(4):
            rd_send(slot, b).start()

    def here_terms(slot, b, own, relay):
        terms = []
        if own:
            rd_send(slot, b).wait_recv()
            terms.append(RD.at[slot, b])
        if relay:
            rx_send(slot, b).wait_recv()
            terms.append(RX.at[b])
        return terms

    def do_ry(slot, own=True, relay=False, halves=(0, 1)):
        for xx in halves:
            terms = here_terms(slot, (1 - y) * 2 + xx, own, relay)
            add_into(slot, start_of(1 - y, xx, k), terms, own)
            ry_send(slot, xx).start()

    def do_rx(slot):
        for b in range(4):
            rd_send(slot, b).wait_recv()
            add_into(slot, start_of(b // 2, b % 2, k), [RD.at[slot, b]])
            rx_send(slot, b).start()

    def do_rz(slot, own=True, relay=False):
        for xx in range(2):
            terms = here_terms(slot, y * 2 + xx, own, relay)
            ry_send(slot, xx).wait_recv()
            terms.append(RY.at[slot, xx])
            add_into(slot, start_of(y, xx, k), terms, own)
            for o in (2, 1, 3):
                rz_send(slot, xx, o).start()

    def piece_sum(slot, xx):
        total = D[slot, pcs(y, xx, k, z)].astype(full)
        for o in (1, 2, 3):
            rz_send(slot, xx, o).wait_recv()
            total = total + RZ[slot, xx, o - 1].astype(full)
        return total

    def rp_send(slot, dst):
        return remote(RP.at[slot], dst, rps.at[slot], rpr.at[slot], (par, z))

    def do_rp(slot, dst_own, dst_other):
        RP[slot] = piece_sum(slot, 1 - x)
        rp_send(slot, dst_other).start()
        dst_own[...] = piece_sum(slot, x)

    def do_rp_layer(layer):
        do_rp(layer, tgrad.at[layer, x], tgrad.at[layer, x])

    def do_rp_head(slot):
        do_rp(slot, hgrad.at[slot - 4], hgrad.at[slot - 4])

    def weight_grad(layer, slot):
        for dy in range(3):
            total = None
            for cv in range(2):
                term = lax.dot_general(
                    A3[layer, cv, pl.ds(dy * cols, px), :],
                    G[slot, cv, pl.ds(cols, px), :],
                    (((0,), (0,)), ((), ())),
                    preferred_element_type=full,
                )
                total = term if total is None else total + term
            D[slot, pl.ds(dy * 96, 96)] = total.astype(low).reshape(96, 8, CUT)

    def input_grad(slot, add):
        def canvas(cv, carry):
            take_g(slot, cv)
            for dx in range(3):
                total = None
                for dy in range(3):
                    term = lax.dot_general(
                        G[slot, cv, pl.ds((2 - dy) * cols, px), :],
                        W[slot, pl.ds((3 * dy + dx) * 32, 32)].reshape(CUT, CUT),
                        (((1,), (1,)), ((), ())),
                        preferred_element_type=full,
                    )
                    total = term if total is None else total + term
                if add:
                    U[dx, cv] = U[dx, cv] + total
                else:
                    U[dx, cv] = total
            return carry

        lax.fori_loop(0, 2, canvas, 0)

    def upstream_row(cv, r):
        at = pl.ds(pl.multiple_of(r * cols, cols), cols)
        return U[1, cv, at, :] + move_left(U[0, cv, at, :]) + move_right(U[2, cv, at, :])

    def fold(value):
        return jnp.sum(value.reshape(cols // 8, 8, CUT), axis=0)

    lane = lax.broadcasted_iota(jnp.int32, (1, CUT), 1)
    box_from = cls_out - 2 * CUT

    def log_one_plus(e):
        return jnp.where(e < 0.015625, e * (1.0 + e * (e * (1.0 / 3.0) - 0.5)), jnp.log(1.0 + e))

    def cls_rows(cut, cv, shift):
        here = lane + cut * CUT
        number = here
        for a in range(1, anchors):
            number = number - jnp.where(here >= a * classes, classes, 0)
        number = number.astype(full) - 200.0

        def row(r, carry):
            b_sum, l_sum = carry
            at = pl.ds(pl.multiple_of(r * cols, cols), cols)
            raw = ACC[at, :] + shift
            LS[cut, cv, at, :] = raw.astype(low)
            marks = MK[cut, cv, at, :].astype(full)
            hit = marks == number
            seen = marks < -50.0
            s = jnp.where(hit, -raw, raw)
            e = jnp.exp(-jnp.abs(s))
            inv = pl.reciprocal(1.0 + e)
            other = e * inv
            q = jnp.where(s >= 0.0, inv, other)
            p = jnp.where(s >= 0.0, other, inv)
            soft = jnp.maximum(s, 0.0) + log_one_plus(e)
            t = jnp.where(seen, jnp.where(hit, focal_alpha, 1.0 - focal_alpha), 0.0) * q * q
            slope = t * (2.0 * p * soft + q) * grad_scale
            g = jnp.where(hit, -slope, slope).astype(low)
            G[4 + cut, cv, pl.ds(pl.multiple_of((r + 1) * cols, cols), cols), :] = g
            return b_sum + fold(g.astype(full)), l_sum + fold(t * soft)

        return row

    def box_rows(cut, cv, shift):
        goal_lane = lax.broadcasted_iota(jnp.int32, (40, LANES), 1) - (box_from - LANES)
        goal_tab = (goal_lane == lax.broadcasted_iota(jnp.int32, (40, LANES), 0)).astype(full)

        def row(r, carry):
            b_sum, l_sum = carry
            at = pl.ds(pl.multiple_of(r * cols, cols), cols)
            raw = ACC[at, :] + shift
            LS[0, cv, at, :] = raw.astype(low)
            marks = MK[cut, cv, at, :].astype(full)
            chosen = marks < -110.0
            want = lax.dot_general(
                GP[cv, r], goal_tab, (((0,), (0,)), ((), ())),
                precision=lax.Precision.HIGHEST, preferred_element_type=full,
            )
            want = jnp.concatenate([jnp.zeros((cols, LANES), full), want], axis=1)
            diff = raw - want
            size = jnp.abs(diff)
            value = jnp.where(
                size < smooth_beta, 0.5 * diff * diff / smooth_beta, size - 0.5 * smooth_beta
            )
            slope = jnp.where(
                size < smooth_beta, diff / smooth_beta, jnp.where(diff > 0.0, 1.0, -1.0)
            )
            g = jnp.where(chosen, slope * grad_scale, 0.0).astype(low)
            G[4 + cut, cv, pl.ds(pl.multiple_of((r + 1) * cols, cols), cols), :] = g
            return b_sum + fold(g.astype(full)), l_sum + fold(jnp.where(chosen, value, 0.0))

        return row

    nothing = jnp.zeros((8, CUT), full)

    def l_copy(cut):
        return remote(LS.at[cut, 1 - x], logits.at[cut], ls.at[cut], lr.at[cut], (par, z))

    def e_copy():
        return remote(LS.at[0, 1 - x], deltas, es.at[0], er.at[0], (par, z))

    @pl.when(is_box)
    def _():
        remote(GP.at[1 - x], GP.at[1 - x], fs.at[2], fr.at[2], (par, z)).wait_recv()

    def head(i, carry):
        cut = jnp.where(i == 2, 0, i + 1)
        slot = 4 + cut
        gathered(slot)
        shift = bias[pl.ds(2 * layers + cut, 1), :]

        def canvas(cv, carry):
            b_sum, l_sum = carry
            ACC[...] = conv(layers, slot, cv)
            return lax.cond(
                is_cls,
                lambda: rim_first(cls_rows(cut, cv, shift), (b_sum, l_sum), lambda: send_g(slot, cv)),
                lambda: rim_first(box_rows(cut, cv, shift), (b_sum, l_sum), lambda: send_g(slot, cv)),
            )

        b_sum, l_sum = lax.fori_loop(0, 2, canvas, (nothing, nothing))

        @pl.when(is_box)
        def _():
            e_copy().start()

        BG[pl.ds(slot, 1), :] = jnp.sum(b_sum, axis=0, keepdims=True)
        BG[pl.ds(7, 1), :] = BG[pl.ds(7, 1), :] + jnp.sum(l_sum, axis=0, keepdims=True)
        weight_grad(layers, slot)
        do_rd(slot)

        @pl.when(is_cls & (i == 2))
        def _():
            do_rz(5)

        input_grad(slot, True)

        @pl.when(is_cls & (i == 0))
        def _():
            do_d(4)
            handed_over(6)

        @pl.when(is_cls & (i == 1))
        def _():
            do_rx(6)

        @pl.when(i != 1)
        def _():
            do_ry(slot)

        return carry

    lax.fori_loop(x, 3 - x, head, 0)

    @pl.when(is_cls)
    def _():
        for cut in range(3):
            l_copy(cut).start()
            logits[cut] = LS[cut, 0]

    @pl.when(is_box)
    def _():
        deltas[...] = LS[0, 1]

    def feature_rows(cv, dst):
        def row(r, carry):
            dst[pl.ds(pl.multiple_of(r * cols, cols), cols), :] = upstream_row(cv, r).astype(dst.dtype)
            return carry

        lax.fori_loop(0, rows, row, 0)

    FS = MK.at[0, 0]
    f_copy = remote(FS, FP, fs.at[3], fr.at[3], (par, z))
    def b_copy(src, dst, dev):
        return remote(src, BR.at[dst], bs.at[dst], br.at[dst], dev)

    def backward(j, carry):
        layer = layers - 1 - j

        def canvas(cv, b_sum):
            def row(r, b_sum):
                at = pl.ds(pl.multiple_of(r * cols, cols), cols)
                g = (upstream_row(cv, r) * silu_slope(Z[layer, cv, at, :])).astype(low)
                G[layer, cv, pl.ds(pl.multiple_of((r + 1) * cols, cols), cols), :] = g
                return b_sum + fold(g.astype(full))

            return rim_first(row, b_sum, lambda: send_g(layer, cv))

        b_sum = lax.fori_loop(0, 2, canvas, nothing)
        BG[pl.ds(layer, 1), :] = jnp.sum(b_sum, axis=0, keepdims=True)
        weight_grad(layer, layer)
        do_rd(layer)

        @pl.when(j == 3)
        def _():
            b_copy(BG, 0, (sib, z)).start()

        @pl.when(is_cls | (j > 0))
        def _():
            do_rz(layer + 1)

        @pl.when(j == layers - 1)
        def _():
            do_ry(0, halves=(0,))

        input_grad(layer, False)

        @pl.when(j == layers - 1)
        def _():
            do_ry(0, halves=(1,))
            feature_rows(1 - x, FS)
            f_copy.start()

        @pl.when(j < layers - 1)
        def _():
            do_ry(layer)

        @pl.when(is_cls & (j == 0))
        def _():
            do_rp_head(5)

        @pl.when(is_cls & (j == 1))
        def _():
            do_rp_head(4)

        @pl.when(j > 1)
        def _():
            do_rp_layer(layer + 2)

        @pl.when(is_box & (j == 1))
        def _():
            do_ry(6, relay=True)

        @pl.when(is_box & (j == 2))
        def _():
            do_rz(6, relay=True)

        @pl.when(is_box & (j == 3))
        def _():
            do_rp_head(6)

        return carry

    lax.fori_loop(0, layers, backward, 0)

    b_copy(BG, 0, (sib, z)).wait_recv()
    BR[6] = BG[...] + BR[0]
    b_copy(BR.at[6], 1, (yn, z)).start()
    feature_rows(x, fgrad)
    b_copy(BR.at[6], 1, (yn, z)).wait_recv()
    total = BR[6] + BR[1]
    for zz in range(4):
        @pl.when(z == zz)
        def _():
            BR[7 + zz] = total
            for o in (1, 2, 3):
                remote(
                    BR.at[7 + zz], BR.at[7 + zz], bs.at[1 + o], br.at[1 + o], (d, zpeer(o))
                ).start()
    do_rz(0)
    do_rp_layer(1)

    for o in (1, 2, 3):
        for zz in range(4):
            @pl.when(zfrom(o) == zz)
            def _():
                remote(
                    BR.at[7 + zz], BR.at[7 + zz], bs.at[1 + o], br.at[1 + o], (d, zpeer(o))
                ).wait_recv()
    total = (BR[7] + BR[8]) + (BR[9] + BR[10])
    BR[5] = total
    last = remote(BR.at[5], bsum.at[x], bs.at[5], br.at[5], (par, z))
    last.start()
    bsum[x] = total
    f_copy.wait_recv()
    fgrad[...] = fgrad[...] + FP[...].astype(full)
    do_rp_layer(0)

    remote(BR.at[5], bsum.at[1 - x], bs.at[5], br.at[5], (par, z)).wait_recv()
    loss = jnp.sum(bsum[0, 7:8, :] + bsum[1, 7:8, :], axis=1, keepdims=True)
    loss_out[...] = jnp.broadcast_to(loss, (8, LANES)) / jnp.maximum(count, 1.0)

    for layer in range(layers):
        rp_send(layer, tgrad.at[layer, 1 - x]).wait_recv()

    @pl.when(is_cls)
    def _():
        e_copy().wait_recv()
        rp_send(6, hgrad.at[2]).wait_recv()
        for b in range(4):
            rx_send(6, b).wait_send()
            d_copy(5, b // 2, b % 2, k).wait_send()
            d_copy(6, b // 2, b % 2, k).wait_send()
        for cut in range(3):
            l_copy(cut).wait_send()
        p_head(2, 4, 3).wait_send()
        p_head(1, 5, 1).wait_send()
        goal_copy.wait_send()

    @pl.when(is_box)
    def _():
        for cut in range(2):
            rp_send(4 + cut, hgrad.at[cut]).wait_recv()
        for cut in range(3):
            l_copy(cut).wait_recv()
        for b in range(4):
            x_copy(5, b // 2, b % 2).wait_send()
            x_copy(6, b // 2, b % 2).wait_send()
            d_copy(6, b // 2, b % 2, k).wait_send()
        e_copy().wait_send()
        p_head(0, 4, 4).wait_send()

    def close_gather(step, carry):
        for xx in range(2):
            for o in (1, 2, 3):
                z_send(step, xx, o).wait_send()
            y_copy(step, xx, y).wait_send()
        return carry

    lax.fori_loop(0, 5 + x, close_gather, 0)

    def close_slot(slot, carry):
        for b in range(4):
            d_copy(slot, b // 2, b % 2, k).wait_send()

        return carry

    lax.fori_loop(0, 5 - x, close_slot, 0)

    def close_layer(layer, carry):
        @pl.when(layer < layers)
        def _():
            p_send(jnp.minimum(layer, layers - 1)).wait_send()

        @pl.when(down_ok() & (layer > 0))
        def _():
            for cv in range(2):
                a_edge(layer, 0, cv).wait_send()

        @pl.when(up_ok() & (layer > 0))
        def _():
            for cv in range(2):
                a_edge(layer, 1, cv).wait_send()

        return carry

    lax.fori_loop(0, layers + 1, close_layer, 0)

    def close_grad(slot, carry):
        @pl.when(is_cls | (slot < 4) | (slot == 6))
        def _():
            for b in range(4):
                rd_send(slot, b).wait_send()

            @pl.when(down_ok())
            def _():
                for cv in range(2):
                    g_edge(slot, 0, cv).wait_send()

            @pl.when(up_ok())
            def _():
                for cv in range(2):
                    g_edge(slot, 1, cv).wait_send()

        @pl.when((slot < 4) | (is_cls & (slot < 6)) | (is_box & (slot == 6)))
        def _():
            for xx in range(2):
                ry_send(slot, xx).wait_send()
                for o in (1, 2, 3):
                    rz_send(slot, xx, o).wait_send()
            rp_send(slot, RP.at[slot]).wait_send()

        return carry

    lax.fori_loop(0, layers + 3, close_grad, 0)
    pltpu_feature.wait_send()

    @pl.when(z < 3)
    def _():
        for across in range(2):
            f_edge(0, across).wait_send()

    @pl.when(z > 0)
    def _():
        for across in range(2):
            f_edge(1, across).wait_send()

    code_copy.wait_send()
    f_copy.wait_send()
    n_copy(0, 4, (sib, z)).wait_send()
    n_copy(1, 5, (yn, z)).wait_send()
    n_copy(2, 6, (par, z)).wait_send()
    b_copy(BG, 0, (sib, z)).wait_send()
    b_copy(BR.at[6], 1, (yn, z)).wait_send()
    for o in (1, 2, 3):
        n_copy(3, 6 + o, (d, zpeer(o))).wait_send()
        remote(BR.at[7], BR.at[7], bs.at[1 + o], br.at[1 + o], (d, zpeer(o))).wait_send()
    last.wait_send()


def finish_kernel(
    step, lg, dl, fg, tg, hg, bsum, loss_in, tw, hw, tm, tv, hm, hv, bw, bm, bv,
    o_lg, o_dl, o_fg, o_tg, o_bg, o_hg, o_tn, o_hn, o_tm, o_tv, o_hm, o_hv, o_tc, o_hc,
    o_loss, o_gb, o_gx, o_wb, o_mb, o_vb,
    TW, TM, TV, TC, HGO, HW, HM, HV, HC, LO, DT, DS, t_out, h_out, m_sem,
    *, layers, rows, cols, cls_out, box_out,
):
    tail = cls_out - 2 * CUT
    last = tail + box_out

    def t_stores(layer):
        pairs = (
            (tg.at[layer, 0], o_tg.at[layer]),
            (tg.at[layer, 1], o_bg.at[layer]),
            (TW.at[layer], o_tn.at[layer]),
            (TM.at[layer], o_tm.at[layer]),
            (TV.at[layer], o_tv.at[layer]),
            (TC.at[layer], o_tc.at[layer]),
        )
        return [pltpu.make_async_copy(a, b, t_out.at[layer, i]) for i, (a, b) in enumerate(pairs)]

    h_stores = [
        pltpu.make_async_copy(a, b, h_out.at[i])
        for i, (a, b) in enumerate(((HGO, o_hg), (HW, o_hn), (HM, o_hm), (HV, o_hv), (HC, o_hc)))
    ]
    lg_store = pltpu.make_async_copy(LO, o_lg, m_sem.at[0])
    fg_store = pltpu.make_async_copy(fg, o_fg, m_sem.at[1])
    fg_store.start()
    for cut, width in ((0, CUT), (1, CUT), (2, tail)):
        LO[:, cut * CUT : cut * CUT + width] = lg[cut][:, :width]
    lg_store.start()

    steps = jnp.broadcast_to(step[0].astype(full), (8, CUT))
    keep_one = (1.0 - jnp.exp(steps * math.log(beta_one)))[0:1, :]
    keep_two = (1.0 - jnp.exp(steps * math.log(beta_two)))[0:1, :]

    def adam(weight, grad, first, second, decay):
        one, two = keep_one[:, : grad.shape[1]], keep_two[:, : grad.shape[1]]
        first_new = beta_one * first + (1.0 - beta_one) * grad
        second_new = beta_two * second + (1.0 - beta_two) * grad * grad
        first_hat = first_new / one
        second_hat = second_new / two
        weight_new = weight - learn_rate * (
            first_hat / (jnp.sqrt(second_hat) + adam_eps) + decay * weight
        )
        return weight_new, first_new, second_new

    for layer in range(layers):
        for t in range(2):
            w_new, m_new, v_new = adam(
                tw[layer, t], tg[layer, t], tm[layer, t], tv[layer, t], decay_rate
            )
            TW[layer, t] = w_new
            TM[layer, t] = m_new
            TV[layer, t] = v_new
            TC[layer, t] = w_new.astype(low)
        for copy in t_stores(layer):
            copy.start()
    for cut, width in ((0, CUT), (1, CUT), (2, last)):
        at = slice(cut * CUT, cut * CUT + width)
        grad = hg[cut][:, :width]
        HGO[:, at] = grad
        w_new, m_new, v_new = adam(hw[:, at], grad, hm[:, at], hv[:, at], decay_rate)
        HW[:, at] = w_new
        HM[:, at] = m_new
        HV[:, at] = v_new
        HC[:, at] = w_new.astype(low)
    for copy in h_stores:
        copy.start()
    o_loss[0] = loss_in[0, 0]
    for q in range(2 * layers + 3):
        if q < 2 * layers:
            grad, width = bsum[q % 2, q // 2 : q // 2 + 1, :], CUT
        elif q < 2 * layers + 2:
            grad, width = bsum[0, q - layers : q - layers + 1, :], CUT
        else:
            lane = lax.broadcasted_iota(jnp.int32, (1, CUT), 1)
            boxes = bsum[1, 6:7, :]
            grad, width = jnp.where(lane < tail, bsum[0, 6:7, :], boxes)[:, :last], last
            o_gx[...] = pltpu.roll(boxes, CUT - tail, 1)[:, :box_out].reshape(box_out)
        at = pl.ds(q * CUT, width)
        w_new, m_new, v_new = adam(
            bw[at].reshape(1, width), grad, bm[at].reshape(1, width), bv[at].reshape(1, width), 0.0
        )
        o_wb[at] = w_new.reshape(width)
        o_mb[at] = m_new.reshape(width)
        o_vb[at] = v_new.reshape(width)
        most = min(width, cls_out + 2 * layers * CUT - q * CUT)
        o_gb[pl.ds(q * CUT, most)] = grad[:, :most].reshape(most)
    pick_lane = lax.broadcasted_iota(jnp.int32, (40, LANES), 1) - (tail - LANES)
    pick = (pick_lane == lax.broadcasted_iota(jnp.int32, (40, LANES), 0)).astype(full).astype(low)
    for r in range(rows):
        DT[r] = lax.dot_general(
            pick, dl[r * cols : (r + 1) * cols, LANES:], (((1,), (1,)), ((), ())), preferred_element_type=full
        )

    def turn(q, carry):
        for r in range(rows):
            DS[q, r : r + 1, :] = DT[r, pl.ds(q, 1), :]
        return carry

    lax.fori_loop(0, box_out, turn, 0)
    o_dl[...] = DS[...].astype(low)

    for layer in range(layers):
        for copy in t_stores(layer):
            copy.wait()
    for copy in h_stores:
        copy.wait()
    lg_store.wait()
    fg_store.wait()


def fused_shards(
    features,
    crop_ids,
    labels,
    positive,
    box_targets,
    tower_weights,
    head_weights,
    biases,
    tower_m,
    tower_v,
    head_m,
    head_v,
    bias_m,
    bias_v,
    step_count,
):
    canvases, rows, cols, channels = features.shape
    layers = tower_weights.shape[0]
    shard_rows = tower_weights.shape[2]
    anchors = labels.shape[-1]
    head_out = head_weights.shape[1]
    box_out = 4 * anchors
    cls_out = head_out - box_out
    px = rows * cols
    piece = shard_rows // 8
    tow = tower_weights.reshape(layers, 2, piece, 8, channels)
    by_anchor = (0, 3, 1, 2)
    marked = jnp.transpose(labels, by_anchor)[0]
    lit = jnp.transpose(positive, by_anchor)[0]
    goals = jnp.transpose(box_targets, by_anchor)[0]
    units = 32 * piece
    block = 4 * piece
    dma = pltpu.SemaphoreType.DMA
    vm = pl.BlockSpec(memory_space=pltpu.VMEM)
    shape = jax.ShapeDtypeStruct
    logits, deltas, fgrad, tgrad, hgrad, bsum, loss = pl.pallas_call(
        partial(
            mega_kernel,
            rows=rows, cols=cols, layers=layers, cls_out=cls_out, box_out=box_out, anchors=anchors, piece=piece,
        ),
        out_shape=(
            shape((3, px, CUT), low),
            shape((px, CUT), low),
            shape((px, CUT), full),
            shape((layers, 2, piece, 8, CUT), full),
            shape((3, piece, 8, CUT), full),
            shape((2, 8, CUT), full),
            shape((8, LANES), full),
        ),
        in_specs=[vm, pl.BlockSpec(memory_space=pltpu.SMEM)] + [vm] * 6,
        out_specs=[vm] * 7,
        scratch_shapes=[
            pltpu.VMEM((7, units, 8, CUT), low),
            pltpu.VMEM((7, units, 8, CUT), low),
            pltpu.VMEM((7, 4, block, 8, CUT), low),
            pltpu.VMEM((7, 2, block, 8, CUT), low),
            pltpu.VMEM((7, 2, 3, piece, 8, CUT), low),
            pltpu.VMEM((4, block, 8, CUT), low),
            pltpu.VMEM((7, piece, 8, CUT), full),
            pltpu.VMEM((layers + 1, 2, px + 2 * cols, 3 * CUT), low),
            pltpu.VMEM((layers + 1, 2, 2, cols, CUT), low),
            pltpu.VMEM((7, 2, px + 2 * cols, CUT), low),
            pltpu.VMEM((layers, 2, px, CUT), full),
            pltpu.VMEM((3, 2, px, CUT), full),
            pltpu.VMEM((px, CUT), full),
            pltpu.VMEM((px, CUT), low),
            pltpu.VMEM((2, rows, 16, cols), full),
            pltpu.VMEM((2, rows, 40, cols), full),
            pltpu.VMEM((3, 2, px, CUT), low),
            pltpu.VMEM((10, 8, LANES), full),
            pltpu.VMEM((8, CUT), full),
            pltpu.VMEM((11, 8, CUT), full),
            pltpu.VMEM((layers, piece, 8, CUT), low),
            pltpu.VMEM((3, piece, 8, CUT), low),
            pltpu.VMEM((16, CUT), full),
            pltpu.VMEM((3, 2, px, CUT), low),
            dma((6,)), dma((6,)),
            dma((6, 2, 3)), dma((6, 2, 3)),
            dma((6, 2)), dma((6, 2)),
            dma((7, 4)), dma((7, 4)),
            dma((2, 4)), dma((2, 4)),
            dma((4,)), dma((4,)),
            dma((layers + 1, 2, 2)), dma((layers + 1, 2, 2)),
            dma((7, 2, 2)), dma((7, 2, 2)),
            dma((3,)), dma((3,)),
            dma((1,)), dma((1,)),
            dma((7, 4)), dma((7, 4)),
            dma((7, 2)), dma((7, 2)),
            dma((7, 2, 3)), dma((7, 2, 3)),
            dma((4,)), dma((4,)),
            dma((7,)), dma((7,)),
            dma((10,)), dma((10,)),
            dma((6,)), dma((6,)),
        ],
        compiler_params=pltpu.CompilerParams(
            vmem_limit_bytes=60 * 1024 * 1024, collective_id=0, has_side_effects=True
        ),
    )(features.reshape(px, channels), crop_ids, marked, lit, goals, tow, head_weights, biases)

    tower_shape = tower_weights.shape
    head_shape = head_weights.shape
    anys = pl.BlockSpec(memory_space=pl.ANY)
    smem = pl.BlockSpec(memory_space=pltpu.SMEM)
    biases_out = biases.shape[0]
    (
        o_lg, o_dl, o_fg, o_tg, o_bg, o_hg, o_tn, o_hn, o_tm, o_tv, o_hm, o_hv, o_tc, o_hc,
        o_loss, o_gb, o_gx, o_wb, o_mb, o_vb,
    ) = pl.pallas_call(
        partial(
            finish_kernel, layers=layers, rows=rows, cols=cols, cls_out=cls_out, box_out=box_out
        ),
        out_shape=(
            shape((px, cls_out), low),
            shape((box_out, rows, cols), low),
            shape((px, channels), full),
            shape((layers, shard_rows, channels), full),
            shape((layers, shard_rows, channels), full),
            shape(head_shape, full),
            shape(tower_shape, full),
            shape(head_shape, full),
            shape(tower_shape, full),
            shape(tower_shape, full),
            shape(head_shape, full),
            shape(head_shape, full),
            shape(tower_shape, low),
            shape(head_shape, low),
            shape((1,), full),
            shape((biases_out - box_out,), full),
            shape((box_out,), full),
            shape((biases_out,), full),
            shape((biases_out,), full),
            shape((biases_out,), full),
        ),
        in_specs=[smem] + [vm] * 16,
        out_specs=[anys, vm] + [anys] * 12 + [smem] + [vm] * 5,
        scratch_shapes=[
            pltpu.VMEM(tower_shape, full),
            pltpu.VMEM(tower_shape, full),
            pltpu.VMEM(tower_shape, full),
            pltpu.VMEM(tower_shape, low),
            pltpu.VMEM(head_shape, full),
            pltpu.VMEM(head_shape, full),
            pltpu.VMEM(head_shape, full),
            pltpu.VMEM(head_shape, full),
            pltpu.VMEM(head_shape, low),
            pltpu.VMEM((px, cls_out), low),
            pltpu.VMEM((rows, 40, cols), full),
            pltpu.VMEM((box_out, rows, cols), full),
            dma((layers, 6)), dma((5,)), dma((2,)),
        ],
        compiler_params=pltpu.CompilerParams(vmem_limit_bytes=60 * 1024 * 1024),
    )(
        step_count, logits, deltas, fgrad, tgrad.reshape(tower_shape), hgrad.reshape(3, shard_rows, CUT), bsum, loss,
        tower_weights, head_weights, tower_m, tower_v, head_m, head_v, biases, bias_m, bias_v,
    )
    field = (canvases, rows, cols, -1)
    return (
        o_lg.reshape(field),
        jnp.transpose(o_dl[None], (0, 2, 3, 1)),
        o_loss.reshape(()),
        o_fg.reshape(field),
        o_tg,
        o_bg,
        o_hg,
        o_gb,
        o_gx,
        o_tn,
        o_hn,
        o_wb,
        o_tm,
        o_tv,
        o_hm,
        o_hv,
        o_mb,
        o_vb,
        o_tc,
        o_hc,
    )


def solution(mesh):
    placed = (
        P("dp", "tower", None, None),
        P("dp", None),
        P("dp", "tower", None, None),
        P("dp", "tower", None, None),
        P("dp", "tower", None, None),
        P(None, None, ("dp", "tower"), None),
        P(("dp", "tower"), None),
        P(),
        P(None, None, ("dp", "tower"), None),
        P(None, None, ("dp", "tower"), None),
        P(("dp", "tower"), None),
        P(("dp", "tower"), None),
        P(),
        P(),
        P(),
    )
    fused = mesh.shape["dp"] == 8 and mesh.shape["tower"] == 4
    return jax.shard_map(
        fused_shards if fused else plain_shards,
        mesh=mesh,
        in_specs=placed,
        out_specs=(
            P("dp", "tower", None, None),
            P("dp", "tower", None, None),
            P(),
            P("dp", "tower", None, None),
            P(None, ("dp", "tower"), None),
            P(None, ("dp", "tower"), None),
            P(("dp", "tower"), None),
            P(),
            P(),
            P(None, None, ("dp", "tower"), None),
            P(("dp", "tower"), None),
            P(),
            P(None, None, ("dp", "tower"), None),
            P(None, None, ("dp", "tower"), None),
            P(("dp", "tower"), None),
            P(("dp", "tower"), None),
            P(),
            P(),
            P(None, None, ("dp", "tower"), None),
            P(("dp", "tower"), None),
        ),
        check_vma=False,
    )
```

```python
import math
from functools import partial

import jax
import jax.numpy as jnp
from jax import lax
from jax.experimental import pallas as pl
from jax.experimental.pallas import tpu as pltpu
from jax.sharding import PartitionSpec as P

beta_one = 0.9
beta_two = 0.999
adam_eps = 1e-08
learn_rate = 0.03
decay_rate = 0.05
focal_alpha = 0.25
smooth_beta = 1.0 / 9.0


def with_halo(shard, sides, width):
    for axis, dim in sides:
        size, length = (lax.axis_size(axis), shard.shape[dim])
        up = [(i, (i + 1) % size) for i in range(size - 1)]
        down = [(j, i) for i, j in up]
        last = lax.slice_in_dim(shard, length - width, length, axis=dim)
        initial = lax.slice_in_dim(shard, 0, width, axis=dim)
        before = lax.ppermute(last, axis, up)
        after = lax.ppermute(initial, axis, down)
        shard = jnp.concatenate([before, shard, after], axis=dim)
    return shard


def act_rim(values):
    return with_halo(values, (("tower", 2),), 1)


def grad_rim(values):
    return with_halo(values, (("tower", 2),), 1)


def pad_cols(values):
    return jnp.pad(values, ((0, 0), (0, 0), (0, 0), (1, 1), (0, 0)))


def silu_value(values):
    return values * jax.nn.sigmoid(values)


def silu_slope(values):
    sig = jax.nn.sigmoid(values)
    return sig * (1.0 + values * (1.0 - sig))


def conv_forward(padded, weight, out_rows, out_cols):
    stacks, canvases, channels = (padded.shape[0], padded.shape[1], padded.shape[-1])
    summed = None
    for row_off in range(3):
        for col_off in range(3):
            tap_index = row_off * 3 + col_off
            window = padded[
                :, :, row_off : row_off + out_rows, col_off : col_off + out_cols, :
            ].reshape(stacks, -1, channels)
            contrib = jnp.einsum(
                "snk,skm->snm",
                window,
                weight[:, tap_index * channels : (tap_index + 1) * channels, :],
                preferred_element_type=jnp.float32,
            )
            summed = contrib if summed is None else summed + contrib
    return summed.reshape(stacks, canvases, out_rows, out_cols, weight.shape[-1])


def conv_input_grad(grad_pad, weight, out_rows, out_cols):
    stacks, canvases, outputs = (grad_pad.shape[0], grad_pad.shape[1], grad_pad.shape[-1])
    channels = weight.shape[1] // 9
    summed = None
    for row_off in range(3):
        for col_off in range(3):
            tap_index = row_off * 3 + col_off
            window = grad_pad[
                :, :, 2 - row_off : 2 - row_off + out_rows, 2 - col_off : 2 - col_off + out_cols, :
            ].reshape(stacks, -1, outputs)
            contrib = jnp.einsum(
                "snm,skm->snk",
                window,
                weight[:, tap_index * channels : (tap_index + 1) * channels, :],
                preferred_element_type=jnp.float32,
            )
            summed = contrib if summed is None else summed + contrib
    return summed.reshape(stacks, canvases, out_rows, out_cols, channels)


def conv_weight_grad(padded, grads):
    stacks, channels = (padded.shape[0], padded.shape[-1])
    out_rows, out_cols = (grads.shape[2], grads.shape[3])
    flat_grads = grads.reshape(stacks, -1, grads.shape[-1])
    pieces = []
    for row_off in range(3):
        for col_off in range(3):
            window = padded[
                :, :, row_off : row_off + out_rows, col_off : col_off + out_cols, :
            ].reshape(stacks, -1, channels)
            pieces.append(
                jnp.einsum("snk,snm->skm", window, flat_grads, preferred_element_type=jnp.float32)
            )
    return jnp.concatenate(pieces, 1)


def adam_update(weight, grad, first, second, step_float, decay):
    first_new = beta_one * first + (1.0 - beta_one) * grad
    second_new = beta_two * second + (1.0 - beta_two) * grad * grad
    first_hat = first_new / (1.0 - jnp.power(beta_one, step_float))
    second_hat = second_new / (1.0 - jnp.power(beta_two, step_float))
    weight_new = weight - learn_rate * (
        first_hat / (jnp.sqrt(second_hat) + adam_eps) + decay * weight
    )
    return (weight_new, first_new, second_new)


def anchor_masks(label_rows, positive_rows, row_flags, classes):
    valid = (label_rows >= 0) & row_flags[:, :, None, None]
    chosen = valid & (positive_rows > 0)
    targets = (
        (label_rows[..., None] == jnp.arange(classes, dtype=jnp.int32)) & chosen[..., None]
    ).astype(jnp.float32)
    return (valid.astype(jnp.float32), chosen.astype(jnp.float32), targets)


def focal_terms(cls_vals, targets, valid_f):
    logit_view = cls_vals.reshape(targets.shape)
    prob = jax.nn.sigmoid(logit_view)
    cross = jax.nn.softplus(logit_view) - targets * logit_view
    prob_true = prob * targets + (1.0 - prob) * (1.0 - targets)
    alpha_weight = focal_alpha * targets + (1.0 - focal_alpha) * (1.0 - targets)
    return jnp.sum(alpha_weight * (1.0 - prob_true) ** 2 * cross * valid_f[..., None])


def smooth_terms(box_vals, goals, chosen_f):
    diff = box_vals.reshape(chosen_f.shape + (4,)) - goals.reshape(chosen_f.shape + (4,))
    abs_diff = jnp.abs(diff)
    smooth = jnp.where(
        abs_diff < smooth_beta, 0.5 * diff * diff / smooth_beta, abs_diff - 0.5 * smooth_beta
    )
    return jnp.sum(smooth * chosen_f[..., None])


def plain_shards(
    features,
    crop_ids,
    labels,
    positive,
    box_targets,
    tower_weights,
    head_weights,
    biases,
    tower_m,
    tower_v,
    head_m,
    head_v,
    bias_m,
    bias_v,
    step_count,
):
    canvases, row_count, col_count, channels = features.shape
    layers = tower_weights.shape[0]
    anchors = labels.shape[-1]
    head_out = head_weights.shape[1]
    box_out = 4 * anchors
    cls_out = head_out - box_out
    classes = cls_out // anchors
    shard = lax.axis_index("tower")
    tower_low, head_stack = (
        lax.all_gather(tower_weights.astype(jnp.bfloat16), ("dp", "tower"), axis=2, tiled=True),
        lax.all_gather(
            head_weights.astype(jnp.bfloat16)[None, None], ("dp", "tower"), axis=2, tiled=True
        ),
    )
    head_low = head_stack[0, 0]
    tower_bias = biases[: 2 * layers * channels].reshape(layers, 2, channels)
    head_bias = biases[2 * layers * channels :]
    cls_weight = head_low[:, :cls_out][None]
    box_weight = head_low[:, cls_out:][None]
    same_rows = crop_ids[:, 1:] == crop_ids[:, :-1]
    edge_true = jnp.ones((crop_ids.shape[0], 1), dtype=jnp.bool_)
    row_ok = jnp.concatenate([edge_true, same_rows], 1) & jnp.concatenate([same_rows, edge_true], 1)
    own_ok = lax.dynamic_slice_in_dim(row_ok, shard * row_count, row_count, 1)
    own_valid, own_chosen, own_targets = anchor_masks(labels, positive, own_ok, classes)
    count_all = lax.psum(jnp.sum(own_chosen), ("dp", "tower"))
    denom = jnp.maximum(count_all, 1.0)
    grad_scale = 1.0 / denom
    kept = []
    preact = []
    current = features[None]
    for layer in range(layers):
        padded = pad_cols(act_rim(current))
        if layer == 0:
            padded = jnp.broadcast_to(padded, (2,) + padded.shape[1:])
        kept.append(padded)
        summed = (
            conv_forward(padded, tower_low[layer], row_count, col_count)
            + tower_bias[layer][:, None, None, None, :]
        )
        preact.append(summed)
        current = silu_value(summed).astype(jnp.bfloat16)
    head_in = pad_cols(act_rim(current))
    kept.append(head_in)
    cls_raw = conv_forward(head_in[0:1], cls_weight, row_count, col_count)[0] + head_bias[:cls_out]
    box_raw = conv_forward(head_in[1:2], box_weight, row_count, col_count)[0] + head_bias[cls_out:]
    focal_value, focal_back = jax.vjp(
        partial(focal_terms, targets=own_targets, valid_f=own_valid), cls_raw
    )
    smooth_value, smooth_back = jax.vjp(
        partial(smooth_terms, goals=box_targets, chosen_f=own_chosen), box_raw
    )
    loss_local = focal_value + smooth_value
    cls_low = focal_back(grad_scale)[0].astype(jnp.bfloat16)
    box_low = smooth_back(grad_scale)[0].astype(jnp.bfloat16)
    head_wgrad = jnp.concatenate(
        [
            conv_weight_grad(head_in[0:1], cls_low[None])[0],
            conv_weight_grad(head_in[1:2], box_low[None])[0],
        ],
        1,
    )
    head_bgrad = jnp.concatenate(
        [
            jnp.sum(cls_low, axis=(0, 1, 2), dtype=jnp.float32),
            jnp.sum(box_low, axis=(0, 1, 2), dtype=jnp.float32),
        ]
    )
    joined = pad_cols(grad_rim(jnp.concatenate([cls_low, box_low], -1)[None]))
    upstream = jnp.concatenate(
        [
            conv_input_grad(joined[..., :cls_out], cls_weight, row_count, col_count),
            conv_input_grad(joined[..., cls_out:], box_weight, row_count, col_count),
        ],
        0,
    )
    tower_grads = [None] * layers
    bias_grads = [None] * layers
    for layer in reversed(range(layers)):
        grad_low = (upstream * silu_slope(preact[layer])).astype(jnp.bfloat16)
        bias_grads[layer] = jnp.sum(grad_low, axis=(1, 2, 3), dtype=jnp.float32)
        tower_grads[layer] = conv_weight_grad(kept[layer], grad_low)
        padded_grad = pad_cols(grad_rim(grad_low))
        upstream = conv_input_grad(padded_grad, tower_low[layer], row_count, col_count)
    feature_grad = upstream[0] + upstream[1]
    tower_shard, head_pair = (
        lax.psum_scatter(
            jnp.stack(tower_grads, 0), ("dp", "tower"), scatter_dimension=2, tiled=True
        ),
        lax.psum_scatter(head_wgrad[None, None], ("dp", "tower"), scatter_dimension=2, tiled=True),
    )
    head_shard = head_pair[0, 0]
    bias_local = jnp.concatenate([jnp.stack(bias_grads, 0).reshape(-1), head_bgrad])
    logits_out = cls_raw.astype(jnp.bfloat16)
    deltas_out = box_raw.astype(jnp.bfloat16)
    bias_grad, loss_total = lax.psum((bias_local, loss_local), ("dp", "tower"))
    loss = loss_total / denom
    step_float = step_count[0].astype(jnp.float32)
    tower_new, tower_m_new, tower_v_new = adam_update(
        tower_weights, tower_shard, tower_m, tower_v, step_float, decay_rate
    )
    head_new, head_m_new, head_v_new = adam_update(
        head_weights, head_shard, head_m, head_v, step_float, decay_rate
    )
    bias_new, bias_m_new, bias_v_new = adam_update(
        biases, bias_grad, bias_m, bias_v, step_float, 0.0
    )
    split_at = bias_grad.shape[0] - box_out
    return (
        logits_out,
        deltas_out,
        loss,
        feature_grad,
        tower_shard[:, 0],
        tower_shard[:, 1],
        head_shard,
        bias_grad[:split_at],
        bias_grad[split_at:],
        tower_new,
        head_new,
        bias_new,
        tower_m_new,
        tower_v_new,
        head_m_new,
        head_v_new,
        bias_m_new,
        bias_v_new,
        tower_new.astype(jnp.bfloat16),
        head_new.astype(jnp.bfloat16),
    )


MESH = pl.DeviceIdType.MESH
low = jnp.bfloat16
full = jnp.float32
LANES = 128
CUT = 256


def mega_kernel(
    feat, crops, marked, lit, goals, tow, hed, bias_all,
    logits, deltas, fgrad, tgrad, hgrad, bsum, loss_out,
    W, D, RD, RY, RZ, RX, RP, A3, HA, G, Z, U, ACC, FP, CP, GP, LS, CNT, BG, BR, TB, HB, bias, MK,
    ps, pr, zs, zr, ys, yr, ds, dr, xs, xr, fs, fr, hs, hr, gs, gr, ls, lr, es, er,
    rds, rdr, rys, ryr, rzs, rzr, rxs, rxr, rps, rpr, ns, nr, bs, br,
    *, rows, cols, layers, cls_out, box_out, anchors, piece,
):
    d = lax.axis_index("dp")
    z = lax.axis_index("tower")
    k = lax.rem(d, 2)
    x = lax.rem(d // 2, 2)
    y = d // 4
    sib = d + 1 - 2 * k
    par = d + 2 - 4 * x
    yn = d + 4 - 8 * y
    is_cls = x == 0
    is_box = x == 1
    block = 4 * piece
    px = rows * cols
    classes = cls_out // anchors

    def remote(src, dst, send, recv, dev):
        return pltpu.make_async_remote_copy(
            src_ref=src, dst_ref=dst, send_sem=send, recv_sem=recv, device_id=dev, device_id_type=MESH
        )

    def blk(yy, xx, kk):
        return pl.ds(((yy * 2 + xx) * 2 + kk) * block, block)

    def pcs(yy, xx, kk, zz):
        return pl.ds(((yy * 2 + xx) * 2 + kk) * block + zz * piece, piece)

    def zpeer(o):
        return lax.rem(z + o, 4)

    def zfrom(o):
        return lax.rem(z + 4 - o, 4)

    barrier = pltpu.get_barrier_semaphore()
    peers = [(sib, z), (par, z), (yn, z), (par, zpeer(1)), (par, zpeer(3))]
    for dev in peers + [(d, zpeer(o)) for o in (1, 2, 3)]:
        pl.semaphore_signal(barrier, inc=1, device_id=dev, device_id_type=MESH)
    pl.semaphore_wait(barrier, 8)

    def f_edge(side, across):
        src = feat.at[pl.ds((rows - 1) * cols if side == 0 else 0, cols)]
        dev = (par if across else d, zpeer(1) if side == 0 else zpeer(3))
        return remote(src, HA.at[0, side, x], hs.at[0, side, across], hr.at[0, side, across], dev)

    def f_edge_in(side, across):
        dst = HA.at[0, side, 1 - x if across else x]
        return remote(dst, dst, hs.at[0, side, across], hr.at[0, side, across], (par, zpeer(1)))

    @pl.when(z < 3)
    def _():
        for across in range(2):
            f_edge(0, across).start()

    @pl.when(z > 0)
    def _():
        for across in range(2):
            f_edge(1, across).start()

    def slot_of(step):
        odd = jnp.where(step == 1, 5, jnp.where(step == 3, 6, 3))
        return jnp.where(is_cls, step, jnp.where(lax.rem(step, 2) == 0, step // 2, odd))

    def p_send(layer):
        theirs = jnp.where(is_cls, jnp.minimum(2 * layer, 5), layer)
        return remote(
            TB.at[layer], W.at[layer, pcs(y, x, k, z)], ps.at[layer], pr.at[theirs], (par, z)
        )

    def p_head(cut, index, theirs):
        return remote(
            HB.at[cut], W.at[4 + cut, pcs(y, x, k, z)], ps.at[index], pr.at[theirs], (par, z)
        )

    def p_recv(step):
        slot = slot_of(step)
        there = W.at[slot, pcs(y, 1 - x, k, z)]
        return remote(there, there, ps.at[step], pr.at[step], (par, z))

    def z_send(step, xx, o):
        here = W.at[slot_of(step), pcs(y, xx, k, z)]
        return remote(here, here, zs.at[step, xx, o - 1], zr.at[step, xx, o - 1], (d, zpeer(o)))

    def z_recv(step, xx, o):
        here = W.at[slot_of(step), pcs(y, xx, k, zfrom(o))]
        return remote(here, here, zs.at[step, xx, o - 1], zr.at[step, xx, o - 1], (d, zpeer(o)))

    def y_copy(step, xx, yy):
        here = W.at[slot_of(step), blk(yy, xx, k)]
        return remote(here, here, ys.at[step, xx], yr.at[step, xx], (yn, z))

    def d_copy(slot, yy, xx, kk):
        here = W.at[slot, blk(yy, xx, kk)]
        return remote(here, here, ds.at[slot, yy * 2 + xx], dr.at[slot, yy * 2 + xx], (sib, z))

    def x_copy(slot, yy, xx):
        here = W.at[slot, blk(yy, xx, k)]
        return remote(here, here, xs.at[slot - 5, yy * 2 + xx], xr.at[slot - 5, yy * 2 + xx], (par, z))

    def has(step):
        return (step < 5) | (is_box & (step < 6))

    def do_z(step):
        @pl.when(has(step))
        def _():
            p_recv(step).wait_recv()
            for xx in range(2):
                for o in (2, 1, 3):
                    z_send(step, xx, o).start()

    def spread(step, yy, xx):
        slot = slot_of(step)

        @pl.when(slot >= 5)
        def _():
            x_copy(slot, yy, xx).start()

        @pl.when(slot != 5)
        def _():
            d_copy(slot, yy, xx, k).start()

    def do_y(step, lead=False):
        @pl.when(has(step))
        def _():
            for xx in range(2):
                for o in (1, 2, 3):
                    z_recv(step, xx, o).wait_recv()
                if lead:
                    if xx == 0:
                        p_recv(step + 1).wait_recv()
                    for o in (2, 1, 3):
                        z_send(step + 1, xx, o).start()
                y_copy(step, xx, y).start()
                spread(step, y, xx)

    def do_d(step):
        @pl.when(has(step))
        def _():
            for xx in range(2):
                y_copy(step, xx, 1 - y).wait_recv()
                spread(step, 1 - y, xx)

    def pump(step, carry=0):
        do_y(step)
        do_d(step - 1)

        @pl.when(step < 5)
        def _():
            do_z(step + 1)

        return carry

    def handed_over(slot):
        for b in range(4):
            x_copy(slot, b // 2, b % 2).wait_recv()
            d_copy(slot, b // 2, b % 2, k).start()

    def gathered(slot):
        for b in range(4):
            d_copy(slot, b // 2, b % 2, 1 - k).wait_recv()

    pltpu_feature = remote(feat, FP, fs.at[0], fr.at[0], (par, z))
    for step in range(layers):
        TB[step] = tow[step, 1 - x].astype(low)
        p_send(step).start()
        W[step, pcs(y, x, k, z)] = tow[step, x].astype(low)
    tail = cls_out + box_out - 2 * CUT
    HB[2] = jnp.zeros((piece, 8, CUT), low)
    for cut, width in ((2, tail), (0, CUT), (1, CUT)):
        part = hed[:, cut * CUT : cut * CUT + width].astype(low)
        HB[cut, :, :, 0:width] = part.reshape(piece, 8, width)

    @pl.when(is_cls)
    def _():
        p_head(2, 4, 3).start()
        p_head(1, 5, 1).start()
        W[4, pcs(y, x, k, z)] = HB[0]

    @pl.when(is_box)
    def _():
        p_head(0, 4, 4).start()
        W[5, pcs(y, x, k, z)] = HB[1]
        W[6, pcs(y, x, k, z)] = HB[2]

    pltpu_feature.start()
    code_copy = remote(CP.at[x], CP.at[x], fs.at[1], fr.at[1], (par, z))
    goal_copy = remote(GP.at[x], GP.at[x], fs.at[2], fr.at[2], (par, z))
    do_z(0)

    def n_copy(index, dst, dev):
        return remote(CNT.at[index], CNT.at[dst], ns.at[dst], nr.at[dst], dev)

    col = lax.broadcasted_iota(jnp.int32, (cols, CUT), 0)
    first_col = col == 0
    last_col = col == cols - 1

    def move_right(v):
        return jnp.where(first_col, 0.0, pltpu.roll(v, 1, 0))

    def move_left(v):
        return jnp.where(last_col, 0.0, pltpu.roll(v, cols - 1, 0))

    def put_row(layer, cv, row, value):
        at = pl.ds(pl.multiple_of(row * cols, cols), cols)
        A3[layer, cv, at, 0:CUT] = move_right(value).astype(low)
        A3[layer, cv, at, CUT : 2 * CUT] = value.astype(low)
        A3[layer, cv, at, 2 * CUT : 3 * CUT] = move_left(value).astype(low)

    def up_ok():
        return z > 0

    def down_ok():
        return z < 3

    def a_edge(layer, side, cv):
        row = rows if side == 0 else 1
        src = A3.at[layer, cv, pl.ds(row * cols, cols), pl.ds(CUT, CUT)]
        dev = (d, lax.rem(z + 1, 4)) if side == 0 else (d, lax.rem(z + 3, 4))
        return remote(src, HA.at[layer, side, cv], hs.at[layer, side, cv], hr.at[layer, side, cv], dev)

    def send_edges(layer, cv):
        @pl.when(down_ok())
        def _():
            a_edge(layer, 0, cv).start()

        @pl.when(up_ok())
        def _():
            a_edge(layer, 1, cv).start()

    def first_edges():
        for side, there in ((0, z > 0), (1, z < 3)):
            @pl.when(there)
            def _():
                for across in range(2):
                    f_edge_in(side, across).wait_recv()
                    cv = 1 - x if across else x
                    put_row(0, cv, 0 if side == 0 else rows + 1, HA[0, side, cv].astype(full))

    def take_edges(layer, cv):
        @pl.when(up_ok())
        def _():
            a_edge(layer, 0, cv).wait_recv()
            put_row(layer, cv, 0, HA[layer, 0, cv].astype(full))

        @pl.when(down_ok())
        def _():
            a_edge(layer, 1, cv).wait_recv()
            put_row(layer, cv, rows + 1, HA[layer, 1, cv].astype(full))

    def rim_first(body, carry, send):
        carry = lax.fori_loop(0, 2, lambda i, c: body(i * (rows - 1), c), carry)
        send()
        return lax.fori_loop(1, rows - 1, body, carry, unroll=3)

    def g_edge(slot, side, cv):
        src = G.at[slot, cv, pl.ds((rows if side == 0 else 1) * cols, cols)]
        dst = G.at[slot, cv, pl.ds(0 if side == 0 else (rows + 1) * cols, cols)]
        dev = (d, lax.rem(z + 1, 4)) if side == 0 else (d, lax.rem(z + 3, 4))
        return remote(src, dst, gs.at[slot, side, cv], gr.at[slot, side, cv], dev)

    def g_recv(slot, side, cv):
        dst = G.at[slot, cv, pl.ds(0 if side == 0 else (rows + 1) * cols, cols)]
        return remote(dst, dst, gs.at[slot, side, cv], gr.at[slot, side, cv], (d, lax.rem(z + 1, 4)))

    def send_g(slot, cv):
        @pl.when(down_ok())
        def _():
            g_edge(slot, 0, cv).start()

        @pl.when(up_ok())
        def _():
            g_edge(slot, 1, cv).start()

    def take_g(slot, cv):
        @pl.when(up_ok())
        def _():
            g_recv(slot, 0, cv).wait_recv()

        @pl.when(down_ok())
        def _():
            g_recv(slot, 1, cv).wait_recv()

    def fill(layer_src, cv):
        def body(r, carry):
            put_row(0, cv, r + 1, layer_src[pl.ds(pl.multiple_of(r * cols, cols), cols), :].astype(full))
            return carry

        lax.fori_loop(0, rows, body, 0)

    fill(feat, x)
    do_y(0, lead=True)

    r_at = lax.broadcasted_iota(jnp.int32, (rows, cols), 0)
    inside = jnp.zeros((rows, cols), jnp.int32)
    for r in range(rows):
        row = z * rows + r
        here = crops[0, row]
        above = crops[0, jnp.maximum(row - 1, 0)]
        below = crops[0, jnp.minimum(row + 1, 4 * rows - 1)]
        ok = jnp.where((here == above) & (here == below), 1, 0)
        inside = jnp.where(r_at == r, ok, inside)
    CP[x] = jnp.zeros((rows, 16, cols), full)
    picked = jnp.zeros((rows, cols), full)
    for a in range(anchors):
        label = marked[a]
        valid = (label >= 0) & (inside > 0)
        chosen = valid & (lit[a] > 0)
        mark = jnp.where(chosen, label - 200, jnp.where(valid, -100, 0)).astype(full)
        picked = picked + jnp.where(chosen, 1.0, 0.0)
        for r in range(rows):
            CP[x, r, a : a + 1, :] = mark[r : r + 1, :]
    CNT[0] = jnp.broadcast_to(jnp.sum(picked), (8, LANES))
    n_copy(0, 4, (sib, z)).start()

    code_copy.start()
    pltpu_feature.wait_recv()
    fill(FP, 1 - x)
    pump(1)
    first_edges()

    def clear(at, layer_count, slot_count):
        def a_body(layer, carry):
            for cv in range(2):
                A3[layer, cv, at, :] = jnp.zeros((cols, 3 * CUT), low)
            return carry

        def g_body(slot, carry):
            for cv in range(2):
                G[slot, cv, at, :] = jnp.zeros((cols, CUT), low)
            return carry

        lax.fori_loop(0, layer_count, a_body, 0)
        lax.fori_loop(0, slot_count, g_body, 0)

    @pl.when(z == 0)
    def _():
        clear(pl.ds(0, cols), layers + 1, layers + 3)

    @pl.when(z == 3)
    def _():
        clear(pl.ds((rows + 1) * cols, cols), layers + 1, layers + 3)

    BG[...] = jnp.zeros((8, CUT), full)
    GP[x] = jnp.zeros((rows, 40, cols), full)

    def goal_rows(q, carry):
        for r in range(rows):
            GP[x, r, pl.ds(q, 1), :] = goals[q, r : r + 1, :]
        return carry

    lax.fori_loop(0, box_out, goal_rows, 0)
    for q in range(2 * layers + 2):
        bias[q : q + 1, :] = bias_all[q * CUT : (q + 1) * CUT].reshape(1, CUT)
    q = 2 * layers + 2
    bias[q : q + 1, :] = jnp.zeros((1, CUT), full)
    bias[q : q + 1, 0:tail] = bias_all[q * CUT : q * CUT + tail].reshape(1, tail)

    U[...] = jnp.zeros(U.shape, full)

    @pl.when(is_cls)
    def _():
        goal_copy.start()

    n_copy(0, 4, (sib, z)).wait_recv()
    CNT[1] = CNT[0] + CNT[4]
    n_copy(1, 5, (yn, z)).start()

    lane_tab = lax.broadcasted_iota(jnp.int32, (16, CUT), 1)
    anchor_tab = lax.broadcasted_iota(jnp.int32, (16, CUT), 0)

    def write_marks():
        remote(CP.at[1 - x], CP.at[1 - x], fs.at[1], fr.at[1], (par, z)).wait_recv()
        spot = lane_tab - (cls_out - 2 * CUT)
        box_tab = jnp.where(
            (spot >= anchor_tab * 4) & (spot < (anchor_tab + 1) * 4) & (anchor_tab < anchors), 1.0, 0.0
        )
        tables = []
        for cut in range(3):
            channel = lane_tab + cut * CUT
            table = jnp.where(
                (channel >= anchor_tab * classes) & (channel < (anchor_tab + 1) * classes) & (channel < cls_out),
                1.0,
                0.0,
            )
            if cut == 2:
                side = x.astype(full)
                table = table * (1.0 - side) + box_tab * side
            tables.append(table.astype(low))

        def row(r, carry):
            at = pl.ds(pl.multiple_of(r * cols, cols), cols)
            for cv in range(2):
                codes = CP[cv, r].astype(low)
                for cut in range(3):
                    MK[cut, cv, at, :] = lax.dot_general(
                        codes, tables[cut], (((0,), (0,)), ((), ())), preferred_element_type=full
                    ).astype(low)
            return carry

        lax.fori_loop(0, rows, row, 0)

    def conv(layer, slot, cv):
        total = None
        for dy in range(3):
            term = jnp.dot(
                A3[layer, cv, pl.ds(dy * cols, px), :],
                W[slot, pl.ds(dy * 96, 96)].reshape(3 * CUT, CUT),
                preferred_element_type=full,
            )
            total = term if total is None else total + term
        return total

    def forward(layer, carry):
        gathered(layer)
        shift = bias[pl.ds(2 * layer + x, 1), :]

        def canvas(cv, carry):
            @pl.when(layer > 0)
            def _():
                take_edges(layer, cv)

            Z[layer, cv] = conv(layer, layer, cv)

            def row(r, carry):
                at = pl.ds(pl.multiple_of(r * cols, cols), cols)
                value = Z[layer, cv, at, :] + shift
                Z[layer, cv, at, :] = value
                put_row(layer + 1, cv, r + 1, silu_value(value))
                return carry

            rim_first(row, 0, lambda: send_edges(layer + 1, cv))
            return carry

        lax.fori_loop(0, 2, canvas, 0)
        first = jnp.where(is_cls, layer + 2, 2 * layer + 2)
        after = jnp.where(is_cls, jnp.minimum(layer + 3, 5), jnp.minimum(2 * layer + 4, 7))
        lax.fori_loop(first, after, pump, 0)

        @pl.when(layer == 0)
        def _():
            n_copy(1, 5, (yn, z)).wait_recv()
            CNT[2] = CNT[1] + CNT[5]
            n_copy(2, 6, (par, z)).start()

        @pl.when(layer == 1)
        def _():
            write_marks()
            n_copy(2, 6, (par, z)).wait_recv()
            CNT[3] = CNT[2] + CNT[6]
            for o in (1, 2, 3):
                n_copy(3, 6 + o, (d, zpeer(o))).start()

        return carry

    lax.fori_loop(0, layers, forward, 0)
    for o in (1, 2, 3):
        n_copy(3, 6 + o, (d, zpeer(o))).wait_recv()
    count = CNT[3] + CNT[7] + CNT[8] + CNT[9]
    grad_scale = (1.0 / jnp.maximum(count, 1.0))[0:1, 0:1]

    @pl.when(is_cls)
    def _():
        handed_over(5)

    for cv in range(2):
        take_edges(layers, cv)

    def rd_send(slot, b):
        src = D.at[slot, blk(b // 2, b % 2, 1 - k)]
        return remote(src, RD.at[slot, b], rds.at[slot, b], rdr.at[slot, b], (sib, z))

    def ry_send(slot, xx):
        src = D.at[slot, blk(1 - y, xx, k)]
        return remote(src, RY.at[slot, xx], rys.at[slot, xx], ryr.at[slot, xx], (yn, z))

    def rz_send(slot, xx, o):
        src = D.at[slot, pcs(y, xx, k, zpeer(o))]
        return remote(
            src, RZ.at[slot, xx, o - 1], rzs.at[slot, xx, o - 1], rzr.at[slot, xx, o - 1], (d, zpeer(o))
        )

    def rx_send(slot, b):
        src = D.at[slot, blk(b // 2, b % 2, k)]
        return remote(src, RX.at[b], rxs.at[b], rxr.at[b], (par, z))

    def add_into(slot, place, terms, own=True):
        units = block // 3

        def body(i, carry):
            here = pl.ds(place + i * units, units)
            there = pl.ds(i * units, units)
            total = D[slot, here].astype(full) if own else None
            for ref in terms:
                term = ref[there].astype(full)
                total = term if total is None else total + term
            D[slot, here] = total.astype(low)
            return carry

        lax.fori_loop(0, 3, body, 0)

    def start_of(yy, xx, kk):
        return ((yy * 2 + xx) * 2 + kk) * block

    def do_rd(slot):
        for b in range(4):
            rd_send(slot, b).start()

    def here_terms(slot, b, own, relay):
        terms = []
        if own:
            rd_send(slot, b).wait_recv()
            terms.append(RD.at[slot, b])
        if relay:
            rx_send(slot, b).wait_recv()
            terms.append(RX.at[b])
        return terms

    def do_ry(slot, own=True, relay=False, halves=(0, 1)):
        for xx in halves:
            terms = here_terms(slot, (1 - y) * 2 + xx, own, relay)
            add_into(slot, start_of(1 - y, xx, k), terms, own)
            ry_send(slot, xx).start()

    def do_rx(slot):
        for b in range(4):
            rd_send(slot, b).wait_recv()
            add_into(slot, start_of(b // 2, b % 2, k), [RD.at[slot, b]])
            rx_send(slot, b).start()

    def do_rz(slot, own=True, relay=False):
        for xx in range(2):
            terms = here_terms(slot, y * 2 + xx, own, relay)
            ry_send(slot, xx).wait_recv()
            terms.append(RY.at[slot, xx])
            add_into(slot, start_of(y, xx, k), terms, own)
            for o in (2, 1, 3):
                rz_send(slot, xx, o).start()

    def piece_sum(slot, xx):
        total = D[slot, pcs(y, xx, k, z)].astype(full)
        for o in (1, 2, 3):
            rz_send(slot, xx, o).wait_recv()
            total = total + RZ[slot, xx, o - 1].astype(full)
        return total

    def rp_send(slot, dst):
        return remote(RP.at[slot], dst, rps.at[slot], rpr.at[slot], (par, z))

    def do_rp(slot, dst_own, dst_other):
        RP[slot] = piece_sum(slot, 1 - x)
        rp_send(slot, dst_other).start()
        dst_own[...] = piece_sum(slot, x)

    def do_rp_layer(layer):
        do_rp(layer, tgrad.at[layer, x], tgrad.at[layer, x])

    def do_rp_head(slot):
        do_rp(slot, hgrad.at[slot - 4], hgrad.at[slot - 4])

    def weight_grad(layer, slot):
        for dy in range(3):
            total = None
            for cv in range(2):
                term = lax.dot_general(
                    A3[layer, cv, pl.ds(dy * cols, px), :],
                    G[slot, cv, pl.ds(cols, px), :],
                    (((0,), (0,)), ((), ())),
                    preferred_element_type=full,
                )
                total = term if total is None else total + term
            D[slot, pl.ds(dy * 96, 96)] = total.astype(low).reshape(96, 8, CUT)

    def input_grad(slot, add):
        def canvas(cv, carry):
            take_g(slot, cv)
            for dx in range(3):
                total = None
                for dy in range(3):
                    term = lax.dot_general(
                        G[slot, cv, pl.ds((2 - dy) * cols, px), :],
                        W[slot, pl.ds((3 * dy + dx) * 32, 32)].reshape(CUT, CUT),
                        (((1,), (1,)), ((), ())),
                        preferred_element_type=full,
                    )
                    total = term if total is None else total + term
                if add:
                    U[dx, cv] = U[dx, cv] + total
                else:
                    U[dx, cv] = total
            return carry

        lax.fori_loop(0, 2, canvas, 0)

    def upstream_row(cv, r):
        at = pl.ds(pl.multiple_of(r * cols, cols), cols)
        return U[1, cv, at, :] + move_left(U[0, cv, at, :]) + move_right(U[2, cv, at, :])

    def fold(value):
        return jnp.sum(value.reshape(cols // 8, 8, CUT), axis=0)

    lane = lax.broadcasted_iota(jnp.int32, (1, CUT), 1)
    box_from = cls_out - 2 * CUT

    def log_one_plus(e):
        return jnp.where(e < 0.015625, e * (1.0 + e * (e * (1.0 / 3.0) - 0.5)), jnp.log(1.0 + e))

    def cls_rows(cut, cv, shift):
        here = lane + cut * CUT
        number = here
        for a in range(1, anchors):
            number = number - jnp.where(here >= a * classes, classes, 0)
        number = number.astype(full) - 200.0

        def row(r, carry):
            b_sum, l_sum = carry
            at = pl.ds(pl.multiple_of(r * cols, cols), cols)
            raw = ACC[at, :] + shift
            LS[cut, cv, at, :] = raw.astype(low)
            marks = MK[cut, cv, at, :].astype(full)
            hit = marks == number
            seen = marks < -50.0
            s = jnp.where(hit, -raw, raw)
            e = jnp.exp(-jnp.abs(s))
            inv = pl.reciprocal(1.0 + e)
            other = e * inv
            q = jnp.where(s >= 0.0, inv, other)
            p = jnp.where(s >= 0.0, other, inv)
            soft = jnp.maximum(s, 0.0) + log_one_plus(e)
            t = jnp.where(seen, jnp.where(hit, focal_alpha, 1.0 - focal_alpha), 0.0) * q * q
            slope = t * (2.0 * p * soft + q) * grad_scale
            g = jnp.where(hit, -slope, slope).astype(low)
            G[4 + cut, cv, pl.ds(pl.multiple_of((r + 1) * cols, cols), cols), :] = g
            return b_sum + fold(g.astype(full)), l_sum + fold(t * soft)

        return row

    def box_rows(cut, cv, shift):
        goal_lane = lax.broadcasted_iota(jnp.int32, (40, LANES), 1) - (box_from - LANES)
        goal_tab = (goal_lane == lax.broadcasted_iota(jnp.int32, (40, LANES), 0)).astype(full)

        def row(r, carry):
            b_sum, l_sum = carry
            at = pl.ds(pl.multiple_of(r * cols, cols), cols)
            raw = ACC[at, :] + shift
            LS[0, cv, at, :] = raw.astype(low)
            marks = MK[cut, cv, at, :].astype(full)
            chosen = marks < -110.0
            want = lax.dot_general(
                GP[cv, r], goal_tab, (((0,), (0,)), ((), ())),
                precision=lax.Precision.HIGHEST, preferred_element_type=full,
            )
            want = jnp.concatenate([jnp.zeros((cols, LANES), full), want], axis=1)
            diff = raw - want
            size = jnp.abs(diff)
            value = jnp.where(
                size < smooth_beta, 0.5 * diff * diff / smooth_beta, size - 0.5 * smooth_beta
            )
            slope = jnp.where(
                size < smooth_beta, diff / smooth_beta, jnp.where(diff > 0.0, 1.0, -1.0)
            )
            g = jnp.where(chosen, slope * grad_scale, 0.0).astype(low)
            G[4 + cut, cv, pl.ds(pl.multiple_of((r + 1) * cols, cols), cols), :] = g
            return b_sum + fold(g.astype(full)), l_sum + fold(jnp.where(chosen, value, 0.0))

        return row

    nothing = jnp.zeros((8, CUT), full)

    def l_copy(cut):
        return remote(LS.at[cut, 1 - x], logits.at[cut], ls.at[cut], lr.at[cut], (par, z))

    def e_copy():
        return remote(LS.at[0, 1 - x], deltas, es.at[0], er.at[0], (par, z))

    @pl.when(is_box)
    def _():
        remote(GP.at[1 - x], GP.at[1 - x], fs.at[2], fr.at[2], (par, z)).wait_recv()

    def head(i, carry):
        cut = jnp.where(i == 2, 0, i + 1)
        slot = 4 + cut
        gathered(slot)
        shift = bias[pl.ds(2 * layers + cut, 1), :]

        def canvas(cv, carry):
            b_sum, l_sum = carry
            ACC[...] = conv(layers, slot, cv)
            return lax.cond(
                is_cls,
                lambda: rim_first(cls_rows(cut, cv, shift), (b_sum, l_sum), lambda: send_g(slot, cv)),
                lambda: rim_first(box_rows(cut, cv, shift), (b_sum, l_sum), lambda: send_g(slot, cv)),
            )

        b_sum, l_sum = lax.fori_loop(0, 2, canvas, (nothing, nothing))

        @pl.when(is_box)
        def _():
            e_copy().start()

        BG[pl.ds(slot, 1), :] = jnp.sum(b_sum, axis=0, keepdims=True)
        BG[pl.ds(7, 1), :] = BG[pl.ds(7, 1), :] + jnp.sum(l_sum, axis=0, keepdims=True)
        weight_grad(layers, slot)
        do_rd(slot)

        @pl.when(is_cls & (i == 2))
        def _():
            do_rz(5)

        input_grad(slot, True)

        @pl.when(is_cls & (i == 1))
        def _():
            do_rx(6)

        @pl.when(i != 1)
        def _():
            do_ry(slot)

        @pl.when(is_cls & (i == 0))
        def _():
            do_d(4)
            handed_over(6)

        return carry

    lax.fori_loop(x, 3 - x, head, 0)

    @pl.when(is_cls)
    def _():
        for cut in range(3):
            l_copy(cut).start()
            logits[cut] = LS[cut, 0]

    @pl.when(is_box)
    def _():
        deltas[...] = LS[0, 1]

    def feature_rows(cv, dst):
        def row(r, carry):
            dst[pl.ds(pl.multiple_of(r * cols, cols), cols), :] = upstream_row(cv, r).astype(dst.dtype)
            return carry

        lax.fori_loop(0, rows, row, 0)

    FS = MK.at[0, 0]
    f_copy = remote(FS, FP, fs.at[3], fr.at[3], (par, z))
    def b_copy(src, dst, dev):
        return remote(src, BR.at[dst], bs.at[dst], br.at[dst], dev)

    def backward(j, carry):
        layer = layers - 1 - j

        def canvas(cv, b_sum):
            def row(r, b_sum):
                at = pl.ds(pl.multiple_of(r * cols, cols), cols)
                g = (upstream_row(cv, r) * silu_slope(Z[layer, cv, at, :])).astype(low)
                G[layer, cv, pl.ds(pl.multiple_of((r + 1) * cols, cols), cols), :] = g
                return b_sum + fold(g.astype(full))

            return rim_first(row, b_sum, lambda: send_g(layer, cv))

        b_sum = lax.fori_loop(0, 2, canvas, nothing)
        BG[pl.ds(layer, 1), :] = jnp.sum(b_sum, axis=0, keepdims=True)
        weight_grad(layer, layer)
        do_rd(layer)

        @pl.when(j == 3)
        def _():
            b_copy(BG, 0, (sib, z)).start()

        @pl.when(is_cls | (j > 0))
        def _():
            do_rz(layer + 1)

        @pl.when(j == layers - 1)
        def _():
            do_ry(0, halves=(0,))

        input_grad(layer, False)

        @pl.when(j == layers - 1)
        def _():
            do_ry(0, halves=(1,))
            feature_rows(1 - x, FS)
            f_copy.start()

        @pl.when(j < layers - 1)
        def _():
            do_ry(layer)

        @pl.when(is_cls & (j == 0))
        def _():
            do_rp_head(5)

        @pl.when(is_cls & (j == 1))
        def _():
            do_rp_head(4)

        @pl.when(j > 1)
        def _():
            do_rp_layer(layer + 2)

        @pl.when(is_box & (j == 1))
        def _():
            do_ry(6, relay=True)

        @pl.when(is_box & (j == 2))
        def _():
            do_rz(6, relay=True)

        @pl.when(is_box & (j == 3))
        def _():
            do_rp_head(6)

        return carry

    lax.fori_loop(0, layers, backward, 0)

    b_copy(BG, 0, (sib, z)).wait_recv()
    BR[6] = BG[...] + BR[0]
    b_copy(BR.at[6], 1, (yn, z)).start()
    feature_rows(x, fgrad)
    b_copy(BR.at[6], 1, (yn, z)).wait_recv()
    total = BR[6] + BR[1]
    for zz in range(4):
        @pl.when(z == zz)
        def _():
            BR[7 + zz] = total
            for o in (1, 2, 3):
                remote(
                    BR.at[7 + zz], BR.at[7 + zz], bs.at[1 + o], br.at[1 + o], (d, zpeer(o))
                ).start()
    do_rz(0)
    do_rp_layer(1)

    for o in (1, 2, 3):
        for zz in range(4):
            @pl.when(zfrom(o) == zz)
            def _():
                remote(
                    BR.at[7 + zz], BR.at[7 + zz], bs.at[1 + o], br.at[1 + o], (d, zpeer(o))
                ).wait_recv()
    total = (BR[7] + BR[8]) + (BR[9] + BR[10])
    BR[5] = total
    last = remote(BR.at[5], bsum.at[x], bs.at[5], br.at[5], (par, z))
    last.start()
    bsum[x] = total
    f_copy.wait_recv()
    fgrad[...] = fgrad[...] + FP[...].astype(full)
    do_rp_layer(0)

    remote(BR.at[5], bsum.at[1 - x], bs.at[5], br.at[5], (par, z)).wait_recv()
    loss = jnp.sum(bsum[0, 7:8, :] + bsum[1, 7:8, :], axis=1, keepdims=True)
    loss_out[...] = jnp.broadcast_to(loss, (8, LANES)) / jnp.maximum(count, 1.0)

    for layer in range(layers):
        rp_send(layer, tgrad.at[layer, 1 - x]).wait_recv()

    @pl.when(is_cls)
    def _():
        e_copy().wait_recv()
        rp_send(6, hgrad.at[2]).wait_recv()
        for b in range(4):
            rx_send(6, b).wait_send()
            d_copy(5, b // 2, b % 2, k).wait_send()
            d_copy(6, b // 2, b % 2, k).wait_send()
        for cut in range(3):
            l_copy(cut).wait_send()
        p_head(2, 4, 3).wait_send()
        p_head(1, 5, 1).wait_send()
        goal_copy.wait_send()

    @pl.when(is_box)
    def _():
        for cut in range(2):
            rp_send(4 + cut, hgrad.at[cut]).wait_recv()
        for cut in range(3):
            l_copy(cut).wait_recv()
        for b in range(4):
            x_copy(5, b // 2, b % 2).wait_send()
            x_copy(6, b // 2, b % 2).wait_send()
            d_copy(6, b // 2, b % 2, k).wait_send()
        e_copy().wait_send()
        p_head(0, 4, 4).wait_send()

    def close_gather(step, carry):
        for xx in range(2):
            for o in (1, 2, 3):
                z_send(step, xx, o).wait_send()
            y_copy(step, xx, y).wait_send()
        return carry

    lax.fori_loop(0, 5 + x, close_gather, 0)

    def close_slot(slot, carry):
        for b in range(4):
            d_copy(slot, b // 2, b % 2, k).wait_send()

        return carry

    lax.fori_loop(0, 5 - x, close_slot, 0)

    def close_layer(layer, carry):
        @pl.when(layer < layers)
        def _():
            p_send(jnp.minimum(layer, layers - 1)).wait_send()

        @pl.when(down_ok() & (layer > 0))
        def _():
            for cv in range(2):
                a_edge(layer, 0, cv).wait_send()

        @pl.when(up_ok() & (layer > 0))
        def _():
            for cv in range(2):
                a_edge(layer, 1, cv).wait_send()

        return carry

    lax.fori_loop(0, layers + 1, close_layer, 0)

    def close_grad(slot, carry):
        @pl.when(is_cls | (slot < 4) | (slot == 6))
        def _():
            for b in range(4):
                rd_send(slot, b).wait_send()

            @pl.when(down_ok())
            def _():
                for cv in range(2):
                    g_edge(slot, 0, cv).wait_send()

            @pl.when(up_ok())
            def _():
                for cv in range(2):
                    g_edge(slot, 1, cv).wait_send()

        @pl.when((slot < 4) | (is_cls & (slot < 6)) | (is_box & (slot == 6)))
        def _():
            for xx in range(2):
                ry_send(slot, xx).wait_send()
                for o in (1, 2, 3):
                    rz_send(slot, xx, o).wait_send()
            rp_send(slot, RP.at[slot]).wait_send()

        return carry

    lax.fori_loop(0, layers + 3, close_grad, 0)
    pltpu_feature.wait_send()

    @pl.when(z < 3)
    def _():
        for across in range(2):
            f_edge(0, across).wait_send()

    @pl.when(z > 0)
    def _():
        for across in range(2):
            f_edge(1, across).wait_send()

    code_copy.wait_send()
    f_copy.wait_send()
    n_copy(0, 4, (sib, z)).wait_send()
    n_copy(1, 5, (yn, z)).wait_send()
    n_copy(2, 6, (par, z)).wait_send()
    b_copy(BG, 0, (sib, z)).wait_send()
    b_copy(BR.at[6], 1, (yn, z)).wait_send()
    for o in (1, 2, 3):
        n_copy(3, 6 + o, (d, zpeer(o))).wait_send()
        remote(BR.at[7], BR.at[7], bs.at[1 + o], br.at[1 + o], (d, zpeer(o))).wait_send()
    last.wait_send()


def finish_kernel(
    step, lg, dl, fg, tg, hg, bsum, loss_in, tw, hw, tm, tv, hm, hv, bw, bm, bv,
    o_lg, o_dl, o_fg, o_tg, o_bg, o_hg, o_tn, o_hn, o_tm, o_tv, o_hm, o_hv, o_tc, o_hc,
    o_loss, o_gb, o_gx, o_wb, o_mb, o_vb,
    TW, TM, TV, TC, HGO, HW, HM, HV, HC, LO, DT, DS, t_out, h_out, m_sem,
    *, layers, rows, cols, cls_out, box_out,
):
    tail = cls_out - 2 * CUT
    last = tail + box_out

    def t_stores(layer):
        pairs = (
            (tg.at[layer, 0], o_tg.at[layer]),
            (tg.at[layer, 1], o_bg.at[layer]),
            (TW.at[layer], o_tn.at[layer]),
            (TM.at[layer], o_tm.at[layer]),
            (TV.at[layer], o_tv.at[layer]),
            (TC.at[layer], o_tc.at[layer]),
        )
        return [pltpu.make_async_copy(a, b, t_out.at[layer, i]) for i, (a, b) in enumerate(pairs)]

    h_stores = [
        pltpu.make_async_copy(a, b, h_out.at[i])
        for i, (a, b) in enumerate(((HGO, o_hg), (HW, o_hn), (HM, o_hm), (HV, o_hv), (HC, o_hc)))
    ]
    lg_store = pltpu.make_async_copy(LO, o_lg, m_sem.at[0])
    fg_store = pltpu.make_async_copy(fg, o_fg, m_sem.at[1])
    fg_store.start()
    for cut, width in ((0, CUT), (1, CUT), (2, tail)):
        LO[:, cut * CUT : cut * CUT + width] = lg[cut][:, :width]
    lg_store.start()

    steps = jnp.broadcast_to(step[0].astype(full), (8, CUT))
    keep_one = (1.0 - jnp.exp(steps * math.log(beta_one)))[0:1, :]
    keep_two = (1.0 - jnp.exp(steps * math.log(beta_two)))[0:1, :]

    def adam(weight, grad, first, second, decay):
        one, two = keep_one[:, : grad.shape[1]], keep_two[:, : grad.shape[1]]
        first_new = beta_one * first + (1.0 - beta_one) * grad
        second_new = beta_two * second + (1.0 - beta_two) * grad * grad
        first_hat = first_new / one
        second_hat = second_new / two
        weight_new = weight - learn_rate * (
            first_hat / (jnp.sqrt(second_hat) + adam_eps) + decay * weight
        )
        return weight_new, first_new, second_new

    for layer in range(layers):
        for t in range(2):
            w_new, m_new, v_new = adam(
                tw[layer, t], tg[layer, t], tm[layer, t], tv[layer, t], decay_rate
            )
            TW[layer, t] = w_new
            TM[layer, t] = m_new
            TV[layer, t] = v_new
            TC[layer, t] = w_new.astype(low)
        for copy in t_stores(layer):
            copy.start()
    for cut, width in ((0, CUT), (1, CUT), (2, last)):
        at = slice(cut * CUT, cut * CUT + width)
        grad = hg[cut][:, :width]
        HGO[:, at] = grad
        w_new, m_new, v_new = adam(hw[:, at], grad, hm[:, at], hv[:, at], decay_rate)
        HW[:, at] = w_new
        HM[:, at] = m_new
        HV[:, at] = v_new
        HC[:, at] = w_new.astype(low)
    for copy in h_stores:
        copy.start()
    o_loss[0] = loss_in[0, 0]
    for q in range(2 * layers + 3):
        if q < 2 * layers:
            grad, width = bsum[q % 2, q // 2 : q // 2 + 1, :], CUT
        elif q < 2 * layers + 2:
            grad, width = bsum[0, q - layers : q - layers + 1, :], CUT
        else:
            lane = lax.broadcasted_iota(jnp.int32, (1, CUT), 1)
            boxes = bsum[1, 6:7, :]
            grad, width = jnp.where(lane < tail, bsum[0, 6:7, :], boxes)[:, :last], last
            o_gx[...] = pltpu.roll(boxes, CUT - tail, 1)[:, :box_out].reshape(box_out)
        at = pl.ds(q * CUT, width)
        w_new, m_new, v_new = adam(
            bw[at].reshape(1, width), grad, bm[at].reshape(1, width), bv[at].reshape(1, width), 0.0
        )
        o_wb[at] = w_new.reshape(width)
        o_mb[at] = m_new.reshape(width)
        o_vb[at] = v_new.reshape(width)
        most = min(width, cls_out + 2 * layers * CUT - q * CUT)
        o_gb[pl.ds(q * CUT, most)] = grad[:, :most].reshape(most)
    pick_lane = lax.broadcasted_iota(jnp.int32, (40, LANES), 1) - (tail - LANES)
    pick = (pick_lane == lax.broadcasted_iota(jnp.int32, (40, LANES), 0)).astype(full).astype(low)
    for r in range(rows):
        DT[r] = lax.dot_general(
            pick, dl[r * cols : (r + 1) * cols, LANES:], (((1,), (1,)), ((), ())), preferred_element_type=full
        )

    def turn(q, carry):
        for r in range(rows):
            DS[q, r : r + 1, :] = DT[r, pl.ds(q, 1), :]
        return carry

    lax.fori_loop(0, box_out, turn, 0)
    o_dl[...] = DS[...].astype(low)

    for layer in range(layers):
        for copy in t_stores(layer):
            copy.wait()
    for copy in h_stores:
        copy.wait()
    lg_store.wait()
    fg_store.wait()


def fused_shards(
    features,
    crop_ids,
    labels,
    positive,
    box_targets,
    tower_weights,
    head_weights,
    biases,
    tower_m,
    tower_v,
    head_m,
    head_v,
    bias_m,
    bias_v,
    step_count,
):
    canvases, rows, cols, channels = features.shape
    layers = tower_weights.shape[0]
    shard_rows = tower_weights.shape[2]
    anchors = labels.shape[-1]
    head_out = head_weights.shape[1]
    box_out = 4 * anchors
    cls_out = head_out - box_out
    px = rows * cols
    piece = shard_rows // 8
    tow = tower_weights.reshape(layers, 2, piece, 8, channels)
    by_anchor = (0, 3, 1, 2)
    marked = jnp.transpose(labels, by_anchor)[0]
    lit = jnp.transpose(positive, by_anchor)[0]
    goals = jnp.transpose(box_targets, by_anchor)[0]
    units = 32 * piece
    block = 4 * piece
    dma = pltpu.SemaphoreType.DMA
    vm = pl.BlockSpec(memory_space=pltpu.VMEM)
    shape = jax.ShapeDtypeStruct
    logits, deltas, fgrad, tgrad, hgrad, bsum, loss = pl.pallas_call(
        partial(
            mega_kernel,
            rows=rows, cols=cols, layers=layers, cls_out=cls_out, box_out=box_out, anchors=anchors, piece=piece,
        ),
        out_shape=(
            shape((3, px, CUT), low),
            shape((px, CUT), low),
            shape((px, CUT), full),
            shape((layers, 2, piece, 8, CUT), full),
            shape((3, piece, 8, CUT), full),
            shape((2, 8, CUT), full),
            shape((8, LANES), full),
        ),
        in_specs=[vm, pl.BlockSpec(memory_space=pltpu.SMEM)] + [vm] * 6,
        out_specs=[vm] * 7,
        scratch_shapes=[
            pltpu.VMEM((7, units, 8, CUT), low),
            pltpu.VMEM((7, units, 8, CUT), low),
            pltpu.VMEM((7, 4, block, 8, CUT), low),
            pltpu.VMEM((7, 2, block, 8, CUT), low),
            pltpu.VMEM((7, 2, 3, piece, 8, CUT), low),
            pltpu.VMEM((4, block, 8, CUT), low),
            pltpu.VMEM((7, piece, 8, CUT), full),
            pltpu.VMEM((layers + 1, 2, px + 2 * cols, 3 * CUT), low),
            pltpu.VMEM((layers + 1, 2, 2, cols, CUT), low),
            pltpu.VMEM((7, 2, px + 2 * cols, CUT), low),
            pltpu.VMEM((layers, 2, px, CUT), full),
            pltpu.VMEM((3, 2, px, CUT), full),
            pltpu.VMEM((px, CUT), full),
            pltpu.VMEM((px, CUT), low),
            pltpu.VMEM((2, rows, 16, cols), full),
            pltpu.VMEM((2, rows, 40, cols), full),
            pltpu.VMEM((3, 2, px, CUT), low),
            pltpu.VMEM((10, 8, LANES), full),
            pltpu.VMEM((8, CUT), full),
            pltpu.VMEM((11, 8, CUT), full),
            pltpu.VMEM((layers, piece, 8, CUT), low),
            pltpu.VMEM((3, piece, 8, CUT), low),
            pltpu.VMEM((16, CUT), full),
            pltpu.VMEM((3, 2, px, CUT), low),
            dma((6,)), dma((6,)),
            dma((6, 2, 3)), dma((6, 2, 3)),
            dma((6, 2)), dma((6, 2)),
            dma((7, 4)), dma((7, 4)),
            dma((2, 4)), dma((2, 4)),
            dma((4,)), dma((4,)),
            dma((layers + 1, 2, 2)), dma((layers + 1, 2, 2)),
            dma((7, 2, 2)), dma((7, 2, 2)),
            dma((3,)), dma((3,)),
            dma((1,)), dma((1,)),
            dma((7, 4)), dma((7, 4)),
            dma((7, 2)), dma((7, 2)),
            dma((7, 2, 3)), dma((7, 2, 3)),
            dma((4,)), dma((4,)),
            dma((7,)), dma((7,)),
            dma((10,)), dma((10,)),
            dma((6,)), dma((6,)),
        ],
        compiler_params=pltpu.CompilerParams(
            vmem_limit_bytes=60 * 1024 * 1024, collective_id=0, has_side_effects=True
        ),
    )(features.reshape(px, channels), crop_ids, marked, lit, goals, tow, head_weights, biases)

    tower_shape = tower_weights.shape
    head_shape = head_weights.shape
    anys = pl.BlockSpec(memory_space=pl.ANY)
    smem = pl.BlockSpec(memory_space=pltpu.SMEM)
    biases_out = biases.shape[0]
    (
        o_lg, o_dl, o_fg, o_tg, o_bg, o_hg, o_tn, o_hn, o_tm, o_tv, o_hm, o_hv, o_tc, o_hc,
        o_loss, o_gb, o_gx, o_wb, o_mb, o_vb,
    ) = pl.pallas_call(
        partial(
            finish_kernel, layers=layers, rows=rows, cols=cols, cls_out=cls_out, box_out=box_out
        ),
        out_shape=(
            shape((px, cls_out), low),
            shape((box_out, rows, cols), low),
            shape((px, channels), full),
            shape((layers, shard_rows, channels), full),
            shape((layers, shard_rows, channels), full),
            shape(head_shape, full),
            shape(tower_shape, full),
            shape(head_shape, full),
            shape(tower_shape, full),
            shape(tower_shape, full),
            shape(head_shape, full),
            shape(head_shape, full),
            shape(tower_shape, low),
            shape(head_shape, low),
            shape((1,), full),
            shape((biases_out - box_out,), full),
            shape((box_out,), full),
            shape((biases_out,), full),
            shape((biases_out,), full),
            shape((biases_out,), full),
        ),
        in_specs=[smem] + [vm] * 16,
        out_specs=[anys, vm] + [anys] * 12 + [smem] + [vm] * 5,
        scratch_shapes=[
            pltpu.VMEM(tower_shape, full),
            pltpu.VMEM(tower_shape, full),
            pltpu.VMEM(tower_shape, full),
            pltpu.VMEM(tower_shape, low),
            pltpu.VMEM(head_shape, full),
            pltpu.VMEM(head_shape, full),
            pltpu.VMEM(head_shape, full),
            pltpu.VMEM(head_shape, full),
            pltpu.VMEM(head_shape, low),
            pltpu.VMEM((px, cls_out), low),
            pltpu.VMEM((rows, 40, cols), full),
            pltpu.VMEM((box_out, rows, cols), full),
            dma((layers, 6)), dma((5,)), dma((2,)),
        ],
        compiler_params=pltpu.CompilerParams(vmem_limit_bytes=60 * 1024 * 1024),
    )(
        step_count, logits, deltas, fgrad, tgrad.reshape(tower_shape), hgrad.reshape(3, shard_rows, CUT), bsum, loss,
        tower_weights, head_weights, tower_m, tower_v, head_m, head_v, biases, bias_m, bias_v,
    )
    field = (canvases, rows, cols, -1)
    return (
        o_lg.reshape(field),
        jnp.transpose(o_dl[None], (0, 2, 3, 1)),
        o_loss.reshape(()),
        o_fg.reshape(field),
        o_tg,
        o_bg,
        o_hg,
        o_gb,
        o_gx,
        o_tn,
        o_hn,
        o_wb,
        o_tm,
        o_tv,
        o_hm,
        o_hv,
        o_mb,
        o_vb,
        o_tc,
        o_hc,
    )


def solution(mesh):
    placed = (
        P("dp", "tower", None, None),
        P("dp", None),
        P("dp", "tower", None, None),
        P("dp", "tower", None, None),
        P("dp", "tower", None, None),
        P(None, None, ("dp", "tower"), None),
        P(("dp", "tower"), None),
        P(),
        P(None, None, ("dp", "tower"), None),
        P(None, None, ("dp", "tower"), None),
        P(("dp", "tower"), None),
        P(("dp", "tower"), None),
        P(),
        P(),
        P(),
    )
    fused = mesh.shape["dp"] == 8 and mesh.shape["tower"] == 4
    return jax.shard_map(
        fused_shards if fused else plain_shards,
        mesh=mesh,
        in_specs=placed,
        out_specs=(
            P("dp", "tower", None, None),
            P("dp", "tower", None, None),
            P(),
            P("dp", "tower", None, None),
            P(None, ("dp", "tower"), None),
            P(None, ("dp", "tower"), None),
            P(("dp", "tower"), None),
            P(),
            P(),
            P(None, None, ("dp", "tower"), None),
            P(("dp", "tower"), None),
            P(),
            P(None, None, ("dp", "tower"), None),
            P(None, None, ("dp", "tower"), None),
            P(("dp", "tower"), None),
            P(("dp", "tower"), None),
            P(),
            P(),
            P(None, None, ("dp", "tower"), None),
            P(("dp", "tower"), None),
        ),
        check_vma=False,
    )
```
